32 devices in a mesh: snp: 2 (over x), rows: 16 (over z, y, core).
Axes of the slice: x: 2, y: 2, z: 4, core: 2. Of those that a mesh axis runs over, the one named last changes fastest.
Arguments:
- genotypes: float32 [3072, 2560], P('snp', 'rows'), may hold values from -1 to 2, as said below
- relationship: float32 [2560, 2560], P('rows', 'snp'), as said below
Outputs:
- updated: float32 [2560, 2560], P('rows', 'snp')
- panel: float32 [2560, 512], P('rows')
The draws below stay inside these ranges and needn't reach their ends.
Inputs may be any that keep to these rules, and one draw needn't show every extreme that they name: `genotypes`: expected count of the alternative allele, a real number between 0 and 2; exactly -1 marks a missing call. `relationship`: symmetric.
All inputs are finite; a program needn't handle non-finite values.
Results may differ from the reference program's by a relative error of at most 0.0007.
The reference program's roundings to bfloat16 on the way (of `centered`) count: a program that leaves them out, or rounds other values in their place, can miss the bound.
Values may be sent and summed in bfloat16 or wider, within the bound.
No kernel may reach another device: no remote copies, remote signals or barrier semaphores. Data moves between devices by JAX's collectives and lax.ppermute only.
A program may use at most 128 MiB of HBM per device.

```python
import math
import jax
import jax.numpy as jnp
from jax import lax

SNPS = 3072
PANEL = 512
INDIV = 2560


def draw_genotypes(key, part):
    key = jax.random.fold_in(key, 11)
    key_freq, key_first, key_second, key_noise_one, key_noise_two, key_missing = jax.random.split(key, 6)
    percent = jax.random.randint(key_freq, (SNPS, 1), 5, 51)
    first_allele = jax.random.randint(key_first, (SNPS, INDIV), 0, 100) < percent
    second_allele = jax.random.randint(key_second, (SNPS, INDIV), 0, 100) < percent
    missing = jax.random.randint(key_missing, (SNPS, INDIV), 0, 50) == 0
    noise_one = jax.random.normal(key_noise_one, (SNPS, INDIV), jnp.float32) * 2.0
    noise_two = jax.random.normal(key_noise_two, (SNPS, INDIV), jnp.float32) * 2.0
    logit_one = jnp.where(first_allele, 2.5, -2.5) + noise_one
    logit_two = jnp.where(second_allele, 2.5, -2.5) + noise_two
    dosage = jax.nn.sigmoid(logit_one) + jax.nn.sigmoid(logit_two)
    return jnp.where(missing, -1.0, dosage).astype(jnp.float32)


def draw_relationship(key, part):
    key = jax.random.fold_in(key, 23)
    key_noise, key_scale = jax.random.split(key, 2)
    spread = 0.02 / math.sqrt(INDIV)
    near_length = 6.0
    far_length = 48.0
    log_spread = 0.35
    noise_field = jax.random.normal(key_noise, (INDIV, INDIV), jnp.float32) * spread
    symmetric = (noise_field + noise_field.T) * 0.70710678
    row_scale = jnp.exp(jax.random.uniform(key_scale, (INDIV,), jnp.float32, -log_spread, log_spread))
    row_index = lax.broadcasted_iota(jnp.int32, (INDIV, INDIV), 0)
    col_index = lax.broadcasted_iota(jnp.int32, (INDIV, INDIV), 1)
    distance = jnp.abs(row_index - col_index).astype(jnp.float32)
    kinship = 0.7 * jnp.exp(-distance / near_length) + 0.3 * jnp.exp(-distance / far_length)
    return (row_scale[:, None] * kinship * row_scale[None, :] + symmetric).astype(jnp.float32)


def setup_inputs(seed: int = 0) -> dict:
    arg_keys = jax.random.split(jax.random.key(seed), 3)
    genotypes = draw_genotypes(jax.random.fold_in(arg_keys[2], 71), 0)
    relationship = draw_relationship(jax.random.fold_in(arg_keys[2], 71), 0)
    return {"genotypes": genotypes, "relationship": relationship}


RIDGE = 0.25

def reference(genotypes, relationship):
    called = genotypes >= 0
    dosage = jnp.where(called, genotypes, 0.0).astype(jnp.float32)
    totals = jnp.sum(dosage, axis=1)
    counts = jnp.sum(called.astype(jnp.float32), axis=1)
    frequency = totals / (2.0 * counts)
    scale_total = jnp.sum(2.0 * frequency * (1.0 - frequency))
    centered = jnp.where(called, dosage - 2.0 * frequency[:, None], 0.0).astype(jnp.bfloat16)
    gram = lax.dot_general(centered.astype(jnp.float32), centered.astype(jnp.float32), (((0,), (0,)), ((), ())), preferred_element_type=jnp.float32)
    combined = relationship + gram / scale_total
    diag_index = jnp.arange(INDIV, dtype=jnp.int32)
    combined = combined.at[diag_index, diag_index].add(RIDGE)
    factor = jnp.linalg.cholesky(combined[:PANEL, :PANEL])
    panel = lax.linalg.triangular_solve(factor, combined[:, :PANEL], left_side=False, lower=True, transpose_a=True)
    updated = combined - jnp.dot(panel, panel.T, precision=lax.Precision.HIGHEST)
    return (updated, panel)
```

```python
import jax
import jax.numpy as jnp
from jax import lax
from jax.experimental import pallas as pl
from jax.experimental.pallas import tpu as pltpu
from jax.sharding import PartitionSpec as P

PANEL = 512
RIDGE = 0.25
GROUP = 4


BLOCK = 128
SUB = 8


def factor_kernel(a_ref, out_ref, work):
    work[...] = a_ref[...]
    lane = lax.broadcasted_iota(jnp.int32, (SUB, BLOCK), 1)
    for g in range(BLOCK // SUB):
        at = g * SUB
        own = work[at : at + SUB, :]
        inside = (lane >= at) & (lane < at + SUB)
        rows = [jnp.broadcast_to(own[u : u + 1, :], (SUB, BLOCK)) for u in range(SUB)]
        e = [
            [
                jnp.broadcast_to(rows[t][:, at + u : at + u + 1], (SUB, BLOCK))
                for t in range(u + 1)
            ]
            for u in range(SUB)
        ]
        rows = [
            jnp.where(inside, jnp.where(lane == at + u, 1.0, 0.0), rows[u])
            for u in range(SUB)
        ]
        low = [[None] * SUB for _ in range(SUB)]
        scale = []
        for t in range(SUB):
            r = lax.rsqrt(e[t][t])
            scale.append(r)
            for u in range(t + 1, SUB):
                low[u][t] = e[u][t] * r
            for u in range(t + 1, SUB):
                for v in range(t + 1, u + 1):
                    e[u][v] = e[u][v] - low[u][t] * low[v][t]
            rows[t] = rows[t] * r
            for u in range(t + 1, SUB):
                rows[u] = rows[u] - low[u][t] * rows[t]
        for below in range(g + 1, BLOCK // SUB):
            base = below * SUB
            rest = work[base : base + SUB, :]
            c = [
                jnp.broadcast_to(rest[:, at + t : at + t + 1], (SUB, BLOCK))
                for t in range(SUB)
            ]
            rest = jnp.where(inside, 0.0, rest)
            for t in range(SUB):
                c[t] = c[t] * scale[t]
                for s in range(t + 1, SUB):
                    c[s] = c[s] - low[s][t] * c[t]
                rest = rest - c[t] * rows[t]
            work[base : base + SUB, :] = rest
        for t in range(SUB):
            work[at + t : at + t + 1, :] = rows[t][0:1, :]
    i = lax.broadcasted_iota(jnp.int32, (BLOCK, BLOCK), 0)
    j = lax.broadcasted_iota(jnp.int32, (BLOCK, BLOCK), 1)
    out_ref[...] = jnp.where(j <= i, work[...], 0.0)


def factor_inverse(a):
    return pl.pallas_call(
        factor_kernel,
        out_shape=jax.ShapeDtypeStruct((BLOCK, BLOCK), jnp.float32),
        in_specs=[pl.BlockSpec(memory_space=pltpu.VMEM)],
        out_specs=pl.BlockSpec(memory_space=pltpu.VMEM),
        scratch_shapes=[pltpu.VMEM((BLOCK, BLOCK), jnp.float32)],
        cost_estimate=pl.CostEstimate(flops=4_000_000_000, bytes_accessed=131072, transcendentals=128),
    )(a)


def precise(a, b, contract):
    return lax.dot_general(
        a,
        b,
        (((1,), (contract,)), ((), ())),
        precision=lax.Precision.HIGHEST,
        preferred_element_type=jnp.float32,
    )


def solve_panel(diag_block, own_columns):
    blocks = PANEL // BLOCK
    rest = jnp.concatenate([diag_block, own_columns], axis=0)
    inverses, columns = [], []
    for k in range(blocks):
        inverse = factor_inverse(rest[:BLOCK, :BLOCK])
        column = precise(rest[BLOCK:, :BLOCK], inverse, 1)
        inverses.append(inverse)
        columns.append(column)
        if k + 1 < blocks:
            left = (blocks - 1 - k) * BLOCK
            rest = rest[BLOCK:, BLOCK:] - precise(column, column[:left], 1)
    own = own_columns.shape[0]
    panel = [c[-own:] for c in columns]
    weights = [None] * blocks
    for k in reversed(range(blocks)):
        total = panel[k]
        for j in range(k + 1, blocks):
            start = (j - k - 1) * BLOCK
            total = total - precise(weights[j], columns[k][start : start + BLOCK], 0)
        weights[k] = precise(total, inverses[k], 0)
    return jnp.concatenate(panel, axis=1), jnp.concatenate(weights, axis=1)


def select_order(blocks, q):
    low = (q & 1) == 1
    high = (q & 2) == 2
    b = [
        jnp.where(low, blocks[k ^ 1], blocks[k]) for k in range(GROUP)
    ]
    return [jnp.where(high, b[k ^ 2], b[k]) for k in range(GROUP)]


def make(n_rows, n_snp):
    lines = n_rows // GROUP

    def rows_xor(x, bits):
        return lax.ppermute(x, "rows", [(r, r ^ bits) for r in range(n_rows)])

    def line_next(x):
        return lax.ppermute(
            x, "rows", [(r, (r + GROUP) % n_rows) for r in range(n_rows)]
        )

    def snp_xor(x, bits):
        return lax.ppermute(x, "snp", [(s, s ^ bits) for s in range(n_snp)])

    def from_first_snp(x, rank):
        got = x
        for s in range(1, n_snp):
            moved = lax.ppermute(x, "snp", [(0, s)])
            got = jnp.where(rank == s, moved, got)
        return got

    def group_gather(x):
        core = rows_xor(x, 1)
        other = rows_xor(x, 2)
        return [x, core, other, rows_xor(other, 1)]

    def rows_sum(x):
        bit = 1
        while bit < n_rows:
            if bit * 2 < n_rows:
                parts = [x] + [rows_xor(x, bit * k) for k in (1, 2, 3)]
                x = (parts[0] + parts[1]) + (parts[2] + parts[3])
                bit *= 4
            else:
                x = x + rows_xor(x, bit)
                bit *= 2
        return x

    def snp_sum(x):
        bit = 1
        while bit < n_snp:
            x = x + snp_xor(x, bit)
            bit *= 2
        return x

    def times(a, b):
        return lax.dot_general(
            a, b, (((1,), (1,)), ((), ())), preferred_element_type=jnp.float32
        )

    def per_device(genotypes, relationship):
        snps, own = genotypes.shape
        width = relationship.shape[1]
        rank = lax.axis_index("rows")
        col = lax.axis_index("snp")
        q = rank % GROUP
        z = rank // GROUP
        part = lines // n_snp

        rel_own = from_first_snp(relationship[:, :PANEL], col)
        rel_ring = [rel_own]
        for _ in range(lines - 1):
            rel_ring.append(line_next(rel_ring[-1]))

        called = genotypes >= 0
        dosage = jnp.where(called, genotypes, 0.0)
        stats = jnp.stack(
            [jnp.sum(dosage, axis=1), jnp.sum(called.astype(jnp.float32), axis=1)]
        )
        stats = rows_sum(stats)
        frequency = stats[0] / (2.0 * stats[1])
        scale_total = snp_sum(jnp.sum(2.0 * frequency * (1.0 - frequency)).reshape(1, 1))
        inverse = (1.0 / scale_total)[0, 0]
        gt = genotypes.T
        centered = jnp.where(gt >= 0, gt - 2.0 * frequency[None, :], 0.0).astype(
            jnp.bfloat16
        )

        ring = [centered]
        for _ in range(lines - 1):
            ring.append(line_next(ring[-1]))
        line = jnp.stack(ring)
        rel_line = jnp.stack(rel_ring)

        def of_line(stack, target):
            return lax.dynamic_index_in_dim(
                stack, jnp.mod(z - target, lines), 0, keepdims=False
            )

        first = of_line(line, 0)
        head = jnp.concatenate(select_order(group_gather(first), q), axis=0)[:PANEL]
        plane = jnp.concatenate(group_gather(centered), axis=0)

        lead = snp_sum(times(jnp.concatenate([first, centered], axis=0), head))
        rel_lead = jnp.concatenate([of_line(rel_line, 0), rel_own], axis=0)
        lead = rel_lead + lead * inverse
        eye_rows = lax.broadcasted_iota(jnp.int32, lead.shape, 0)
        eye_cols = lax.broadcasted_iota(jnp.int32, lead.shape, 1)
        ids = jnp.where(eye_rows < own, q * own + eye_rows, (rank - 1) * own + eye_rows)
        lead = lead + jnp.where(ids == eye_cols, RIDGE, 0.0)
        own_columns = lead[own:]
        diag_block = jnp.concatenate(
            select_order(group_gather(lead[:own]), q), axis=0
        )[:PANEL]

        mine = None
        for bits in range(n_snp):
            target = col ^ bits
            cols = jnp.concatenate(
                [of_line(line, target * part + j) for j in range(part)], axis=0
            )
            gram = times(plane, cols)
            side = times(cols, head)
            if bits:
                gram, side = snp_xor(gram, bits), snp_xor(side, bits)
                mine = (mine[0] + gram, mine[1] + side)
            else:
                mine = (gram, side)
        gram, side = mine
        rel_side = jnp.concatenate(
            [of_line(rel_line, col * part + j) for j in range(part)], axis=0
        )
        side = rel_side + side * inverse
        side_rows = lax.broadcasted_iota(jnp.int32, side.shape, 0)
        side_ids = (
            (col * part + side_rows // own) * GROUP + q
        ) * own + side_rows % own
        side = side + jnp.where(
            side_ids == lax.broadcasted_iota(jnp.int32, side.shape, 1), RIDGE, 0.0
        )
        side = select_order(group_gather(side), q)
        side = jnp.stack([s.reshape(part, own, PANEL) for s in side], axis=1)
        side = side.reshape(width, PANEL)

        gram = gram.reshape(GROUP, own, part * own)
        pieces = [gram[0]] + [rows_xor(gram[k], k) for k in range(1, GROUP)]
        pieces = select_order(pieces, q)
        summed = jnp.stack([p.reshape(own, part, own) for p in pieces], axis=2)
        summed = summed.reshape(own, width)
        row_ids = rank * own + lax.broadcasted_iota(jnp.int32, (own, width), 0)
        col_ids = col * width + lax.broadcasted_iota(jnp.int32, (own, width), 1)
        combined = relationship + summed * inverse
        combined = combined + jnp.where(row_ids == col_ids, RIDGE, 0.0)

        panel, weights = solve_panel(diag_block, own_columns)
        updated = combined - precise(weights, side, 1)
        return updated, panel

    return per_device


def solution(mesh):
    return jax.shard_map(
        make(mesh.shape["rows"], mesh.shape["snp"]),
        mesh=mesh,
        in_specs=(P("snp", "rows"), P("rows", "snp")),
        out_specs=(P("rows", "snp"), P("rows", None)),
        check_vma=False,
    )
```

```python
import jax
import jax.numpy as jnp
from jax import lax
from jax.experimental import pallas as pl
from jax.experimental.pallas import tpu as pltpu
from jax.sharding import PartitionSpec as P

PANEL = 512
RIDGE = 0.25
GROUP = 4


BLOCK = 128
SUB = 8


def factor_kernel(a_ref, out_ref, work):
    work[...] = a_ref[...]
    lane = lax.broadcasted_iota(jnp.int32, (SUB, BLOCK), 1)
    for g in range(BLOCK // SUB):
        at = g * SUB
        own = work[at : at + SUB, :]
        inside = (lane >= at) & (lane < at + SUB)
        rows = [jnp.broadcast_to(own[u : u + 1, :], (SUB, BLOCK)) for u in range(SUB)]
        e = [
            [
                jnp.broadcast_to(rows[t][:, at + u : at + u + 1], (SUB, BLOCK))
                for t in range(u + 1)
            ]
            for u in range(SUB)
        ]
        rows = [
            jnp.where(inside, jnp.where(lane == at + u, 1.0, 0.0), rows[u])
            for u in range(SUB)
        ]
        low = [[None] * SUB for _ in range(SUB)]
        scale = []
        for t in range(SUB):
            r = lax.rsqrt(e[t][t])
            scale.append(r)
            for u in range(t + 1, SUB):
                low[u][t] = e[u][t] * r
            for u in range(t + 1, SUB):
                for v in range(t + 1, u + 1):
                    e[u][v] = e[u][v] - low[u][t] * low[v][t]
            rows[t] = rows[t] * r
            for u in range(t + 1, SUB):
                rows[u] = rows[u] - low[u][t] * rows[t]
        for below in range(g + 1, BLOCK // SUB):
            base = below * SUB
            rest = work[base : base + SUB, :]
            c = [
                jnp.broadcast_to(rest[:, at + t : at + t + 1], (SUB, BLOCK))
                for t in range(SUB)
            ]
            rest = jnp.where(inside, 0.0, rest)
            for t in range(SUB):
                c[t] = c[t] * scale[t]
                for s in range(t + 1, SUB):
                    c[s] = c[s] - low[s][t] * c[t]
                rest = rest - c[t] * rows[t]
            work[base : base + SUB, :] = rest
        for t in range(SUB):
            work[at + t : at + t + 1, :] = rows[t][0:1, :]
    i = lax.broadcasted_iota(jnp.int32, (BLOCK, BLOCK), 0)
    j = lax.broadcasted_iota(jnp.int32, (BLOCK, BLOCK), 1)
    out_ref[...] = jnp.where(j <= i, work[...], 0.0)


def factor_inverse(a):
    return pl.pallas_call(
        factor_kernel,
        out_shape=jax.ShapeDtypeStruct((BLOCK, BLOCK), jnp.float32),
        in_specs=[pl.BlockSpec(memory_space=pltpu.VMEM)],
        out_specs=pl.BlockSpec(memory_space=pltpu.VMEM),
        scratch_shapes=[pltpu.VMEM((BLOCK, BLOCK), jnp.float32)],
        cost_estimate=pl.CostEstimate(flops=4_000_000_000, bytes_accessed=131072, transcendentals=128),
    )(a)


def precise(a, b, contract):
    return lax.dot_general(
        a,
        b,
        (((1,), (contract,)), ((), ())),
        precision=lax.Precision.HIGHEST,
        preferred_element_type=jnp.float32,
    )


def factor_blocks(square, waits):
    blocks = PANEL // BLOCK
    rest = square
    inverses, columns = [], []
    for k in range(blocks):
        block = rest[:BLOCK, :BLOCK]
        if waits[k] is not None:
            block = after(block, waits[k])
        inverse = factor_inverse(block)
        inverses.append(inverse)
        if k + 1 < blocks:
            column = precise(rest[BLOCK:, :BLOCK], inverse, 1)
            columns.append(column)
            rest = rest[BLOCK:, BLOCK:] - precise(column, column, 1)
    return inverses, columns


def lower_inverse(inverses, columns):
    blocks = PANEL // BLOCK
    rows = [inverses[0]]
    for k in range(1, blocks):
        left = jnp.concatenate(
            [columns[j][(k - j - 1) * BLOCK : (k - j) * BLOCK] for j in range(k)],
            axis=1,
        )
        upper = jnp.concatenate(
            [
                jnp.pad(rows[j], ((0, 0), (0, (k - 1 - j) * BLOCK)))
                for j in range(k)
            ],
            axis=0,
        )
        rows.append(
            jnp.concatenate(
                [-precise(inverses[k], precise(left, upper, 0), 0), inverses[k]],
                axis=1,
            )
        )
    return jnp.concatenate(
        [
            jnp.pad(rows[j], ((0, 0), (0, (blocks - 1 - j) * BLOCK)))
            for j in range(blocks)
        ],
        axis=0,
    )


LOWER = [(i, j) for i in range(PANEL // BLOCK) for j in range(i + 1)]


def stack_lower(square):
    return jnp.concatenate(
        [
            square[i * BLOCK : (i + 1) * BLOCK, j * BLOCK : (j + 1) * BLOCK]
            for i, j in LOWER
        ],
        axis=0,
    )


def unstack_lower(stack):
    blocks = PANEL // BLOCK
    place = {pair: n for n, pair in enumerate(LOWER)}
    rows = []
    for i in range(blocks):
        row = []
        for j in range(blocks):
            if j <= i:
                n = place[(i, j)]
                row.append(stack[n * BLOCK : (n + 1) * BLOCK])
            else:
                row.append(jnp.zeros((BLOCK, BLOCK), stack.dtype))
        rows.append(jnp.concatenate(row, axis=1))
    return jnp.concatenate(rows, axis=0)


def select_order(blocks, member):
    bit = 1
    while bit < len(blocks):
        swap = (member & bit) != 0
        blocks = [
            jnp.where(swap, blocks[k ^ bit], blocks[k]) for k in range(len(blocks))
        ]
        bit *= 2
    return blocks


def after(x, done):
    return lax.optimization_barrier((x, done))[0]


def times(a, b):
    return lax.dot_general(
        a, b, (((1,), (1,)), ((), ())), preferred_element_type=jnp.float32
    )


def make(n_rows, n_snp):
    lines = n_rows // GROUP

    def rows_xor(x, bits):
        return lax.ppermute(x, "rows", [(r, r ^ bits) for r in range(n_rows)])

    def line_send(x, pairs):
        moves = [
            (a * GROUP + q, b * GROUP + q) for a, b in pairs for q in range(GROUP)
        ]
        return lax.ppermute(x, "rows", moves)

    def snp_xor(x, bits):
        return lax.ppermute(x, "snp", [(s, s ^ bits) for s in range(n_snp)])

    def from_first_snp(x, rank):
        got = x
        for s in range(1, n_snp):
            moved = lax.ppermute(x, "snp", [(0, s)])
            got = jnp.where(rank == s, moved, got)
        return got

    def group_gather(x):
        core = rows_xor(x, 1)
        other = rows_xor(x, 2)
        return [x, core, other, rows_xor(other, 1)]

    def rows_sum(x):
        bit = 1
        while bit < n_rows:
            if bit * 2 < n_rows:
                parts = [x] + [rows_xor(x, bit * k) for k in (1, 2, 3)]
                x = (parts[0] + parts[1]) + (parts[2] + parts[3])
                bit *= 4
            else:
                x = x + rows_xor(x, bit)
                bit *= 2
        return x

    def snp_sum(x):
        bit = 1
        while bit < n_snp:
            x = x + snp_xor(x, bit)
            bit *= 2
        return x

    def from_plane_0(x, z):
        got = x
        for target in range(1, lines):
            got = jnp.where(z == target, line_send(x, [(0, target)]), got)
        return got

    def per_device(genotypes, relationship):
        snps, own = genotypes.shape
        width = relationship.shape[1]
        rank = lax.axis_index("rows")
        col = lax.axis_index("snp")
        q = rank % GROUP
        z = rank // GROUP
        part = lines // n_snp

        rel_own = from_first_snp(relationship[:, :PANEL], col)

        called = genotypes >= 0
        dosage = jnp.where(called, genotypes, 0.0)
        stats = jnp.stack(
            [jnp.sum(dosage, axis=1), jnp.sum(called.astype(jnp.float32), axis=1)]
        )
        rel_other = rows_xor(rel_own, 2)
        stats, rel_other = lax.optimization_barrier((rows_sum(stats), rel_other))
        rel_panel = [rel_own, rows_xor(rel_own, 1), rel_other, rows_xor(rel_other, 1)]
        rel_panel = jnp.concatenate(select_order(rel_panel, q), axis=0)[:PANEL]
        frequency = stats[0] / (2.0 * stats[1])
        scale_total = snp_sum(jnp.sum(2.0 * frequency * (1.0 - frequency)).reshape(1, 1))
        inverse = (1.0 / scale_total)[0, 0]
        gt = lax.optimization_barrier(genotypes.T)
        centered = jnp.where(gt >= 0, gt - 2.0 * frequency[None, :], 0.0).astype(
            jnp.bfloat16
        )

        around = [(a, (a - 1) % lines) for a in range(lines)]
        ring = [centered, line_send(centered, around)]
        plane = jnp.concatenate(select_order(group_gather(centered), q), axis=0)
        plane, ring[1], rel_panel, inverse = lax.optimization_barrier(
            (plane, ring[1], rel_panel, inverse)
        )

        share = len(LOWER) * BLOCK // GROUP
        piece = share // n_snp
        partial = stack_lower(times(plane[:PANEL], plane[:PANEL]))
        partial = lax.dynamic_slice_in_dim(partial, q * share, share, 0)
        rel_lower = stack_lower(
            rel_panel
            + jnp.where(
                lax.broadcasted_iota(jnp.int32, rel_panel.shape, 0)
                == lax.broadcasted_iota(jnp.int32, rel_panel.shape, 1),
                RIDGE,
                0.0,
            )
        )
        total = lax.dynamic_slice_in_dim(partial, col * piece, piece, 0)
        for bits in range(1, n_snp):
            total = total + snp_xor(
                lax.dynamic_slice_in_dim(partial, (col ^ bits) * piece, piece, 0), bits
            )
        total = total * inverse + lax.dynamic_slice_in_dim(
            rel_lower, q * share + col * piece, piece, 0
        )
        total = from_plane_0(total, z)
        ring.append(line_send(ring[1], around))
        total, ring[2] = lax.optimization_barrier((total, ring[2]))

        total = select_order(
            [total] + [snp_xor(total, bits) for bits in range(1, n_snp)], col
        )
        total = jnp.concatenate(total, axis=0)
        total = jnp.concatenate(select_order(group_gather(total), q), axis=0)
        for step in range(2, lines - 1):
            ring.append(line_send(ring[-1], around))
        total, line = lax.optimization_barrier((total, jnp.stack(ring)))
        diag_block = unstack_lower(total)

        def of_line(stack, target):
            return lax.dynamic_index_in_dim(
                stack, jnp.mod(target - z, lines), 0, keepdims=False
            )

        def columns_of(stack, target):
            return jnp.concatenate(
                [of_line(stack, target * part + j) for j in range(part)], axis=0
            )

        cols = [columns_of(line, col ^ bits) for bits in range(n_snp)]
        leaving = [times(plane, cols[bits]) for bits in range(1, n_snp)]
        gram_got = [snp_xor(leaving[bits - 1], bits) for bits in range(1, n_snp)]

        rel_ring = [rel_own]
        for step in range(lines - 1):
            block = rel_ring[-1]
            if step == 0:
                block = after(block, leaving)
            rel_ring.append(line_send(block, around))
        rel_side = columns_of(jnp.stack(rel_ring), col)

        first = of_line(line, 0)
        head = jnp.concatenate(select_order(group_gather(first), q), axis=0)[:PANEL]
        lead = times(centered, head)
        side_out = [times(cols[bits], head) for bits in range(1, n_snp)]
        lead_got = snp_sum(lead)
        side = times(cols[0], head)
        for bits in range(1, n_snp):
            side = side + snp_xor(side_out[bits - 1], bits)

        own_columns = rel_own + lead_got * inverse
        ids = rank * own + lax.broadcasted_iota(jnp.int32, own_columns.shape, 0)
        own_columns = own_columns + jnp.where(
            ids == lax.broadcasted_iota(jnp.int32, own_columns.shape, 1), RIDGE, 0.0
        )
        side = rel_side + side * inverse
        side_rows = lax.broadcasted_iota(jnp.int32, side.shape, 0)
        side_ids = (
            (col * part + side_rows // own) * GROUP + q
        ) * own + side_rows % own
        side = side + jnp.where(
            side_ids == lax.broadcasted_iota(jnp.int32, side.shape, 1), RIDGE, 0.0
        )
        side = select_order(group_gather(side), q)
        side = jnp.stack([s.reshape(part, own, PANEL) for s in side], axis=1)
        side = side.reshape(width, PANEL)

        inverses, columns = factor_blocks(
            diag_block, [leaving, head, (lead, side_out, gram_got), None]
        )

        gram = times(plane, cols[0])
        for got in gram_got:
            gram = gram + got
        gram = gram.reshape(GROUP, own, part * own)
        pieces = [
            lax.dynamic_index_in_dim(gram, q ^ k, 0, keepdims=False)
            for k in range(GROUP)
        ]
        pieces = [pieces[0]] + [rows_xor(pieces[k], k) for k in range(1, GROUP)]
        pieces = select_order(pieces, q)
        summed = jnp.stack([p.reshape(own, part, own) for p in pieces], axis=2)
        summed = summed.reshape(own, width)
        row_ids = rank * own + lax.broadcasted_iota(jnp.int32, (own, width), 0)
        col_ids = col * width + lax.broadcasted_iota(jnp.int32, (own, width), 1)
        combined = relationship + summed * inverse
        combined = combined + jnp.where(row_ids == col_ids, RIDGE, 0.0)

        whole = lower_inverse(inverses, columns)
        panel = precise(own_columns, whole, 1)
        weights = precise(panel, whole, 0)
        updated = combined - precise(weights, side, 1)
        return updated, panel

    return per_device


def solution(mesh):
    return jax.shard_map(
        make(mesh.shape["rows"], mesh.shape["snp"]),
        mesh=mesh,
        in_specs=(P("snp", "rows"), P("rows", "snp")),
        out_specs=(P("rows", "snp"), P("rows", None)),
        check_vma=False,
    )
```

```python
import functools

import jax
import jax.numpy as jnp
from jax import lax
from jax.experimental import pallas as pl
from jax.experimental.pallas import tpu as pltpu
from jax.sharding import PartitionSpec as P

PANEL = 512
RIDGE = 0.25
GROUP = 4


BLOCK = 128
SUB = 8


def factor_kernel(a_ref, *refs):
    out_ref, work = refs[-2:]
    work[...] = a_ref[...]
    lane = lax.broadcasted_iota(jnp.int32, (SUB, BLOCK), 1)
    for g in range(BLOCK // SUB):
        at = g * SUB
        own = work[at : at + SUB, :]
        inside = (lane >= at) & (lane < at + SUB)
        rows = [jnp.broadcast_to(own[u : u + 1, :], (SUB, BLOCK)) for u in range(SUB)]
        e = [
            [
                jnp.broadcast_to(rows[t][:, at + u : at + u + 1], (SUB, BLOCK))
                for t in range(u + 1)
            ]
            for u in range(SUB)
        ]
        rows = [
            jnp.where(inside, jnp.where(lane == at + u, 1.0, 0.0), rows[u])
            for u in range(SUB)
        ]
        low = [[None] * SUB for _ in range(SUB)]
        scale = []
        for t in range(SUB):
            r = lax.rsqrt(e[t][t])
            scale.append(r)
            for u in range(t + 1, SUB):
                low[u][t] = e[u][t] * r
            for u in range(t + 1, SUB):
                for v in range(t + 1, u + 1):
                    e[u][v] = e[u][v] - low[u][t] * low[v][t]
            rows[t] = rows[t] * r
            for u in range(t + 1, SUB):
                rows[u] = rows[u] - low[u][t] * rows[t]
        for below in range(g + 1, BLOCK // SUB):
            base = below * SUB
            rest = work[base : base + SUB, :]
            c = [
                jnp.broadcast_to(rest[:, at + t : at + t + 1], (SUB, BLOCK))
                for t in range(SUB)
            ]
            rest = jnp.where(inside, 0.0, rest)
            for t in range(SUB):
                c[t] = c[t] * scale[t]
                for s in range(t + 1, SUB):
                    c[s] = c[s] - low[s][t] * c[t]
                rest = rest - c[t] * rows[t]
            work[base : base + SUB, :] = rest
        for t in range(SUB):
            work[at + t : at + t + 1, :] = rows[t][0:1, :]
    i = lax.broadcasted_iota(jnp.int32, (BLOCK, BLOCK), 0)
    j = lax.broadcasted_iota(jnp.int32, (BLOCK, BLOCK), 1)
    out_ref[...] = jnp.where(j <= i, work[...], 0.0)


def factor_inverse(a, waits):
    return pl.pallas_call(
        factor_kernel,
        out_shape=jax.ShapeDtypeStruct((BLOCK, BLOCK), jnp.float32),
        in_specs=[pl.BlockSpec(memory_space=pltpu.VMEM)]
        + [pl.BlockSpec(memory_space=pl.ANY)] * len(waits),
        out_specs=pl.BlockSpec(memory_space=pltpu.VMEM),
        scratch_shapes=[pltpu.VMEM((BLOCK, BLOCK), jnp.float32)],
        cost_estimate=pl.CostEstimate(flops=4_000_000, bytes_accessed=131072, transcendentals=128),
    )(a, *waits)


def precise(a, b, contract):
    return lax.dot_general(
        a,
        b,
        (((1,), (contract,)), ((), ())),
        precision=lax.Precision.HIGHEST,
        preferred_element_type=jnp.float32,
    )


def factor_blocks(square, waits):
    blocks = PANEL // BLOCK
    rest = square
    inverses, columns = [], []
    for k in range(blocks):
        block = rest[:BLOCK, :BLOCK]
        inverse = factor_inverse(block, waits[k])
        inverses.append(inverse)
        if k + 1 < blocks:
            column = precise(rest[BLOCK:, :BLOCK], inverse, 1)
            columns.append(column)
            rest = rest[BLOCK:, BLOCK:] - precise(column, column, 1)
    return inverses, columns


def lower_inverse(inverses, columns):
    blocks = PANEL // BLOCK
    rows = [inverses[0]]
    for k in range(1, blocks):
        left = jnp.concatenate(
            [columns[j][(k - j - 1) * BLOCK : (k - j) * BLOCK] for j in range(k)],
            axis=1,
        )
        upper = jnp.concatenate(
            [
                jnp.pad(rows[j], ((0, 0), (0, (k - 1 - j) * BLOCK)))
                for j in range(k)
            ],
            axis=0,
        )
        rows.append(
            jnp.concatenate(
                [-precise(inverses[k], precise(left, upper, 0), 0), inverses[k]],
                axis=1,
            )
        )
    return jnp.concatenate(
        [
            jnp.pad(rows[j], ((0, 0), (0, (blocks - 1 - j) * BLOCK)))
            for j in range(blocks)
        ],
        axis=0,
    )


def select_order(blocks, member):
    bit = 1
    while bit < len(blocks):
        swap = (member & bit) != 0
        blocks = [
            jnp.where(swap, blocks[k ^ bit], blocks[k]) for k in range(len(blocks))
        ]
        bit *= 2
    return blocks


def nothing(*refs):
    pass


def tip(x):
    return x[:8, :BLOCK]


def after(x, *done):
    here = pl.BlockSpec(memory_space=pl.ANY)
    return pl.pallas_call(
        nothing,
        out_shape=jax.ShapeDtypeStruct(x.shape, x.dtype),
        in_specs=[here] * (1 + len(done)),
        out_specs=here,
        input_output_aliases={0: 0},
    )(x, *done)


def times(a, b):
    return lax.dot_general(
        a, b, (((1,), (1,)), ((), ())), preferred_element_type=jnp.float32
    )


def update_kernel(own, part, place, scale, rel, weights, *refs):
    pieces, sides, out = refs[:GROUP], refs[GROUP : 2 * GROUP], refs[2 * GROUP]
    i = lax.broadcasted_iota(jnp.int32, (own, own), 0)
    j = lax.broadcasted_iota(jnp.int32, (own, own), 1)
    ridge = jnp.where(i == j, RIDGE, 0.0)

    def for_member(mine):
        for k in range(GROUP):
            product = precise(weights[...], sides[k][...], 1)
            for n in range(part):
                at = (n * GROUP + (mine ^ k)) * own
                cut = slice(n * own, (n + 1) * own)
                value = rel[:, at : at + own] + pieces[k][:, cut] * scale[0]
                value = value - product[:, cut]
                if k == 0:
                    value = value + ridge * jnp.where(place[1] == n, 1.0, 0.0)
                out[:, at : at + own] = value

    for mine in range(GROUP):
        pl.when(place[0] == mine)(functools.partial(for_member, mine))


def final_update(place, scale, rel, weights, pieces, sides):
    own, width = rel.shape
    part = width // (GROUP * own)
    smem = pl.BlockSpec(memory_space=pltpu.SMEM)
    vmem = pl.BlockSpec(memory_space=pltpu.VMEM)
    return pl.pallas_call(
        functools.partial(update_kernel, own, part),
        out_shape=jax.ShapeDtypeStruct((own, width), jnp.float32),
        in_specs=[smem, smem] + [vmem] * (2 + 2 * GROUP),
        out_specs=vmem,
        compiler_params=pltpu.CompilerParams(vmem_limit_bytes=48 * 2**20),
        cost_estimate=pl.CostEstimate(
            flops=2 * own * width * PANEL, bytes_accessed=4 * width * PANEL, transcendentals=0
        ),
    )(place, scale, rel, weights, *pieces, *sides)


def make(n_rows, n_snp):
    lines = n_rows // GROUP

    def rows_xor(x, bits):
        return lax.ppermute(x, "rows", [(r, r ^ bits) for r in range(n_rows)])

    def snp_xor(x, bits):
        return lax.ppermute(x, "snp", [(s, s ^ bits) for s in range(n_snp)])

    def from_first_snp(x, rank):
        got = x
        for s in range(1, n_snp):
            got = jnp.where(rank == s, lax.ppermute(x, "snp", [(0, s)]), got)
        return got

    def group_gather(x):
        core = rows_xor(x, 1)
        other = rows_xor(x, 2)
        return [x, core, other, rows_xor(other, 1)]

    def rows_sum(x):
        bit = 1
        while bit < n_rows:
            if bit * 2 < n_rows:
                parts = [x] + [rows_xor(x, bit * k) for k in (1, 2, 3)]
                x = (parts[0] + parts[1]) + (parts[2] + parts[3])
                bit *= 4
            else:
                x = x + rows_xor(x, bit)
                bit *= 2
        return x

    def snp_sum(x):
        bit = 1
        while bit < n_snp:
            x = x + snp_xor(x, bit)
            bit *= 2
        return x

    def from_plane_0(x, z):
        bit = lines // 2
        while bit >= 1:
            moves = [
                (a * GROUP + k, (a + bit) * GROUP + k)
                for a in range(0, lines, 2 * bit)
                for k in range(GROUP)
            ]
            x = jnp.where((z & bit) != 0, lax.ppermute(x, "rows", moves), x)
            bit //= 2
        return x

    def per_device(genotypes, relationship):
        snps, own = genotypes.shape
        width = relationship.shape[1]
        rank = lax.axis_index("rows")
        col = lax.axis_index("snp")
        q = rank % GROUP
        z = rank // GROUP
        part = lines // n_snp

        rel_own = from_first_snp(relationship[:, :PANEL], col)

        called = genotypes >= 0
        dosage = jnp.where(called, genotypes, 0.0)
        stats = jnp.stack(
            [jnp.sum(dosage, axis=1), jnp.sum(called.astype(jnp.float32), axis=1)]
        )
        stats = rows_sum(stats)
        frequency = stats[0] / (2.0 * stats[1])
        scale_part = jnp.sum(2.0 * frequency * (1.0 - frequency))
        gt = lax.optimization_barrier(genotypes.T)
        centered = jnp.where(gt >= 0, gt - 2.0 * frequency[None, :], 0.0).astype(
            jnp.bfloat16
        )

        far = lines // 2
        core = rows_xor(centered, 1)
        other = rows_xor(centered, 2)
        near = {k: rows_xor(centered, k * GROUP) for k in range(1, far)}
        half = snps // 2
        far_parts = [
            rows_xor(centered[:, :half], far * GROUP),
            rows_xor(centered[:, half:], far * GROUP),
        ]
        other = after(other, far_parts[0], *near.values())
        plane = [centered, core, other, rows_xor(other, 1)]
        plane = jnp.concatenate(select_order(plane, q), axis=0)

        piece = PANEL // n_snp
        rows = times(centered, plane[:PANEL])
        rows = jnp.concatenate(
            [rows, jnp.broadcast_to(scale_part.reshape(1, 1), (8, PANEL))], axis=0
        )
        total = lax.dynamic_slice_in_dim(rows, col * piece, piece, 1)
        for bits in range(1, n_snp):
            total = total + snp_xor(
                lax.dynamic_slice_in_dim(rows, (col ^ bits) * piece, piece, 1), bits
            )
        inverse = 1.0 / total[own, 0]
        ids = rank * own + lax.broadcasted_iota(jnp.int32, rel_own.shape, 0)
        rel_own = rel_own + jnp.where(
            ids == lax.broadcasted_iota(jnp.int32, rel_own.shape, 1), RIDGE, 0.0
        )
        total = total[:own] * inverse + lax.dynamic_slice_in_dim(
            rel_own, col * piece, piece, 1
        )
        far_parts[1] = after(far_parts[1], rows)
        total = from_plane_0(after(total, far_parts[1]), z)

        passed = jnp.concatenate(far_parts, axis=1)
        line = {0: centered, far: passed, **near}
        for k in range(1, far):
            line[far + k] = after(rows_xor(passed, k * GROUP), total)
        line = [line[k] for k in range(lines)]
        first = select_order(line, z)[0]
        line = select_order(line, z ^ (col * part))
        line = [
            jnp.concatenate(line[bits * part : (bits + 1) * part], axis=0)
            for bits in range(n_snp)
        ]

        head_other = rows_xor(first, 2)
        head = [first, rows_xor(first, 1), head_other, rows_xor(head_other, 1)]
        head = jnp.concatenate(select_order(head, q), axis=0)[:PANEL]
        lead = times(centered, head)
        side_out = [times(line[bits], head) for bits in range(1, n_snp)]
        lead_got = snp_sum(lead)
        side = times(line[0], head)
        for bits in range(1, n_snp):
            side = side + snp_xor(side_out[bits - 1], bits)

        total = select_order(
            [total] + [snp_xor(total, bits) for bits in range(1, n_snp)], col
        )
        total = jnp.concatenate(total, axis=1)

        leaving = [
            times(plane, after(line[bits], total)) for bits in range(1, n_snp)
        ]
        gram_got = [snp_xor(leaving[bits - 1], bits) for bits in range(1, n_snp)]

        rel_far = rows_xor(after(rel_own, line[0]), far * GROUP)
        rel_line = {0: rel_own, far: rel_far}
        for k in range(1, far):
            rel_line[k] = rows_xor(rel_own, k * GROUP)
        total = after(
            total, head_other, rel_far, *[rel_line[k] for k in range(1, far)]
        )
        for k in range(1, far):
            rel_line[far + k] = rows_xor(rel_far, k * GROUP)
        total = jnp.concatenate(select_order(group_gather(total), q), axis=0)
        diag_block = total[:PANEL]

        rel_side = [rel_line[k] for k in range(lines)]
        rel_side = select_order(rel_side, z ^ (col * part))[:part]
        rel_side = jnp.concatenate(rel_side, axis=0)
        side = rel_side + side * inverse
        own_columns = rel_own + lead_got * inverse

        gram = times(plane, line[0])
        for got in gram_got:
            gram = gram + got
        gram = gram.reshape(GROUP, own, part * own)
        pieces = [
            lax.dynamic_index_in_dim(gram, q ^ k, 0, keepdims=False)
            for k in range(GROUP)
        ]

        inverses, columns = factor_blocks(
            diag_block,
            [
                [tip(lead)] + [tip(x) for x in side_out] + [tip(rel_side)],
                [tip(pieces[1])],
                [tip(side)],
                [],
            ],
        )
        pieces = [pieces[0]] + [rows_xor(pieces[k], k) for k in range(1, GROUP)]
        sides = group_gather(side)

        whole = lower_inverse(inverses, columns)
        panel = precise(own_columns, whole, 1)
        weights = precise(panel, whole, 0)
        place = jnp.stack([q, z - col * part]).astype(jnp.int32)
        updated = final_update(
            place, inverse.reshape(1), relationship, weights, pieces, sides
        )
        return updated, panel

    return per_device


def solution(mesh):
    return jax.shard_map(
        make(mesh.shape["rows"], mesh.shape["snp"]),
        mesh=mesh,
        in_specs=(P("snp", "rows"), P("rows", "snp")),
        out_specs=(P("rows", "snp"), P("rows", None)),
        check_vma=False,
    )
```

```python
import functools

import jax
import jax.numpy as jnp
from jax import lax
from jax.experimental import pallas as pl
from jax.experimental.pallas import tpu as pltpu
from jax.sharding import PartitionSpec as P

PANEL = 512
RIDGE = 0.25
GROUP = 4
BLOCK = 128
SUB = 8

VMEM = pl.BlockSpec(memory_space=pltpu.VMEM)
SMEM = pl.BlockSpec(memory_space=pltpu.SMEM)
ANYWHERE = pl.BlockSpec(memory_space=pl.ANY)
ROOM = pltpu.CompilerParams(vmem_limit_bytes=40 * 2**20)


def precise(a, b, contract):
    return lax.dot_general(
        a,
        b,
        (((1,), (contract,)), ((), ())),
        precision=lax.Precision.HIGHEST,
        preferred_element_type=jnp.float32,
    )


def times(a, b):
    return lax.dot_general(
        a, b, (((1,), (1,)), ((), ())), preferred_element_type=jnp.float32
    )


def cost(flops):
    return pl.CostEstimate(flops=flops, bytes_accessed=131072, transcendentals=0)


def f32(*shape):
    return jax.ShapeDtypeStruct(shape, jnp.float32)


def invert_factor(work):
    lane = lax.broadcasted_iota(jnp.int32, (SUB, BLOCK), 1)
    for g in range(BLOCK // SUB):
        at = g * SUB
        own = work[at : at + SUB, :]
        inside = (lane >= at) & (lane < at + SUB)
        rows = [jnp.broadcast_to(own[u : u + 1, :], (SUB, BLOCK)) for u in range(SUB)]
        e = [
            [
                jnp.broadcast_to(rows[t][:, at + u : at + u + 1], (SUB, BLOCK))
                for t in range(u + 1)
            ]
            for u in range(SUB)
        ]
        rows = [
            jnp.where(inside, jnp.where(lane == at + u, 1.0, 0.0), rows[u])
            for u in range(SUB)
        ]
        low = [[None] * SUB for _ in range(SUB)]
        scale = []
        for t in range(SUB):
            r = lax.rsqrt(e[t][t])
            scale.append(r)
            for u in range(t + 1, SUB):
                low[u][t] = e[u][t] * r
            for u in range(t + 1, SUB):
                for v in range(t + 1, u + 1):
                    e[u][v] = e[u][v] - low[u][t] * low[v][t]
            rows[t] = rows[t] * r
            for u in range(t + 1, SUB):
                rows[u] = rows[u] - low[u][t] * rows[t]
        for below in range(g + 1, BLOCK // SUB):
            base = below * SUB
            rest = work[base : base + SUB, :]
            c = [
                jnp.broadcast_to(rest[:, at + t : at + t + 1], (SUB, BLOCK))
                for t in range(SUB)
            ]
            rest = jnp.where(inside, 0.0, rest)
            for t in range(SUB):
                c[t] = c[t] * scale[t]
                for s in range(t + 1, SUB):
                    c[s] = c[s] - low[s][t] * c[t]
                rest = rest - c[t] * rows[t]
            work[base : base + SUB, :] = rest
        for t in range(SUB):
            work[at + t : at + t + 1, :] = rows[t][0:1, :]


def factor_step_kernel(size, n_in, *refs):
    place, squares = refs[0], refs[1 : 1 + n_in]
    if size > BLOCK:
        inverse, column, rest, work = refs[-4:]
    else:
        inverse, work = refs[-2:]
    if n_in == 1:
        square = squares[0]
    else:
        square = rest_in = refs[-5]
        own = squares[0].shape[0]

        def assemble(mine):
            for k in range(GROUP):
                start = (mine ^ k) * own
                if start < size:
                    stop = min(start + own, size)
                    rest_in[start:stop, :] = squares[k][: stop - start, :]

        for mine in range(GROUP):
            pl.when(place[0] == mine)(functools.partial(assemble, mine))
    work[...] = square[:BLOCK, :BLOCK]
    invert_factor(work)
    i = lax.broadcasted_iota(jnp.int32, (BLOCK, BLOCK), 0)
    j = lax.broadcasted_iota(jnp.int32, (BLOCK, BLOCK), 1)
    value = jnp.where(j <= i, work[...], 0.0)
    inverse[...] = value
    if size > BLOCK:
        below = precise(square[BLOCK:, :BLOCK], value, 1)
        column[...] = below
        for n in range(size // BLOCK - 1):
            cut = slice(n * BLOCK, size - BLOCK)
            across = slice(n * BLOCK, (n + 1) * BLOCK)
            rest[cut, across] = square[
                (n + 1) * BLOCK :, (n + 1) * BLOCK : (n + 2) * BLOCK
            ] - precise(below[n * BLOCK :, :], below[across, :], 1)


def factor_step(place, squares, size, waits):
    left = size - BLOCK
    out_shape = [f32(BLOCK, BLOCK)]
    scratch = [pltpu.VMEM((BLOCK, BLOCK), jnp.float32)]
    if left:
        out_shape += [f32(left, BLOCK), f32(left, left)]
    n_in = len(squares)
    kernel = functools.partial(factor_step_kernel, size, n_in)
    if n_in > 1:

        def kernel(*refs):
            *others, work, whole = refs
            outs = 3 if left else 1
            return factor_step_kernel(
                size, n_in, *others[:-outs], whole, *others[-outs:], work
            )

        scratch.append(pltpu.VMEM((size, size), jnp.float32))
    return pl.pallas_call(
        kernel,
        out_shape=out_shape,
        in_specs=[SMEM] + [VMEM] * n_in + [ANYWHERE] * len(waits),
        out_specs=[VMEM] * len(out_shape),
        scratch_shapes=scratch,
        compiler_params=ROOM,
        cost_estimate=cost(6_000_000_000),
    )(place, *squares, *waits)


def solve_kernel(blocks, columns, *refs):
    inverses, below = refs[:blocks], refs[blocks : 2 * blocks - 1]
    panel, weights = refs[-2:]
    found = []
    for k in range(blocks):
        total = columns[:, k * BLOCK : (k + 1) * BLOCK]
        for j in range(k):
            start = (k - j - 1) * BLOCK
            total = total - precise(found[j], below[j][start : start + BLOCK, :], 1)
        found.append(precise(total, inverses[k][...], 1))
        panel[:, k * BLOCK : (k + 1) * BLOCK] = found[k]
    for k in reversed(range(blocks)):
        total = found[k]
        for j in range(k + 1, blocks):
            start = (j - k - 1) * BLOCK
            total = total - precise(found[j], below[k][start : start + BLOCK, :], 0)
        found[k] = precise(total, inverses[k][...], 0)
        weights[:, k * BLOCK : (k + 1) * BLOCK] = found[k]


def solve(columns, inverses, below):
    own = columns.shape[0]
    return pl.pallas_call(
        functools.partial(solve_kernel, len(inverses)),
        out_shape=[f32(own, PANEL), f32(own, PANEL)],
        in_specs=[VMEM] * (2 * len(inverses)),
        out_specs=[VMEM, VMEM],
        compiler_params=ROOM,
        cost_estimate=cost(4 * own * PANEL * PANEL),
    )(columns, *inverses, *below)


def head_kernel(n_left, sizes, place, *refs):
    left, head = refs[:n_left], refs[n_left : n_left + GROUP]
    outs = refs[-len(sizes) :]
    own = head[0].shape[0]

    def for_member(mine):
        for k in range(GROUP):
            start = (mine ^ k) * own
            width = min(own, PANEL - start)
            if width > 0:
                at = 0
                for out, count in zip(outs, sizes):
                    for n in range(count):
                        product = times(left[at][...], head[k][...])
                        out[n * own : (n + 1) * own, start : start + width] = product[
                            :, :width
                        ]
                        at += 1

    for mine in range(GROUP):
        pl.when(place[0] == mine)(functools.partial(for_member, mine))


def head_products(place, groups, head, waits):
    own = head[0].shape[0]
    left = [x for group in groups for x in group]
    sizes = [len(group) for group in groups]
    return pl.pallas_call(
        functools.partial(head_kernel, len(left), sizes),
        out_shape=[f32(n * own, PANEL) for n in sizes],
        in_specs=[SMEM] + [VMEM] * (len(left) + GROUP) + [ANYWHERE] * len(waits),
        out_specs=[VMEM] * len(sizes),
        compiler_params=ROOM,
        cost_estimate=cost(2 * len(left) * own * PANEL * head[0].shape[1]),
    )(place, *left, *head, *waits)


def gram_kernel(n_cols, n_more, *refs):
    plane, cols = refs[:GROUP], refs[GROUP : GROUP + n_cols]
    more = refs[GROUP + n_cols : GROUP + n_cols + n_more]
    outs = refs[-GROUP:]
    own = plane[0].shape[0]
    for k in range(GROUP):
        for j in range(n_cols):
            product = times(cols[j][...], plane[k][...])
            across = slice(j * own, (j + 1) * own)
            for x in more:
                product = product + x[across, k * own : (k + 1) * own]
            outs[k][:, across] = product.T


def gram_out_kernel(n_cols, *refs):
    plane, cols, out = refs[:GROUP], refs[GROUP : GROUP + n_cols], refs[-1]
    own = plane[0].shape[0]
    for k in range(GROUP):
        for j in range(n_cols):
            out[j * own : (j + 1) * own, k * own : (k + 1) * own] = times(
                cols[j][...], plane[k][...]
            )


def gram_products(plane, cols, more, waits):
    own, depth = plane[0].shape
    width = len(cols) * own
    if more is None:
        kernel = functools.partial(gram_out_kernel, len(cols))
        out_shape, out_specs, more = f32(width, GROUP * own), VMEM, []
    else:
        kernel = functools.partial(gram_kernel, len(cols), len(more))
        out_shape, out_specs = [f32(own, width)] * GROUP, [VMEM] * GROUP
    return pl.pallas_call(
        kernel,
        out_shape=out_shape,
        in_specs=[VMEM] * (GROUP + len(cols) + len(more))
        + [ANYWHERE] * len(waits),
        out_specs=out_specs,
        compiler_params=ROOM,
        cost_estimate=cost(2 * GROUP * own * width * depth),
    )(*plane, *cols, *more, *waits)


def update_kernel(own, part, place, scale, rel, weights, *refs):
    pieces, sides, out = refs[:GROUP], refs[GROUP : 2 * GROUP], refs[2 * GROUP]
    i = lax.broadcasted_iota(jnp.int32, (own, own), 0)
    j = lax.broadcasted_iota(jnp.int32, (own, own), 1)
    ridge = jnp.where(i == j, RIDGE, 0.0)

    def for_member(mine):
        for k in range(GROUP):
            product = precise(weights[...], sides[k][...], 1)
            for n in range(part):
                at = (n * GROUP + (mine ^ k)) * own
                cut = slice(n * own, (n + 1) * own)
                value = rel[:, at : at + own] + pieces[k][:, cut] * scale[0]
                value = value - product[:, cut]
                if k == 0:
                    value = value + ridge * jnp.where(place[1] == n, 1.0, 0.0)
                out[:, at : at + own] = value

    for mine in range(GROUP):
        pl.when(place[0] == mine)(functools.partial(for_member, mine))


def final_update(place, scale, rel, weights, pieces, sides):
    own, width = rel.shape
    part = width // (GROUP * own)
    return pl.pallas_call(
        functools.partial(update_kernel, own, part),
        out_shape=f32(own, width),
        in_specs=[SMEM, SMEM] + [VMEM] * (2 + 2 * GROUP),
        out_specs=VMEM,
        compiler_params=ROOM,
        cost_estimate=cost(2 * own * width * PANEL),
    )(place, scale, rel, weights, *pieces, *sides)


def nothing(*refs):
    pass


def after(x, *done):
    return pl.pallas_call(
        nothing,
        out_shape=jax.ShapeDtypeStruct(x.shape, x.dtype),
        in_specs=[ANYWHERE] * (1 + len(done)),
        out_specs=ANYWHERE,
        input_output_aliases={0: 0},
    )(x, *done)


def select_order(blocks, member):
    bit = 1
    while bit < len(blocks):
        swap = (member & bit) != 0
        blocks = [
            jnp.where(swap, blocks[k ^ bit], blocks[k]) for k in range(len(blocks))
        ]
        bit *= 2
    return blocks


def make(n_rows, n_snp):
    lines = n_rows // GROUP
    part = lines // n_snp
    far = lines // 2

    def rows_xor(x, bits):
        return lax.ppermute(x, "rows", [(r, r ^ bits) for r in range(n_rows)])

    def snp_xor(x, bits):
        return lax.ppermute(x, "snp", [(s, s ^ bits) for s in range(n_snp)])

    def from_first_snp(x, rank):
        got = x
        for s in range(1, n_snp):
            got = jnp.where(rank == s, lax.ppermute(x, "snp", [(0, s)]), got)
        return got

    def group_gather(x):
        core = rows_xor(x, 1)
        other = rows_xor(x, 2)
        return [x, core, other, rows_xor(other, 1)]

    def line_gather(x, hold):
        near = {k: rows_xor(x, k * GROUP) for k in range(1, far)}
        passed = hold(rows_xor(x, far * GROUP), list(near.values()))
        parts = {0: x, far: passed, **near}
        for k in range(1, far):
            parts[far + k] = rows_xor(passed, k * GROUP)
        return [parts[k] for k in range(lines)]

    def rows_sum(x):
        bit = 1
        while bit < n_rows:
            if bit * 2 < n_rows:
                parts = [x] + [rows_xor(x, bit * k) for k in (1, 2, 3)]
                x = (parts[0] + parts[1]) + (parts[2] + parts[3])
                bit *= 4
            else:
                x = x + rows_xor(x, bit)
                bit *= 2
        return x

    def snp_sum(x):
        bit = 1
        while bit < n_snp:
            x = x + snp_xor(x, bit)
            bit *= 2
        return x

    def per_device(genotypes, relationship):
        own = genotypes.shape[1]
        rank = lax.axis_index("rows")
        col = lax.axis_index("snp")
        q = rank % GROUP
        z = rank // GROUP
        place = jnp.stack([q, z - col * part]).astype(jnp.int32)

        called = genotypes >= 0
        dosage = jnp.where(called, genotypes, 0.0)
        stats = jnp.stack(
            [jnp.sum(dosage, axis=1), jnp.sum(called.astype(jnp.float32), axis=1)]
        )
        stats = rows_sum(stats)
        frequency = stats[0] / (2.0 * stats[1])
        scale_part = jnp.sum(2.0 * frequency * (1.0 - frequency))
        gt = lax.optimization_barrier(genotypes.T)
        centered = jnp.where(gt >= 0, gt - 2.0 * frequency[None, :], 0.0).astype(
            jnp.bfloat16
        )

        rel_own = from_first_snp(relationship[:, :PANEL], col)
        ids = rank * own + lax.broadcasted_iota(jnp.int32, rel_own.shape, 0)
        rel_own = rel_own + jnp.where(
            ids == lax.broadcasted_iota(jnp.int32, rel_own.shape, 1), RIDGE, 0.0
        )

        core, other = rows_xor(centered, 1), rows_xor(centered, 2)
        line = line_gather(centered, lambda x, near: after(x, rel_own, *near))
        line[-1] = after(line[-1], other)
        plane = [centered, core, other, rows_xor(other, 1)]
        first = select_order(line, z)[0]
        ordered = select_order(line, z ^ (col * part))
        groups = [ordered[bits * part : (bits + 1) * part] for bits in range(n_snp)]
        rel_line = line_gather(after(rel_own, line[-1]), lambda x, near: x)

        leaving = [gram_products(plane, groups[b], None, []) for b in range(1, n_snp)]
        gram_got = [snp_xor(leaving[b - 1], b) for b in range(1, n_snp)]

        head = [first, rows_xor(first, 1)]
        head.append(after(rows_xor(first, 2), *rel_line[1 : far + 1]))
        head.append(rows_xor(head[2], 1))
        (rows,) = head_products(place, [[first]], head, gram_got)
        rows = jnp.concatenate(
            [rows, jnp.broadcast_to(scale_part.reshape(1, 1), (SUB, PANEL))], axis=0
        )
        total = snp_sum(rows)
        inverse = 1.0 / total[own, 0]
        total = total[:own] * inverse + select_order(rel_line, z)[0]
        sides = head_products(place, groups, head, [rows])
        diagonal = group_gather(after(total, *sides[1:]))

        pieces = gram_products(plane, groups[0], gram_got, [rows])
        moved = [pieces[0]] + [rows_xor(pieces[k], k) for k in range(1, GROUP)]

        inv, column, square = factor_step(place, diagonal, PANEL, [])
        inverses, below = [inv], [column]
        side = sides[0]
        for bits in range(1, n_snp):
            side = side + after(snp_xor(sides[bits], bits), inverses[0])
        rel_side = select_order(rel_line, z ^ (col * part))[:part]
        side = jnp.concatenate(
            [
                rel_side[j] + side[j * own : (j + 1) * own] * inverse
                for j in range(part)
            ],
            axis=0,
        )
        sides = group_gather(side)

        waits = [[], [side] + moved[1:], [], [sides[2]]]
        for k in range(1, PANEL // BLOCK):
            inv, *more = factor_step(place, [square], PANEL - k * BLOCK, waits[k])
            inverses.append(inv)
            if more:
                column, square = more
                below.append(column)

        (lead,) = head_products(place, [[centered]], head, [inverses[0]])
        own_columns = rel_own + snp_sum(lead) * inverse
        panel, weights = solve(own_columns, inverses, below)
        updated = final_update(
            place, inverse.reshape(1), relationship, weights, moved, sides
        )
        return updated, panel

    return per_device


def solution(mesh):
    return jax.shard_map(
        make(mesh.shape["rows"], mesh.shape["snp"]),
        mesh=mesh,
        in_specs=(P("snp", "rows"), P("rows", "snp")),
        out_specs=(P("rows", "snp"), P("rows", None)),
        check_vma=False,
    )
```

```python
import functools

import jax
import jax.numpy as jnp
from jax import lax
from jax.experimental import pallas as pl
from jax.experimental.pallas import tpu as pltpu
from jax.sharding import PartitionSpec as P

PANEL = 512
RIDGE = 0.25
GROUP = 4
BLOCK = 128
SUB = 8

VMEM = pl.BlockSpec(memory_space=pltpu.VMEM)
SMEM = pl.BlockSpec(memory_space=pltpu.SMEM)
ANYWHERE = pl.BlockSpec(memory_space=pl.ANY)


def precise(a, b, contract):
    return lax.dot_general(
        a,
        b,
        (((1,), (contract,)), ((), ())),
        precision=lax.Precision.HIGHEST,
        preferred_element_type=jnp.float32,
    )


def times(a, b):
    return lax.dot_general(
        a, b, (((1,), (1,)), ((), ())), preferred_element_type=jnp.float32
    )


def split(x):
    high = x.astype(jnp.bfloat16)
    return high, (x - high.astype(jnp.float32)).astype(jnp.bfloat16)


def cost(flops):
    return pl.CostEstimate(flops=flops, bytes_accessed=131072, transcendentals=0)


def room(*arrays):
    total = sum(x.size * x.dtype.itemsize for x in arrays)
    return pltpu.CompilerParams(vmem_limit_bytes=total * 3 // 2 + 3 * 2**20)


def f32(*shape):
    return jax.ShapeDtypeStruct(shape, jnp.float32)


def invert_factor(work):
    lane = lax.broadcasted_iota(jnp.int32, (SUB, BLOCK), 1)
    for g in range(BLOCK // SUB):
        at = g * SUB
        own = work[at : at + SUB, :]
        inside = (lane >= at) & (lane < at + SUB)
        rows = [jnp.broadcast_to(own[u : u + 1, :], (SUB, BLOCK)) for u in range(SUB)]
        e = [
            [
                jnp.broadcast_to(rows[t][:, at + u : at + u + 1], (SUB, BLOCK))
                for t in range(u + 1)
            ]
            for u in range(SUB)
        ]
        rows = [
            jnp.where(inside, jnp.where(lane == at + u, 1.0, 0.0), rows[u])
            for u in range(SUB)
        ]
        low = [[None] * SUB for _ in range(SUB)]
        scale = []
        for t in range(SUB):
            r = lax.rsqrt(e[t][t])
            scale.append(r)
            for u in range(t + 1, SUB):
                low[u][t] = e[u][t] * r
            for u in range(t + 1, SUB):
                for v in range(t + 1, u + 1):
                    e[u][v] = e[u][v] - low[u][t] * low[v][t]
            rows[t] = rows[t] * r
            for u in range(t + 1, SUB):
                rows[u] = rows[u] - low[u][t] * rows[t]
        for below in range(g + 1, BLOCK // SUB):
            base = below * SUB
            rest = work[base : base + SUB, :]
            c = [
                jnp.broadcast_to(rest[:, at + t : at + t + 1], (SUB, BLOCK))
                for t in range(SUB)
            ]
            rest = jnp.where(inside, 0.0, rest)
            for t in range(SUB):
                c[t] = c[t] * scale[t]
                for s in range(t + 1, SUB):
                    c[s] = c[s] - low[s][t] * c[t]
                rest = rest - c[t] * rows[t]
            work[base : base + SUB, :] = rest
        for t in range(SUB):
            work[at + t : at + t + 1, :] = rows[t][0:1, :]


def factor_step_kernel(size, n_in, *refs):
    place, squares = refs[0], refs[1 : 1 + n_in]
    if size > BLOCK:
        inverse, column, rest, work = refs[-4:]
    else:
        inverse, work = refs[-2:]
    if n_in == 1:
        square = squares[0]
    else:
        square = rest_in = refs[-5]
        own = squares[0].shape[0]

        def assemble(mine):
            for k in range(GROUP):
                start = (mine ^ k) * own
                if start < size:
                    stop = min(start + own, size)
                    rest_in[start:stop, :] = squares[k][: stop - start, :]

        for mine in range(GROUP):
            pl.when(place[0] == mine)(functools.partial(assemble, mine))
    work[...] = square[:BLOCK, :BLOCK]
    invert_factor(work)
    i = lax.broadcasted_iota(jnp.int32, (BLOCK, BLOCK), 0)
    j = lax.broadcasted_iota(jnp.int32, (BLOCK, BLOCK), 1)
    value = jnp.where(j <= i, work[...], 0.0)
    inverse[...] = value
    if size > BLOCK:
        below = precise(square[BLOCK:, :BLOCK], value, 1)
        column[...] = below
        for n in range(size // BLOCK - 1):
            cut = slice(n * BLOCK, size - BLOCK)
            across = slice(n * BLOCK, (n + 1) * BLOCK)
            rest[cut, across] = square[
                (n + 1) * BLOCK :, (n + 1) * BLOCK : (n + 2) * BLOCK
            ] - precise(below[n * BLOCK :, :], below[across, :], 1)


def factor_step(place, squares, size, waits):
    left = size - BLOCK
    out_shape = [f32(BLOCK, BLOCK)]
    scratch = [pltpu.VMEM((BLOCK, BLOCK), jnp.float32)]
    if left:
        out_shape += [f32(left, BLOCK), f32(left, left)]
    n_in = len(squares)
    kernel = functools.partial(factor_step_kernel, size, n_in)
    if n_in > 1:

        def kernel(*refs):
            *others, work, whole = refs
            outs = 3 if left else 1
            return factor_step_kernel(
                size, n_in, *others[:-outs], whole, *others[-outs:], work
            )

        scratch.append(pltpu.VMEM((size, size), jnp.float32))
    return pl.pallas_call(
        kernel,
        out_shape=out_shape,
        in_specs=[SMEM] + [VMEM] * n_in + [ANYWHERE] * len(waits),
        out_specs=[VMEM] * len(out_shape),
        scratch_shapes=scratch,
        compiler_params=room(*out_shape, f32(size, size), *squares),
        cost_estimate=cost(6_000_000_000),
    )(place, *squares, *waits)


def solve_kernel(blocks, columns, *refs):
    inverses, below = refs[:blocks], refs[blocks : 2 * blocks - 1]
    panel, weights = refs[-2:]
    found = []
    for k in range(blocks):
        total = columns[:, k * BLOCK : (k + 1) * BLOCK]
        for j in range(k):
            start = (k - j - 1) * BLOCK
            total = total - precise(found[j], below[j][start : start + BLOCK, :], 1)
        found.append(precise(total, inverses[k][...], 1))
        panel[:, k * BLOCK : (k + 1) * BLOCK] = found[k]
    for k in reversed(range(blocks)):
        total = found[k]
        for j in range(k + 1, blocks):
            start = (j - k - 1) * BLOCK
            total = total - precise(found[j], below[k][start : start + BLOCK, :], 0)
        found[k] = precise(total, inverses[k][...], 0)
        weights[:, k * BLOCK : (k + 1) * BLOCK] = found[k]


def solve(columns, inverses, below):
    own = columns.shape[0]
    return pl.pallas_call(
        functools.partial(solve_kernel, len(inverses)),
        out_shape=[f32(own, PANEL), f32(own, PANEL)],
        in_specs=[VMEM] * (2 * len(inverses)),
        out_specs=[VMEM, VMEM],
        compiler_params=room(columns, columns, columns, *inverses, *below),
        cost_estimate=cost(4 * own * PANEL * PANEL),
    )(columns, *inverses, *below)


def head_kernel(n_left, sizes, place, *refs):
    left, head = refs[:n_left], refs[n_left : n_left + GROUP]
    outs = refs[-len(sizes) :]
    own = head[0].shape[0]

    def for_member(mine):
        for k in range(GROUP):
            start = (mine ^ k) * own
            width = min(own, PANEL - start)
            if width > 0:
                at = 0
                for out, count in zip(outs, sizes):
                    for n in range(count):
                        product = times(left[at][...], head[k][...])
                        out[n * own : (n + 1) * own, start : start + width] = product[
                            :, :width
                        ]
                        at += 1

    for mine in range(GROUP):
        pl.when(place[0] == mine)(functools.partial(for_member, mine))


def head_products(place, groups, head, waits):
    own = head[0].shape[0]
    left = [x for group in groups for x in group]
    sizes = [len(group) for group in groups]
    return pl.pallas_call(
        functools.partial(head_kernel, len(left), sizes),
        out_shape=[f32(n * own, PANEL) for n in sizes],
        in_specs=[SMEM] + [VMEM] * (len(left) + GROUP) + [ANYWHERE] * len(waits),
        out_specs=[VMEM] * len(sizes),
        compiler_params=room(*left, *head, f32(len(left) * own, PANEL)),
        cost_estimate=cost(2 * len(left) * own * PANEL * head[0].shape[1]),
    )(place, *left, *head, *waits)


def gram_kernel(n_cols, n_more, *refs):
    plane, cols = refs[:GROUP], refs[GROUP : GROUP + n_cols]
    more = refs[GROUP + n_cols : GROUP + n_cols + n_more]
    outs = refs[-GROUP:]
    own = plane[0].shape[0]
    for k in range(GROUP):
        for j in range(n_cols):
            product = times(cols[j][...], plane[k][...])
            across = slice(j * own, (j + 1) * own)
            for x in more:
                product = product + x[across, k * own : (k + 1) * own]
            outs[k][:, across] = product.T


def gram_out_kernel(n_cols, *refs):
    plane, cols, out = refs[:GROUP], refs[GROUP : GROUP + n_cols], refs[-1]
    own = plane[0].shape[0]
    for k in range(GROUP):
        for j in range(n_cols):
            out[j * own : (j + 1) * own, k * own : (k + 1) * own] = times(
                cols[j][...], plane[k][...]
            )


def gram_products(plane, cols, more, waits):
    own, depth = plane[0].shape
    width = len(cols) * own
    if more is None:
        kernel = functools.partial(gram_out_kernel, len(cols))
        out_shape, out_specs, more = f32(width, GROUP * own), VMEM, []
    else:
        kernel = functools.partial(gram_kernel, len(cols), len(more))
        out_shape, out_specs = [f32(own, width)] * GROUP, [VMEM] * GROUP
    return pl.pallas_call(
        kernel,
        out_shape=out_shape,
        in_specs=[VMEM] * (GROUP + len(cols) + len(more))
        + [ANYWHERE] * len(waits),
        out_specs=out_specs,
        compiler_params=room(*plane, *cols, *more, f32(GROUP * own, width)),
        cost_estimate=cost(2 * GROUP * own * width * depth),
    )(*plane, *cols, *more, *waits)


def update_kernel(own, part, place, scale, rel, weights, *refs):
    pieces, sides, out = refs[:GROUP], refs[GROUP : 2 * GROUP], refs[2 * GROUP]
    i = lax.broadcasted_iota(jnp.int32, (own, own), 0)
    j = lax.broadcasted_iota(jnp.int32, (own, own), 1)
    ridge = jnp.where(i == j, RIDGE, 0.0)

    high, low = split(weights[...])

    def for_member(mine):
        for k in range(GROUP):
            side_high, side_low = split(sides[k][...])
            product = times(high, side_low) + times(low, side_high)
            product = product + times(high, side_high)
            for n in range(part):
                at = (n * GROUP + (mine ^ k)) * own
                cut = slice(n * own, (n + 1) * own)
                value = rel[:, at : at + own] + pieces[k][:, cut] * scale[0]
                value = value - product[:, cut]
                if k == 0:
                    value = value + ridge * jnp.where(place[1] == n, 1.0, 0.0)
                out[:, at : at + own] = value

    for mine in range(GROUP):
        pl.when(place[0] == mine)(functools.partial(for_member, mine))


def final_update(place, scale, rel, weights, pieces, sides):
    own, width = rel.shape
    part = width // (GROUP * own)
    return pl.pallas_call(
        functools.partial(update_kernel, own, part),
        out_shape=f32(own, width),
        in_specs=[SMEM, SMEM] + [VMEM] * (2 + 2 * GROUP),
        out_specs=VMEM,
        compiler_params=room(rel, rel, weights, *pieces, *sides, *sides),
        cost_estimate=cost(2 * own * width * PANEL),
    )(place, scale, rel, weights, *pieces, *sides)


def nothing(*refs):
    pass


def after(x, *done):
    return pl.pallas_call(
        nothing,
        out_shape=jax.ShapeDtypeStruct(x.shape, x.dtype),
        in_specs=[ANYWHERE] * (1 + len(done)),
        out_specs=ANYWHERE,
        input_output_aliases={0: 0},
        compiler_params=pltpu.CompilerParams(vmem_limit_bytes=2**20),
    )(x, *done)


def select_order(blocks, member):
    bit = 1
    while bit < len(blocks):
        swap = (member & bit) != 0
        blocks = [
            jnp.where(swap, blocks[k ^ bit], blocks[k]) for k in range(len(blocks))
        ]
        bit *= 2
    return blocks


def make(n_rows, n_snp):
    lines = n_rows // GROUP
    part = lines // n_snp
    far = lines // 2

    def rows_xor(x, bits):
        return lax.ppermute(x, "rows", [(r, r ^ bits) for r in range(n_rows)])

    def snp_xor(x, bits):
        return lax.ppermute(x, "snp", [(s, s ^ bits) for s in range(n_snp)])

    def from_first_snp(x, rank):
        got = x
        for s in range(1, n_snp):
            got = jnp.where(rank == s, lax.ppermute(x, "snp", [(0, s)]), got)
        return got

    def group_gather(x):
        core = rows_xor(x, 1)
        other = rows_xor(x, 2)
        return [x, core, other, rows_xor(other, 1)]

    def line_gather(x, hold):
        near = {k: rows_xor(x, k * GROUP) for k in range(1, far)}
        passed = hold(rows_xor(x, far * GROUP), list(near.values()))
        parts = {0: x, far: passed, **near}
        for k in range(1, far):
            parts[far + k] = rows_xor(passed, k * GROUP)
        return [parts[k] for k in range(lines)]

    def rows_sum(x):
        bit = 1
        while bit < n_rows:
            if bit * 2 < n_rows:
                parts = [x] + [rows_xor(x, bit * k) for k in (1, 2, 3)]
                x = (parts[0] + parts[1]) + (parts[2] + parts[3])
                bit *= 4
            else:
                x = x + rows_xor(x, bit)
                bit *= 2
        return x

    def snp_sum(x):
        bit = 1
        while bit < n_snp:
            x = x + snp_xor(x, bit)
            bit *= 2
        return x

    def per_device(genotypes, relationship):
        own = genotypes.shape[1]
        rank = lax.axis_index("rows")
        col = lax.axis_index("snp")
        q = rank % GROUP
        z = rank // GROUP
        place = jnp.stack([q, z - col * part]).astype(jnp.int32)

        called = genotypes >= 0
        dosage = jnp.where(called, genotypes, 0.0)
        stats = jnp.stack(
            [jnp.sum(dosage, axis=1), jnp.sum(called.astype(jnp.float32), axis=1)]
        )
        stats = rows_sum(stats)
        frequency = stats[0] / (2.0 * stats[1])
        scale_part = jnp.sum(2.0 * frequency * (1.0 - frequency))
        gt = lax.optimization_barrier(genotypes.T)
        centered = jnp.where(gt >= 0, gt - 2.0 * frequency[None, :], 0.0).astype(
            jnp.bfloat16
        )

        rel_own = from_first_snp(relationship[:, :PANEL], col)
        ids = rank * own + lax.broadcasted_iota(jnp.int32, rel_own.shape, 0)
        rel_own = rel_own + jnp.where(
            ids == lax.broadcasted_iota(jnp.int32, rel_own.shape, 1), RIDGE, 0.0
        )

        core, other = rows_xor(centered, 1), rows_xor(centered, 2)
        line = line_gather(centered, lambda x, near: after(x, rel_own, *near))
        line[-1] = after(line[-1], other)
        plane = [centered, core, other, rows_xor(other, 1)]
        first = select_order(line, z)[0]
        member = after((z ^ (col * part)).astype(jnp.int32).reshape(1), first)[0]
        ordered = select_order(line, member)
        groups = [ordered[bits * part : (bits + 1) * part] for bits in range(n_snp)]
        rel_line = line_gather(after(rel_own, line[-1]), lambda x, near: x)

        leaving = [gram_products(plane, groups[b], None, []) for b in range(1, n_snp)]
        gram_got = [snp_xor(leaving[b - 1], b) for b in range(1, n_snp)]

        head = [first, rows_xor(first, 1)]
        head.append(after(rows_xor(first, 2), *rel_line[1 : far + 1]))
        head.append(rows_xor(head[2], 1))
        (rows,) = head_products(place, [[first]], head, [])
        rows = jnp.concatenate(
            [rows, jnp.broadcast_to(scale_part.reshape(1, 1), (SUB, PANEL))], axis=0
        )
        total = snp_sum(rows)
        inverse = 1.0 / total[own, 0]
        total = total[:own] * inverse + select_order(rel_line, z)[0]
        sides = head_products(place, groups, head, [rows] + gram_got)
        pieces = gram_products(plane, groups[0], gram_got, [rows])
        diagonal = group_gather(after(total, *sides[1:], pieces[1]))

        moved = [pieces[0]] + [rows_xor(pieces[k], k) for k in range(1, GROUP)]

        inv, column, square = factor_step(place, diagonal, PANEL, [])
        inverses, below = [inv], [column]
        side = sides[0]
        for bits in range(1, n_snp):
            side = side + after(snp_xor(sides[bits], bits), inverses[0])
        rel_side = select_order(rel_line, z ^ (col * part))[:part]
        side = jnp.concatenate(
            [
                rel_side[j] + side[j * own : (j + 1) * own] * inverse
                for j in range(part)
            ],
            axis=0,
        )
        sides = group_gather(side)

        waits = [[], [side] + moved[1:], [], [sides[2]]]
        for k in range(1, PANEL // BLOCK):
            inv, *more = factor_step(place, [square], PANEL - k * BLOCK, waits[k])
            inverses.append(inv)
            if more:
                column, square = more
                below.append(column)

        (lead,) = head_products(place, [[centered]], head, [inverses[0]])
        own_columns = rel_own + snp_sum(lead) * inverse
        panel, weights = solve(own_columns, inverses, below)
        updated = final_update(
            place, inverse.reshape(1), relationship, weights, moved, sides
        )
        return updated, panel

    return per_device


def solution(mesh):
    return jax.shard_map(
        make(mesh.shape["rows"], mesh.shape["snp"]),
        mesh=mesh,
        in_specs=(P("snp", "rows"), P("rows", "snp")),
        out_specs=(P("rows", "snp"), P("rows", None)),
        check_vma=False,
    )
```

```python
import functools

import jax
import jax.numpy as jnp
from jax import lax
from jax.experimental import pallas as pl
from jax.experimental.pallas import tpu as pltpu
from jax.sharding import PartitionSpec as P

PANEL = 512
RIDGE = 0.25
GROUP = 4
BLOCK = 128
SUB = 8

VMEM = pl.BlockSpec(memory_space=pltpu.VMEM)
SMEM = pl.BlockSpec(memory_space=pltpu.SMEM)
ANYWHERE = pl.BlockSpec(memory_space=pl.ANY)


def precise(a, b, contract):
    return lax.dot_general(
        a,
        b,
        (((1,), (contract,)), ((), ())),
        precision=lax.Precision.HIGHEST,
        preferred_element_type=jnp.float32,
    )


def times(a, b):
    return lax.dot_general(
        a, b, (((1,), (1,)), ((), ())), preferred_element_type=jnp.float32
    )


def split(x):
    high = x.astype(jnp.bfloat16)
    return high, (x - high.astype(jnp.float32)).astype(jnp.bfloat16)


def cost(flops):
    return pl.CostEstimate(flops=flops, bytes_accessed=131072, transcendentals=0)


def room(*arrays):
    total = sum(x.size * x.dtype.itemsize for x in arrays)
    return pltpu.CompilerParams(vmem_limit_bytes=total * 3 // 2 + 3 * 2**20)


def f32(*shape):
    return jax.ShapeDtypeStruct(shape, jnp.float32)


def invert_factor(work):
    lane = lax.broadcasted_iota(jnp.int32, (SUB, BLOCK), 1)
    for g in range(BLOCK // SUB):
        at = g * SUB
        own = work[at : at + SUB, :]
        inside = (lane >= at) & (lane < at + SUB)
        rows = [jnp.broadcast_to(own[u : u + 1, :], (SUB, BLOCK)) for u in range(SUB)]
        e = [
            [
                jnp.broadcast_to(rows[t][:, at + u : at + u + 1], (SUB, BLOCK))
                for t in range(u + 1)
            ]
            for u in range(SUB)
        ]
        rows = [
            jnp.where(inside, jnp.where(lane == at + u, 1.0, 0.0), rows[u])
            for u in range(SUB)
        ]
        low = [[None] * SUB for _ in range(SUB)]
        scale = []
        for t in range(SUB):
            r = lax.rsqrt(e[t][t])
            scale.append(r)
            for u in range(t + 1, SUB):
                low[u][t] = e[u][t] * r
            for u in range(t + 1, SUB):
                for v in range(t + 1, u + 1):
                    e[u][v] = e[u][v] - low[u][t] * low[v][t]
            rows[t] = rows[t] * r
            for u in range(t + 1, SUB):
                rows[u] = rows[u] - low[u][t] * rows[t]
        for below in range(g + 1, BLOCK // SUB):
            base = below * SUB
            rest = work[base : base + SUB, :]
            c = [
                jnp.broadcast_to(rest[:, at + t : at + t + 1], (SUB, BLOCK))
                for t in range(SUB)
            ]
            rest = jnp.where(inside, 0.0, rest)
            for t in range(SUB):
                c[t] = c[t] * scale[t]
                for s in range(t + 1, SUB):
                    c[s] = c[s] - low[s][t] * c[t]
                rest = rest - c[t] * rows[t]
            work[base : base + SUB, :] = rest
        for t in range(SUB):
            work[at + t : at + t + 1, :] = rows[t][0:1, :]


def factor_step_kernel(size, n_in, *refs):
    place, squares = refs[0], refs[1 : 1 + n_in]
    if size > BLOCK:
        inverse, column, rest, work = refs[-4:]
    else:
        inverse, work = refs[-2:]
    if n_in == 1:
        square = squares[0]
    else:
        square = rest_in = refs[-5]
        own = squares[0].shape[0]

        def assemble(mine):
            for k in range(GROUP):
                start = (mine ^ k) * own
                if start < size:
                    stop = min(start + own, size)
                    rest_in[start:stop, :] = squares[k][: stop - start, :]

        for mine in range(GROUP):
            pl.when(place[0] == mine)(functools.partial(assemble, mine))
    work[...] = square[:BLOCK, :BLOCK]
    invert_factor(work)
    i = lax.broadcasted_iota(jnp.int32, (BLOCK, BLOCK), 0)
    j = lax.broadcasted_iota(jnp.int32, (BLOCK, BLOCK), 1)
    value = jnp.where(j <= i, work[...], 0.0)
    inverse[...] = value
    if size > BLOCK:
        below = precise(square[BLOCK:, :BLOCK], value, 1)
        column[...] = below
        for n in range(size // BLOCK - 1):
            cut = slice(n * BLOCK, size - BLOCK)
            across = slice(n * BLOCK, (n + 1) * BLOCK)
            rest[cut, across] = square[
                (n + 1) * BLOCK :, (n + 1) * BLOCK : (n + 2) * BLOCK
            ] - precise(below[n * BLOCK :, :], below[across, :], 1)


def factor_step(place, squares, size, waits):
    left = size - BLOCK
    out_shape = [f32(BLOCK, BLOCK)]
    scratch = [pltpu.VMEM((BLOCK, BLOCK), jnp.float32)]
    if left:
        out_shape += [f32(left, BLOCK), f32(left, left)]
    n_in = len(squares)
    kernel = functools.partial(factor_step_kernel, size, n_in)
    if n_in > 1:

        def kernel(*refs):
            *others, work, whole = refs
            outs = 3 if left else 1
            return factor_step_kernel(
                size, n_in, *others[:-outs], whole, *others[-outs:], work
            )

        scratch.append(pltpu.VMEM((size, size), jnp.float32))
    return pl.pallas_call(
        kernel,
        out_shape=out_shape,
        in_specs=[SMEM] + [VMEM] * n_in + [ANYWHERE] * len(waits),
        out_specs=[VMEM] * len(out_shape),
        scratch_shapes=scratch,
        compiler_params=room(*out_shape, f32(size, size), *squares),
        cost_estimate=cost(3_500_000_000),
    )(place, *squares, *waits)


def solve_kernel(blocks, n_lead, rel, scale, *refs):
    lead, refs = refs[:n_lead], refs[n_lead:]
    inverses, below = refs[:blocks], refs[blocks : 2 * blocks - 1]
    panel, weights = refs[-2:]
    found = []
    for k in range(blocks):
        across = slice(k * BLOCK, (k + 1) * BLOCK)
        total = lead[0][:, across]
        for x in lead[1:]:
            total = total + x[:, across]
        total = rel[:, across] + total * scale[0:1, :]
        for j in range(k):
            start = (k - j - 1) * BLOCK
            total = total - precise(found[j], below[j][start : start + BLOCK, :], 1)
        found.append(precise(total, inverses[k][...], 1))
        panel[:, k * BLOCK : (k + 1) * BLOCK] = found[k]
    for k in reversed(range(blocks)):
        total = found[k]
        for j in range(k + 1, blocks):
            start = (j - k - 1) * BLOCK
            total = total - precise(found[j], below[k][start : start + BLOCK, :], 0)
        found[k] = precise(total, inverses[k][...], 0)
        weights[:, k * BLOCK : (k + 1) * BLOCK] = found[k]


def solve(rel, scale, lead, inverses, below):
    own = rel.shape[0]
    return pl.pallas_call(
        functools.partial(solve_kernel, len(inverses), len(lead)),
        out_shape=[f32(own, PANEL), f32(own, PANEL)],
        in_specs=[VMEM] * (1 + len(lead) + 2 * len(inverses)),
        out_specs=[VMEM, VMEM],
        compiler_params=room(rel, rel, rel, *lead, *inverses, *below),
        cost_estimate=cost(4 * own * PANEL * PANEL),
    )(rel, scale, *lead, *inverses, *below)


def head_kernel(n_left, sizes, place, *refs):
    left, head = refs[:n_left], refs[n_left : n_left + GROUP]
    outs = refs[-len(sizes) :]
    own = head[0].shape[0]

    def for_member(mine):
        for k in range(GROUP):
            start = (mine ^ k) * own
            width = min(own, PANEL - start)
            if width > 0:
                at = 0
                for out, count in zip(outs, sizes):
                    for n in range(count):
                        product = times(left[at][...], head[k][...])
                        out[n * own : (n + 1) * own, start : start + width] = product[
                            :, :width
                        ]
                        at += 1

    for mine in range(GROUP):
        pl.when(place[0] == mine)(functools.partial(for_member, mine))


def head_products(place, groups, head, waits):
    own = head[0].shape[0]
    left = [x for group in groups for x in group]
    sizes = [len(group) for group in groups]
    return pl.pallas_call(
        functools.partial(head_kernel, len(left), sizes),
        out_shape=[f32(n * own, PANEL) for n in sizes],
        in_specs=[SMEM] + [VMEM] * (len(left) + GROUP) + [ANYWHERE] * len(waits),
        out_specs=[VMEM] * len(sizes),
        compiler_params=room(*left, *head, f32(len(left) * own, PANEL)),
        cost_estimate=cost(2 * len(left) * own * PANEL * head[0].shape[1]),
    )(place, *left, *head, *waits)


def message_kernel(place, scale, *refs):
    first, cols, head, out = refs[0], refs[1 : -1 - GROUP], refs[-1 - GROUP : -1], refs[-1]
    own = first.shape[0]
    out[own : own + SUB, :] = jnp.full((SUB, PANEL), scale[0], jnp.float32)

    def for_member(mine):
        for k in range(GROUP):
            start = (mine ^ k) * own
            width = min(own, PANEL - start)
            if width > 0:
                for n, block in enumerate((first,) + tuple(cols)):
                    base = n * own + (SUB if n else 0)
                    product = times(block[...], head[k][...])
                    out[base : base + own, start : start + width] = product[:, :width]

    for mine in range(GROUP):
        pl.when(place[0] == mine)(functools.partial(for_member, mine))


def message(place, scale, first, cols, head):
    own = first.shape[0]
    rows = (1 + len(cols)) * own + SUB
    return pl.pallas_call(
        message_kernel,
        out_shape=f32(rows, PANEL),
        in_specs=[SMEM, SMEM] + [VMEM] * (1 + len(cols) + GROUP),
        out_specs=VMEM,
        compiler_params=room(first, *cols, *head, f32(rows, PANEL)),
        cost_estimate=cost(2 * rows * PANEL * first.shape[1]),
    )(place, scale, first, *cols, *head)


def sums_kernel(n_got, part, mine, *refs):
    got, keep, rel_first = refs[:n_got], refs[n_got], refs[n_got + 1]
    rel_side = refs[n_got + 2 : n_got + 2 + part]
    total, side, inverse = refs[-3:]
    own = total.shape[0]
    scale = mine[own : own + 1, :]
    rows = mine[:own, :]
    for x in got:
        scale = scale + x[own : own + 1, :]
        rows = rows + x[:own, :]
    scale = 1.0 / scale
    total[...] = rel_first[...] + rows * scale
    for n in range(part):
        cut = slice(n * own, (n + 1) * own)
        rows = keep[cut, :]
        for x in got:
            rows = rows + x[(n + 1) * own + SUB : (n + 2) * own + SUB, :]
        side[cut, :] = rel_side[n][...] + rows * scale
    inverse[...] = jnp.broadcast_to(scale[:, :BLOCK], (SUB, BLOCK))


def sums(mine, got, keep, rel_first, rel_side):
    own = rel_first.shape[0]
    part = len(rel_side)
    return pl.pallas_call(
        functools.partial(sums_kernel, len(got), part),
        out_shape=[f32(own, PANEL), f32(part * own, PANEL), f32(SUB, BLOCK)],
        in_specs=[VMEM] * (3 + len(got) + part),
        out_specs=[VMEM] * 3,
        compiler_params=room(mine, *got, keep, keep, rel_first, rel_first, *rel_side),
        cost_estimate=cost(10_000_000),
    )(mine, *got, keep, rel_first, *rel_side)


def gram_kernel(n_cols, n_more, *refs):
    plane, cols = refs[:GROUP], refs[GROUP : GROUP + n_cols]
    more = refs[GROUP + n_cols : GROUP + n_cols + n_more]
    outs = refs[-GROUP:]
    own = plane[0].shape[0]
    for k in range(GROUP):
        for j in range(n_cols):
            product = times(cols[j][...], plane[k][...])
            across = slice(j * own, (j + 1) * own)
            for x in more:
                product = product + x[across, k * own : (k + 1) * own]
            outs[k][:, across] = product.T


def gram_out_kernel(n_cols, *refs):
    plane, cols, out = refs[:GROUP], refs[GROUP : GROUP + n_cols], refs[-1]
    own = plane[0].shape[0]
    for k in range(GROUP):
        for j in range(n_cols):
            out[j * own : (j + 1) * own, k * own : (k + 1) * own] = times(
                cols[j][...], plane[k][...]
            )


def gram_products(plane, cols, more, waits):
    own, depth = plane[0].shape
    width = len(cols) * own
    if more is None:
        kernel = functools.partial(gram_out_kernel, len(cols))
        out_shape, out_specs, more = f32(width, GROUP * own), VMEM, []
    else:
        kernel = functools.partial(gram_kernel, len(cols), len(more))
        out_shape, out_specs = [f32(own, width)] * GROUP, [VMEM] * GROUP
    return pl.pallas_call(
        kernel,
        out_shape=out_shape,
        in_specs=[VMEM] * (GROUP + len(cols) + len(more))
        + [ANYWHERE] * len(waits),
        out_specs=out_specs,
        compiler_params=room(*plane, *cols, *more, f32(GROUP * own, width)),
        cost_estimate=cost(2 * GROUP * own * width * depth),
    )(*plane, *cols, *more, *waits)


def update_kernel(own, part, place, scale, rel, weights, *refs):
    pieces, sides, out = refs[:GROUP], refs[GROUP : 2 * GROUP], refs[2 * GROUP]
    i = lax.broadcasted_iota(jnp.int32, (own, own), 0)
    j = lax.broadcasted_iota(jnp.int32, (own, own), 1)
    ridge = jnp.where(i == j, RIDGE, 0.0)

    high, low = split(weights[...])

    def for_member(mine):
        for k in range(GROUP):
            side_high, side_low = split(sides[k][...])
            product = times(high, side_low) + times(low, side_high)
            product = product + times(high, side_high)
            for n in range(part):
                at = (n * GROUP + (mine ^ k)) * own
                cut = slice(n * own, (n + 1) * own)
                value = rel[:, at : at + own] + pieces[k][:, cut] * scale[0:1, 0:1]
                value = value - product[:, cut]
                if k == 0:
                    value = value + ridge * jnp.where(place[1] == n, 1.0, 0.0)
                out[:, at : at + own] = value

    for mine in range(GROUP):
        pl.when(place[0] == mine)(functools.partial(for_member, mine))


def final_update(place, scale, rel, weights, pieces, sides):
    own, width = rel.shape
    part = width // (GROUP * own)
    return pl.pallas_call(
        functools.partial(update_kernel, own, part),
        out_shape=f32(own, width),
        in_specs=[SMEM] + [VMEM] * (3 + 2 * GROUP),
        out_specs=VMEM,
        compiler_params=room(rel, rel, weights, *pieces, *sides, *sides),
        cost_estimate=cost(2 * own * width * PANEL),
    )(place, scale, rel, weights, *pieces, *sides)


def nothing(*refs):
    pass


def after(x, *done):
    return pl.pallas_call(
        nothing,
        out_shape=jax.ShapeDtypeStruct(x.shape, x.dtype),
        in_specs=[ANYWHERE] * (1 + len(done)),
        out_specs=ANYWHERE,
        input_output_aliases={0: 0},
        compiler_params=pltpu.CompilerParams(vmem_limit_bytes=2**20),
    )(x, *done)


def select_order(blocks, member):
    bit = 1
    while bit < len(blocks):
        swap = (member & bit) != 0
        blocks = [
            jnp.where(swap, blocks[k ^ bit], blocks[k]) for k in range(len(blocks))
        ]
        bit *= 2
    return blocks


def make(n_rows, n_snp):
    lines = n_rows // GROUP
    part = lines // n_snp
    far = lines // 2

    def rows_xor(x, bits):
        return lax.ppermute(x, "rows", [(r, r ^ bits) for r in range(n_rows)])

    def snp_xor(x, bits):
        return lax.ppermute(x, "snp", [(s, s ^ bits) for s in range(n_snp)])

    def from_first_snp(x, rank):
        got = x
        for s in range(1, n_snp):
            got = jnp.where(rank == s, lax.ppermute(x, "snp", [(0, s)]), got)
        return got

    def group_gather(x):
        core = rows_xor(x, 1)
        other = rows_xor(x, 2)
        return [x, core, other, rows_xor(other, 1)]

    def line_gather(x, hold):
        near = {k: rows_xor(x, k * GROUP) for k in range(1, far)}
        passed = hold(rows_xor(x, far * GROUP), list(near.values()))
        parts = {0: x, far: passed, **near}
        for k in range(1, far):
            parts[far + k] = rows_xor(passed, k * GROUP)
        return [parts[k] for k in range(lines)]

    def rows_sum(x):
        bit = 1
        while bit < n_rows:
            if bit * 2 < n_rows:
                parts = [x] + [rows_xor(x, bit * k) for k in (1, 2, 3)]
                x = (parts[0] + parts[1]) + (parts[2] + parts[3])
                bit *= 4
            else:
                x = x + rows_xor(x, bit)
                bit *= 2
        return x

    def snp_sum(x):
        bit = 1
        while bit < n_snp:
            x = x + snp_xor(x, bit)
            bit *= 2
        return x

    def per_device(genotypes, relationship):
        own = genotypes.shape[1]
        rank = lax.axis_index("rows")
        col = lax.axis_index("snp")
        q = rank % GROUP
        z = rank // GROUP
        place = jnp.stack([q, z - col * part]).astype(jnp.int32)

        called = genotypes >= 0
        dosage = jnp.where(called, genotypes, 0.0)
        stats = jnp.stack(
            [jnp.sum(dosage, axis=1), jnp.sum(called.astype(jnp.float32), axis=1)]
        )
        stats = rows_sum(stats)
        frequency = stats[0] / (2.0 * stats[1])
        scale_part = jnp.sum(2.0 * frequency * (1.0 - frequency))
        gt = lax.optimization_barrier(genotypes.T)
        centered = jnp.where(gt >= 0, gt - 2.0 * frequency[None, :], 0.0).astype(
            jnp.bfloat16
        )

        rel_own = from_first_snp(relationship[:, :PANEL], col)
        ids = rank * own + lax.broadcasted_iota(jnp.int32, rel_own.shape, 0)
        rel_own = rel_own + jnp.where(
            ids == lax.broadcasted_iota(jnp.int32, rel_own.shape, 1), RIDGE, 0.0
        )

        core, other = rows_xor(centered, 1), rows_xor(centered, 2)
        line = line_gather(centered, lambda x, near: after(x, rel_own, *near))
        line[-1] = after(line[-1], other)
        plane = [centered, core, other, rows_xor(other, 1)]
        first = select_order(line, z)[0]
        member = after((z ^ (col * part)).astype(jnp.int32).reshape(1), first)
        ordered = select_order(line, member[0])
        groups = [ordered[bits * part : (bits + 1) * part] for bits in range(n_snp)]

        leaving = [gram_products(plane, groups[b], None, []) for b in range(1, n_snp)]

        head = [first, rows_xor(first, 1)]
        head.append(after(rows_xor(first, 2), *leaving))
        head.append(rows_xor(head[2], 1))
        messages = [
            message(place, scale_part.reshape(1), first, groups[b], head)
            for b in range(1, n_snp)
        ]
        got = [snp_xor(messages[b - 1], b) for b in range(1, n_snp)]
        keep, lead = head_products(place, [groups[0], [centered]], head, messages)
        rel_line = line_gather(after(rel_own, member), lambda x, near: after(x, keep))
        total, side, scale = sums(
            messages[0],
            got,
            keep,
            select_order(rel_line, z)[0],
            select_order(rel_line, z ^ (col * part))[:part],
        )

        diagonal = group_gather(total)
        side = after(side, diagonal[2])
        sides = [side, rows_xor(side, 1), rows_xor(side, 2)]

        gram_got = [
            snp_xor(after(leaving[b - 1], messages[0]), b) for b in range(1, n_snp)
        ]
        pieces = gram_products(plane, groups[0], gram_got, [])
        moved = [pieces[0]] + [rows_xor(pieces[k], k) for k in range(1, GROUP)]
        leads = [lead] + [snp_xor(after(lead, total), b) for b in range(1, n_snp)]

        squares, inverses, below = diagonal, [], []
        waits = [[], gram_got, [sides[2]], [pieces[1]]]
        for k in range(PANEL // BLOCK):
            inv, *more = factor_step(place, squares, PANEL - k * BLOCK, waits[k])
            inverses.append(inv)
            if more:
                below.append(more[0])
                squares = [more[1]]
        sides[2] = after(sides[2], inverses[2])
        sides.append(rows_xor(sides[2], 1))

        panel, weights = solve(rel_own, scale, leads, inverses, below)
        updated = final_update(place, scale, relationship, weights, moved, sides)
        return updated, panel

    return per_device


def solution(mesh):
    return jax.shard_map(
        make(mesh.shape["rows"], mesh.shape["snp"]),
        mesh=mesh,
        in_specs=(P("snp", "rows"), P("rows", "snp")),
        out_specs=(P("rows", "snp"), P("rows", None)),
        check_vma=False,
    )
```

```python
import functools

import jax
import jax.numpy as jnp
from jax import lax
from jax.experimental import pallas as pl
from jax.experimental.pallas import tpu as pltpu
from jax.sharding import PartitionSpec as P

PANEL = 512
RIDGE = 0.25
GROUP = 4
BLOCK = 128
SUB = 8

VMEM = pl.BlockSpec(memory_space=pltpu.VMEM)
SMEM = pl.BlockSpec(memory_space=pltpu.SMEM)
ANYWHERE = pl.BlockSpec(memory_space=pl.ANY)


def precise(a, b, contract):
    return lax.dot_general(
        a,
        b,
        (((1,), (contract,)), ((), ())),
        precision=lax.Precision.HIGHEST,
        preferred_element_type=jnp.float32,
    )


def times(a, b):
    return lax.dot_general(
        a, b, (((1,), (1,)), ((), ())), preferred_element_type=jnp.float32
    )


def split(x):
    high = x.astype(jnp.bfloat16)
    return high, (x - high.astype(jnp.float32)).astype(jnp.bfloat16)


def cost(flops):
    return pl.CostEstimate(flops=flops, bytes_accessed=131072, transcendentals=0)


def room(*arrays):
    total = sum(x.size * x.dtype.itemsize for x in arrays)
    return pltpu.CompilerParams(vmem_limit_bytes=total * 5 // 4 + 2**20)


def f32(*shape):
    return jax.ShapeDtypeStruct(shape, jnp.float32)


def invert_factor(work):
    lane = lax.broadcasted_iota(jnp.int32, (SUB, BLOCK), 1)
    row = lax.broadcasted_iota(jnp.int32, (SUB, BLOCK), 0)
    for g in range(BLOCK // SUB):
        at = g * SUB
        own = work[at : at + SUB, :]
        inside = (lane >= at) & (lane < at + SUB)
        rows = [jnp.broadcast_to(own[u : u + 1, :], (SUB, BLOCK)) for u in range(SUB)]
        e = [
            [
                jnp.broadcast_to(rows[t][:, at + u : at + u + 1], (SUB, BLOCK))
                for t in range(u + 1)
            ]
            for u in range(SUB)
        ]
        rows = [
            jnp.where(inside, jnp.where(lane == at + u, 1.0, 0.0), rows[u])
            for u in range(SUB)
        ]
        low = [[None] * SUB for _ in range(SUB)]
        scale = []
        for t in range(SUB):
            r = lax.rsqrt(e[t][t])
            scale.append(r)
            for u in range(t + 1, SUB):
                low[u][t] = e[u][t] * r
            for u in range(t + 1, SUB):
                for v in range(t + 1, u + 1):
                    e[u][v] = e[u][v] - low[u][t] * low[v][t]
            rows[t] = rows[t] * r
            for u in range(t + 1, SUB):
                rows[u] = rows[u] - low[u][t] * rows[t]
        last = BLOCK // SUB
        if g + 1 < last:
            base = at + SUB
            rest = work[base : base + SUB, :]
            c = [
                jnp.broadcast_to(rest[:, at + t : at + t + 1], (SUB, BLOCK))
                for t in range(SUB)
            ]
            rest = jnp.where(inside, 0.0, rest)
            for t in range(SUB):
                c[t] = c[t] * scale[t]
                for s in range(t + 1, SUB):
                    c[s] = c[s] - low[s][t] * c[t]
                rest = rest - c[t] * rows[t]
            work[base : base + SUB, :] = rest
        done = rows[0]
        for t in range(1, SUB):
            done = jnp.where(row == t, rows[t], done)
        if g + 2 < last:
            turned = done.T
        for below in range(g + 2, last):
            base = below * SUB
            rest = jnp.where(inside, 0.0, work[base : base + SUB, :])
            for t in range(SUB):
                c = jnp.broadcast_to(turned[base : base + SUB, t : t + 1], (SUB, BLOCK))
                rest = rest - c * rows[t]
            work[base : base + SUB, :] = rest
        work[at : at + SUB, :] = done


def factor_step_kernel(size, n_in, *refs):
    place, squares = refs[0], refs[1 : 1 + n_in]
    if size > BLOCK:
        inverse, column, rest, work = refs[-4:]
    else:
        inverse, work = refs[-2:]
    if n_in == 1:
        square = squares[0]
    else:
        square = rest_in = refs[-5]
        own = squares[0].shape[0]

        def assemble(mine):
            for k in range(GROUP):
                start = (mine ^ k) * own
                if start < size:
                    stop = min(start + own, size)
                    rest_in[start:stop, :] = squares[k][: stop - start, :]

        for mine in range(GROUP):
            pl.when(place[0] == mine)(functools.partial(assemble, mine))
    work[...] = square[:BLOCK, :BLOCK]
    invert_factor(work)
    i = lax.broadcasted_iota(jnp.int32, (BLOCK, BLOCK), 0)
    j = lax.broadcasted_iota(jnp.int32, (BLOCK, BLOCK), 1)
    value = jnp.where(j <= i, work[...], 0.0)
    inverse[...] = value
    if size > BLOCK:
        below = precise(square[BLOCK:, :BLOCK], value, 1)
        column[...] = below
        for n in range(size // BLOCK - 1):
            cut = slice(n * BLOCK, size - BLOCK)
            across = slice(n * BLOCK, (n + 1) * BLOCK)
            rest[cut, across] = square[
                (n + 1) * BLOCK :, (n + 1) * BLOCK : (n + 2) * BLOCK
            ] - precise(below[n * BLOCK :, :], below[across, :], 1)


def factor_step(place, squares, size, waits):
    left = size - BLOCK
    out_shape = [f32(BLOCK, BLOCK)]
    scratch = [pltpu.VMEM((BLOCK, BLOCK), jnp.float32)]
    if left:
        out_shape += [f32(left, BLOCK), f32(left, left)]
    n_in = len(squares)
    kernel = functools.partial(factor_step_kernel, size, n_in)
    if n_in > 1:

        def kernel(*refs):
            *others, work, whole = refs
            outs = 3 if left else 1
            return factor_step_kernel(
                size, n_in, *others[:-outs], whole, *others[-outs:], work
            )

        scratch.append(pltpu.VMEM((size, size), jnp.float32))
    return pl.pallas_call(
        kernel,
        out_shape=out_shape,
        in_specs=[SMEM] + [VMEM] * n_in + [ANYWHERE] * len(waits),
        out_specs=[VMEM] * len(out_shape),
        scratch_shapes=scratch,
        compiler_params=room(*out_shape, f32(size, size), *squares),
        cost_estimate=cost(3_500_000_000),
    )(place, *squares, *waits)


def solve_kernel(blocks, n_lead, rel, scale, *refs):
    lead, refs = refs[:n_lead], refs[n_lead:]
    inverses, below = refs[:blocks], refs[blocks : 2 * blocks - 1]
    panel, weights = refs[-2:]
    found = []
    for k in range(blocks):
        across = slice(k * BLOCK, (k + 1) * BLOCK)
        total = lead[0][:, across]
        for x in lead[1:]:
            total = total + x[:, across]
        total = rel[:, across] + total * scale[0:1, :]
        for j in range(k):
            start = (k - j - 1) * BLOCK
            total = total - precise(found[j], below[j][start : start + BLOCK, :], 1)
        found.append(precise(total, inverses[k][...], 1))
        panel[:, k * BLOCK : (k + 1) * BLOCK] = found[k]
    for k in reversed(range(blocks)):
        total = found[k]
        for j in range(k + 1, blocks):
            start = (j - k - 1) * BLOCK
            total = total - precise(found[j], below[k][start : start + BLOCK, :], 0)
        found[k] = precise(total, inverses[k][...], 0)
        weights[:, k * BLOCK : (k + 1) * BLOCK] = found[k]


def solve(rel, scale, lead, inverses, below):
    own = rel.shape[0]
    return pl.pallas_call(
        functools.partial(solve_kernel, len(inverses), len(lead)),
        out_shape=[f32(own, PANEL), f32(own, PANEL)],
        in_specs=[VMEM] * (1 + len(lead) + 2 * len(inverses)),
        out_specs=[VMEM, VMEM],
        compiler_params=room(rel, rel, rel, *lead, *inverses, *below),
        cost_estimate=cost(4 * own * PANEL * PANEL),
    )(rel, scale, *lead, *inverses, *below)


def head_kernel(n_left, sizes, place, *refs):
    left, head = refs[:n_left], refs[n_left : n_left + GROUP]
    outs = refs[-len(sizes) :]
    own = head[0].shape[0]

    def for_member(mine):
        for k in range(GROUP):
            start = (mine ^ k) * own
            width = min(own, PANEL - start)
            if width > 0:
                at = 0
                for out, count in zip(outs, sizes):
                    for n in range(count):
                        product = times(left[at][...], head[k][...])
                        out[n * own : (n + 1) * own, start : start + width] = product[
                            :, :width
                        ]
                        at += 1

    for mine in range(GROUP):
        pl.when(place[0] == mine)(functools.partial(for_member, mine))


def head_products(place, groups, head, waits):
    own = head[0].shape[0]
    left = [x for group in groups for x in group]
    sizes = [len(group) for group in groups]
    return pl.pallas_call(
        functools.partial(head_kernel, len(left), sizes),
        out_shape=[f32(n * own, PANEL) for n in sizes],
        in_specs=[SMEM] + [VMEM] * (len(left) + GROUP) + [ANYWHERE] * len(waits),
        out_specs=[VMEM] * len(sizes),
        compiler_params=room(*left, *head, f32(len(left) * own, PANEL)),
        cost_estimate=cost(2 * len(left) * own * PANEL * head[0].shape[1]),
    )(place, *left, *head, *waits)


def message_kernel(n_cols, place, scale, *refs):
    first, cols, out = refs[0], refs[1 : 1 + n_cols], refs[-1]
    head = refs[1 + n_cols : 1 + n_cols + GROUP]
    own = first.shape[0]
    out[own : own + SUB, :] = jnp.full((SUB, PANEL), scale[0], jnp.float32)

    def for_member(mine):
        for k in range(GROUP):
            start = (mine ^ k) * own
            width = min(own, PANEL - start)
            if width > 0:
                for n, block in enumerate((first,) + tuple(cols)):
                    base = n * own + (SUB if n else 0)
                    product = times(block[...], head[k][...])
                    out[base : base + own, start : start + width] = product[:, :width]

    for mine in range(GROUP):
        pl.when(place[0] == mine)(functools.partial(for_member, mine))


def message(place, scale, first, cols, head, waits):
    own = first.shape[0]
    rows = (1 + len(cols)) * own + SUB
    return pl.pallas_call(
        functools.partial(message_kernel, len(cols)),
        out_shape=f32(rows, PANEL),
        in_specs=[SMEM, SMEM]
        + [VMEM] * (1 + len(cols) + GROUP)
        + [ANYWHERE] * len(waits),
        out_specs=VMEM,
        compiler_params=room(first, *cols, *head, f32(rows, PANEL)),
        cost_estimate=cost(2 * rows * PANEL * first.shape[1]),
    )(place, scale, first, *cols, *head, *waits)


def sums_kernel(n_got, part, mine, *refs):
    got, keep, rel_first = refs[:n_got], refs[n_got], refs[n_got + 1]
    rel_side = refs[n_got + 2 : n_got + 2 + part]
    total, side, inverse = refs[-3:]
    own = total.shape[0]
    scale = mine[own : own + 1, :]
    rows = mine[:own, :]
    for x in got:
        scale = scale + x[own : own + 1, :]
        rows = rows + x[:own, :]
    scale = 1.0 / scale
    total[...] = rel_first[...] + rows * scale
    for n in range(part):
        cut = slice(n * own, (n + 1) * own)
        rows = keep[cut, :]
        for x in got:
            rows = rows + x[(n + 1) * own + SUB : (n + 2) * own + SUB, :]
        side[cut, :] = rel_side[n][...] + rows * scale
    inverse[...] = jnp.broadcast_to(scale[:, :BLOCK], (SUB, BLOCK))


def sums(mine, got, keep, rel_first, rel_side):
    own = rel_first.shape[0]
    part = len(rel_side)
    return pl.pallas_call(
        functools.partial(sums_kernel, len(got), part),
        out_shape=[f32(own, PANEL), f32(part * own, PANEL), f32(SUB, BLOCK)],
        in_specs=[VMEM] * (3 + len(got) + part),
        out_specs=[VMEM] * 3,
        compiler_params=room(mine, *got, keep, keep, rel_first, rel_first, *rel_side),
        cost_estimate=cost(10_000_000),
    )(mine, *got, keep, rel_first, *rel_side)


def gram_kernel(n_cols, n_more, *refs):
    plane, cols = refs[:GROUP], refs[GROUP : GROUP + n_cols]
    more = refs[GROUP + n_cols : GROUP + n_cols + n_more]
    outs = refs[-GROUP:]
    own = plane[0].shape[0]
    for k in range(GROUP):
        for j in range(n_cols):
            product = times(cols[j][...], plane[k][...])
            across = slice(j * own, (j + 1) * own)
            for x in more:
                product = product + x[across, k * own : (k + 1) * own]
            outs[k][:, across] = product.T


def gram_out_kernel(n_cols, *refs):
    plane, cols, out = refs[:GROUP], refs[GROUP : GROUP + n_cols], refs[-1]
    own = plane[0].shape[0]
    for k in range(GROUP):
        for j in range(n_cols):
            out[j * own : (j + 1) * own, k * own : (k + 1) * own] = times(
                cols[j][...], plane[k][...]
            )


def gram_products(plane, cols, more, waits):
    own, depth = plane[0].shape
    width = len(cols) * own
    if more is None:
        kernel = functools.partial(gram_out_kernel, len(cols))
        out_shape, out_specs, more = f32(width, GROUP * own), VMEM, []
    else:
        kernel = functools.partial(gram_kernel, len(cols), len(more))
        out_shape, out_specs = [f32(own, width)] * GROUP, [VMEM] * GROUP
    return pl.pallas_call(
        kernel,
        out_shape=out_shape,
        in_specs=[VMEM] * (GROUP + len(cols) + len(more))
        + [ANYWHERE] * len(waits),
        out_specs=out_specs,
        compiler_params=room(*plane, *cols, *more, f32(GROUP * own, width)),
        cost_estimate=cost(2 * GROUP * own * width * depth),
    )(*plane, *cols, *more, *waits)


def update_kernel(own, part, place, scale, rel, weights, *refs):
    pieces, sides, out = refs[:GROUP], refs[GROUP : 2 * GROUP], refs[2 * GROUP]
    i = lax.broadcasted_iota(jnp.int32, (own, own), 0)
    j = lax.broadcasted_iota(jnp.int32, (own, own), 1)
    ridge = jnp.where(i == j, RIDGE, 0.0)

    high, low = split(weights[...])

    def for_member(mine):
        for k in range(GROUP):
            side_high, side_low = split(sides[k][...])
            product = times(high, side_low) + times(low, side_high)
            product = product + times(high, side_high)
            for n in range(part):
                at = (n * GROUP + (mine ^ k)) * own
                cut = slice(n * own, (n + 1) * own)
                value = rel[:, at : at + own] + pieces[k][:, cut] * scale[0:1, 0:1]
                value = value - product[:, cut]
                if k == 0:
                    value = value + ridge * jnp.where(place[1] == n, 1.0, 0.0)
                out[:, at : at + own] = value

    for mine in range(GROUP):
        pl.when(place[0] == mine)(functools.partial(for_member, mine))


def final_update(place, scale, rel, weights, pieces, sides):
    own, width = rel.shape
    part = width // (GROUP * own)
    return pl.pallas_call(
        functools.partial(update_kernel, own, part),
        out_shape=f32(own, width),
        in_specs=[SMEM] + [VMEM] * (3 + 2 * GROUP),
        out_specs=VMEM,
        compiler_params=room(rel, rel, weights, *pieces, *sides, *sides),
        cost_estimate=cost(2 * own * width * PANEL),
    )(place, scale, rel, weights, *pieces, *sides)


def nothing(*refs):
    pass


def after(x, *done):
    return pl.pallas_call(
        nothing,
        out_shape=jax.ShapeDtypeStruct(x.shape, x.dtype),
        in_specs=[ANYWHERE] * (1 + len(done)),
        out_specs=ANYWHERE,
        input_output_aliases={0: 0},
        compiler_params=pltpu.CompilerParams(vmem_limit_bytes=2**20),
    )(x, *done)


def select_order(blocks, member):
    bit = 1
    while bit < len(blocks):
        swap = (member & bit) != 0
        blocks = [
            jnp.where(swap, blocks[k ^ bit], blocks[k]) for k in range(len(blocks))
        ]
        bit *= 2
    return blocks


def make(n_rows, n_snp):
    lines = n_rows // GROUP
    part = lines // n_snp
    far = lines // 2

    def rows_xor(x, bits):
        return lax.ppermute(x, "rows", [(r, r ^ bits) for r in range(n_rows)])

    def snp_xor(x, bits):
        return lax.ppermute(x, "snp", [(s, s ^ bits) for s in range(n_snp)])

    def from_first_snp(x, rank):
        got = x
        for s in range(1, n_snp):
            got = jnp.where(rank == s, lax.ppermute(x, "snp", [(0, s)]), got)
        return got

    def group_gather(x):
        core = rows_xor(x, 1)
        other = rows_xor(x, 2)
        return [x, core, other, rows_xor(other, 1)]

    def line_gather(x, hold):
        near = {k: rows_xor(x, k * GROUP) for k in range(1, far)}
        passed = hold(rows_xor(x, far * GROUP), list(near.values()))
        parts = {0: x, far: passed, **near}
        for k in range(1, far):
            parts[far + k] = rows_xor(passed, k * GROUP)
        return [parts[k] for k in range(lines)]

    def rows_sum(x):
        bit = 1
        while bit < n_rows:
            if bit * 2 < n_rows:
                parts = [x] + [rows_xor(x, bit * k) for k in (1, 2, 3)]
                x = (parts[0] + parts[1]) + (parts[2] + parts[3])
                bit *= 4
            else:
                x = x + rows_xor(x, bit)
                bit *= 2
        return x

    def snp_sum(x):
        bit = 1
        while bit < n_snp:
            x = x + snp_xor(x, bit)
            bit *= 2
        return x

    def per_device(genotypes, relationship):
        own = genotypes.shape[1]
        rank = lax.axis_index("rows")
        col = lax.axis_index("snp")
        q = rank % GROUP
        z = rank // GROUP
        place = jnp.stack([q, z - col * part]).astype(jnp.int32)

        called = genotypes >= 0
        dosage = jnp.where(called, genotypes, 0.0)
        stats = jnp.stack(
            [jnp.sum(dosage, axis=1), jnp.sum(called.astype(jnp.float32), axis=1)]
        )
        stats = rows_sum(stats)
        frequency = stats[0] / (2.0 * stats[1])
        scale_part = jnp.sum(2.0 * frequency * (1.0 - frequency))
        gt = lax.optimization_barrier(genotypes.T)
        centered = jnp.where(gt >= 0, gt - 2.0 * frequency[None, :], 0.0).astype(
            jnp.bfloat16
        )

        rel_own = from_first_snp(relationship[:, :PANEL], col)
        ids = rank * own + lax.broadcasted_iota(jnp.int32, rel_own.shape, 0)
        rel_own = rel_own + jnp.where(
            ids == lax.broadcasted_iota(jnp.int32, rel_own.shape, 1), RIDGE, 0.0
        )

        core, other = rows_xor(centered, 1), rows_xor(centered, 2)
        line = line_gather(centered, lambda x, near: after(x, rel_own, *near))
        line[-1] = after(line[-1], other)
        plane = [centered, core, other, rows_xor(other, 1)]
        first = select_order(line, z)[0]
        member = after((z ^ (col * part)).astype(jnp.int32).reshape(1), first)
        ordered = select_order(line, member[0])
        groups = [ordered[bits * part : (bits + 1) * part] for bits in range(n_snp)]

        leaving = [gram_products(plane, groups[b], None, []) for b in range(1, n_snp)]

        head = [first, rows_xor(first, 1)]
        rel_line = line_gather(after(rel_own, head[1]), lambda x, near: x)
        head.append(after(rows_xor(first, 2), *rel_line[1 : far + 1], *leaving))
        head.append(rows_xor(head[2], 1))
        messages = [
            message(
                place,
                scale_part.reshape(1),
                first,
                groups[b],
                head,
                [],
            )
            for b in range(1, n_snp)
        ]
        got = [snp_xor(messages[b - 1], b) for b in range(1, n_snp)]
        keep, lead = head_products(place, [groups[0], [centered]], head, messages)
        total, side, scale = sums(
            messages[0],
            got,
            keep,
            select_order(rel_line, z)[0],
            select_order(rel_line, z ^ (col * part))[:part],
        )

        diagonal = group_gather(total)
        side = after(side, diagonal[2])
        sides = [side, rows_xor(side, 1), rows_xor(side, 2)]

        gram_got = [
            snp_xor(after(leaving[b - 1], messages[0]), b) for b in range(1, n_snp)
        ]
        pieces = gram_products(plane, groups[0], gram_got, [])
        moved = [pieces[0]] + [rows_xor(pieces[k], k) for k in range(1, GROUP)]
        leads = [lead] + [snp_xor(after(lead, total), b) for b in range(1, n_snp)]

        squares, inverses, below = diagonal, [], []
        waits = [[], gram_got, [pieces[1]], []]
        for k in range(PANEL // BLOCK):
            inv, *more = factor_step(place, squares, PANEL - k * BLOCK, waits[k])
            inverses.append(inv)
            if more:
                below.append(more[0])
                squares = [more[1]]
        sides[2] = after(sides[2], inverses[2])
        sides.append(rows_xor(sides[2], 1))

        panel, weights = solve(rel_own, scale, leads, inverses, below)
        updated = final_update(place, scale, relationship, weights, moved, sides)
        return updated, panel

    return per_device


def solution(mesh):
    return jax.shard_map(
        make(mesh.shape["rows"], mesh.shape["snp"]),
        mesh=mesh,
        in_specs=(P("snp", "rows"), P("rows", "snp")),
        out_specs=(P("rows", "snp"), P("rows", None)),
        check_vma=False,
    )
```

```python
import functools

import jax
import jax.numpy as jnp
from jax import lax
from jax.experimental import pallas as pl
from jax.experimental.pallas import tpu as pltpu
from jax.sharding import PartitionSpec as P

PANEL = 512
RIDGE = 0.25
GROUP = 4
BLOCK = 128
SUB = 8

VMEM = pl.BlockSpec(memory_space=pltpu.VMEM)
SMEM = pl.BlockSpec(memory_space=pltpu.SMEM)
ANYWHERE = pl.BlockSpec(memory_space=pl.ANY)


def precise(a, b, contract):
    return lax.dot_general(
        a,
        b,
        (((1,), (contract,)), ((), ())),
        precision=lax.Precision.HIGHEST,
        preferred_element_type=jnp.float32,
    )


def times(a, b):
    return lax.dot_general(
        a, b, (((1,), (1,)), ((), ())), preferred_element_type=jnp.float32
    )


def split(x):
    high = x.astype(jnp.bfloat16)
    return high, (x - high.astype(jnp.float32)).astype(jnp.bfloat16)


def cost(flops):
    return pl.CostEstimate(flops=flops, bytes_accessed=131072, transcendentals=0)


def room(*arrays):
    total = sum(x.size * x.dtype.itemsize for x in arrays)
    return pltpu.CompilerParams(vmem_limit_bytes=total * 3 // 2 + 3 * 2**20)


def f32(*shape):
    return jax.ShapeDtypeStruct(shape, jnp.float32)


def invert_factor(work):
    lane = lax.broadcasted_iota(jnp.int32, (SUB, BLOCK), 1)
    for g in range(BLOCK // SUB):
        at = g * SUB
        own = work[at : at + SUB, :]
        inside = (lane >= at) & (lane < at + SUB)
        rows = [jnp.broadcast_to(own[u : u + 1, :], (SUB, BLOCK)) for u in range(SUB)]
        e = [
            [
                jnp.broadcast_to(rows[t][:, at + u : at + u + 1], (SUB, BLOCK))
                for t in range(u + 1)
            ]
            for u in range(SUB)
        ]
        rows = [
            jnp.where(inside, jnp.where(lane == at + u, 1.0, 0.0), rows[u])
            for u in range(SUB)
        ]
        low = [[None] * SUB for _ in range(SUB)]
        scale = []
        for t in range(SUB):
            r = lax.rsqrt(e[t][t])
            scale.append(r)
            for u in range(t + 1, SUB):
                low[u][t] = e[u][t] * r
            for u in range(t + 1, SUB):
                for v in range(t + 1, u + 1):
                    e[u][v] = e[u][v] - low[u][t] * low[v][t]
            rows[t] = rows[t] * r
            for u in range(t + 1, SUB):
                rows[u] = rows[u] - low[u][t] * rows[t]
        for below in range(g + 1, BLOCK // SUB):
            base = below * SUB
            rest = work[base : base + SUB, :]
            c = [
                jnp.broadcast_to(rest[:, at + t : at + t + 1], (SUB, BLOCK))
                for t in range(SUB)
            ]
            rest = jnp.where(inside, 0.0, rest)
            for t in range(SUB):
                c[t] = c[t] * scale[t]
                for s in range(t + 1, SUB):
                    c[s] = c[s] - low[s][t] * c[t]
                rest = rest - c[t] * rows[t]
            work[base : base + SUB, :] = rest
        for t in range(SUB):
            work[at + t : at + t + 1, :] = rows[t][0:1, :]


def factor_step_kernel(size, n_in, *refs):
    place, squares = refs[0], refs[1 : 1 + n_in]
    if size > BLOCK:
        inverse, column, rest, work = refs[-4:]
    else:
        inverse, work = refs[-2:]
    if n_in == 1:
        square = squares[0]
    else:
        square = rest_in = refs[-5]
        own = squares[0].shape[0]

        def assemble(mine):
            for k in range(GROUP):
                start = (mine ^ k) * own
                if start < size:
                    stop = min(start + own, size)
                    rest_in[start:stop, :] = squares[k][: stop - start, :]

        for mine in range(GROUP):
            pl.when(place[0] == mine)(functools.partial(assemble, mine))
    work[...] = square[:BLOCK, :BLOCK]
    invert_factor(work)
    i = lax.broadcasted_iota(jnp.int32, (BLOCK, BLOCK), 0)
    j = lax.broadcasted_iota(jnp.int32, (BLOCK, BLOCK), 1)
    value = jnp.where(j <= i, work[...], 0.0)
    inverse[...] = value
    if size > BLOCK:
        below = precise(square[BLOCK:, :BLOCK], value, 1)
        column[...] = below
        for n in range(size // BLOCK - 1):
            cut = slice(n * BLOCK, size - BLOCK)
            across = slice(n * BLOCK, (n + 1) * BLOCK)
            rest[cut, across] = square[
                (n + 1) * BLOCK :, (n + 1) * BLOCK : (n + 2) * BLOCK
            ] - precise(below[n * BLOCK :, :], below[across, :], 1)


def factor_step(place, squares, size, waits):
    left = size - BLOCK
    out_shape = [f32(BLOCK, BLOCK)]
    scratch = [pltpu.VMEM((BLOCK, BLOCK), jnp.float32)]
    if left:
        out_shape += [f32(left, BLOCK), f32(left, left)]
    n_in = len(squares)
    kernel = functools.partial(factor_step_kernel, size, n_in)
    if n_in > 1:

        def kernel(*refs):
            *others, work, whole = refs
            outs = 3 if left else 1
            return factor_step_kernel(
                size, n_in, *others[:-outs], whole, *others[-outs:], work
            )

        scratch.append(pltpu.VMEM((size, size), jnp.float32))
    return pl.pallas_call(
        kernel,
        out_shape=out_shape,
        in_specs=[SMEM] + [VMEM] * n_in + [ANYWHERE] * len(waits),
        out_specs=[VMEM] * len(out_shape),
        scratch_shapes=scratch,
        compiler_params=room(*out_shape, f32(size, size), *squares),
        cost_estimate=cost(6_000_000_000),
    )(place, *squares, *waits)


def solve_kernel(blocks, columns, *refs):
    inverses, below = refs[:blocks], refs[blocks : 2 * blocks - 1]
    panel, weights = refs[-2:]
    found = []
    for k in range(blocks):
        total = columns[:, k * BLOCK : (k + 1) * BLOCK]
        for j in range(k):
            start = (k - j - 1) * BLOCK
            total = total - precise(found[j], below[j][start : start + BLOCK, :], 1)
        found.append(precise(total, inverses[k][...], 1))
        panel[:, k * BLOCK : (k + 1) * BLOCK] = found[k]
    for k in reversed(range(blocks)):
        total = found[k]
        for j in range(k + 1, blocks):
            start = (j - k - 1) * BLOCK
            total = total - precise(found[j], below[k][start : start + BLOCK, :], 0)
        found[k] = precise(total, inverses[k][...], 0)
        weights[:, k * BLOCK : (k + 1) * BLOCK] = found[k]


def solve(columns, inverses, below):
    own = columns.shape[0]
    return pl.pallas_call(
        functools.partial(solve_kernel, len(inverses)),
        out_shape=[f32(own, PANEL), f32(own, PANEL)],
        in_specs=[VMEM] * (2 * len(inverses)),
        out_specs=[VMEM, VMEM],
        compiler_params=room(columns, columns, columns, *inverses, *below),
        cost_estimate=cost(4 * own * PANEL * PANEL),
    )(columns, *inverses, *below)


def head_kernel(n_left, sizes, place, *refs):
    left, head = refs[:n_left], refs[n_left : n_left + GROUP]
    outs = refs[-len(sizes) :]
    own = head[0].shape[0]

    def for_member(mine):
        for k in range(GROUP):
            start = (mine ^ k) * own
            width = min(own, PANEL - start)
            if width > 0:
                at = 0
                for out, count in zip(outs, sizes):
                    for n in range(count):
                        product = times(left[at][...], head[k][...])
                        out[n * own : (n + 1) * own, start : start + width] = product[
                            :, :width
                        ]
                        at += 1

    for mine in range(GROUP):
        pl.when(place[0] == mine)(functools.partial(for_member, mine))


def head_products(place, groups, head, waits):
    own = head[0].shape[0]
    left = [x for group in groups for x in group]
    sizes = [len(group) for group in groups]
    return pl.pallas_call(
        functools.partial(head_kernel, len(left), sizes),
        out_shape=[f32(n * own, PANEL) for n in sizes],
        in_specs=[SMEM] + [VMEM] * (len(left) + GROUP) + [ANYWHERE] * len(waits),
        out_specs=[VMEM] * len(sizes),
        compiler_params=room(*left, *head, f32(len(left) * own, PANEL)),
        cost_estimate=cost(2 * len(left) * own * PANEL * head[0].shape[1]),
    )(place, *left, *head, *waits)


def gram_kernel(n_cols, n_more, *refs):
    plane, cols = refs[:GROUP], refs[GROUP : GROUP + n_cols]
    more = refs[GROUP + n_cols : GROUP + n_cols + n_more]
    outs = refs[-GROUP:]
    own = plane[0].shape[0]
    for k in range(GROUP):
        for j in range(n_cols):
            product = times(cols[j][...], plane[k][...])
            across = slice(j * own, (j + 1) * own)
            for x in more:
                product = product + x[across, k * own : (k + 1) * own]
            outs[k][:, across] = product.T


def gram_out_kernel(n_cols, *refs):
    plane, cols, out = refs[:GROUP], refs[GROUP : GROUP + n_cols], refs[-1]
    own = plane[0].shape[0]
    for k in range(GROUP):
        for j in range(n_cols):
            out[j * own : (j + 1) * own, k * own : (k + 1) * own] = times(
                cols[j][...], plane[k][...]
            )


def gram_products(plane, cols, more, waits):
    own, depth = plane[0].shape
    width = len(cols) * own
    if more is None:
        kernel = functools.partial(gram_out_kernel, len(cols))
        out_shape, out_specs, more = f32(width, GROUP * own), VMEM, []
    else:
        kernel = functools.partial(gram_kernel, len(cols), len(more))
        out_shape, out_specs = [f32(own, width)] * GROUP, [VMEM] * GROUP
    return pl.pallas_call(
        kernel,
        out_shape=out_shape,
        in_specs=[VMEM] * (GROUP + len(cols) + len(more))
        + [ANYWHERE] * len(waits),
        out_specs=out_specs,
        compiler_params=room(*plane, *cols, *more, f32(GROUP * own, width)),
        cost_estimate=cost(2 * GROUP * own * width * depth),
    )(*plane, *cols, *more, *waits)


def update_kernel(own, part, place, scale, rel, weights, *refs):
    pieces, sides, out = refs[:GROUP], refs[GROUP : 2 * GROUP], refs[2 * GROUP]
    i = lax.broadcasted_iota(jnp.int32, (own, own), 0)
    j = lax.broadcasted_iota(jnp.int32, (own, own), 1)
    ridge = jnp.where(i == j, RIDGE, 0.0)

    high, low = split(weights[...])

    def for_member(mine):
        for k in range(GROUP):
            side_high, side_low = split(sides[k][...])
            product = times(high, side_low) + times(low, side_high)
            product = product + times(high, side_high)
            for n in range(part):
                at = (n * GROUP + (mine ^ k)) * own
                cut = slice(n * own, (n + 1) * own)
                value = rel[:, at : at + own] + pieces[k][:, cut] * scale[0]
                value = value - product[:, cut]
                if k == 0:
                    value = value + ridge * jnp.where(place[1] == n, 1.0, 0.0)
                out[:, at : at + own] = value

    for mine in range(GROUP):
        pl.when(place[0] == mine)(functools.partial(for_member, mine))


def final_update(place, scale, rel, weights, pieces, sides):
    own, width = rel.shape
    part = width // (GROUP * own)
    return pl.pallas_call(
        functools.partial(update_kernel, own, part),
        out_shape=f32(own, width),
        in_specs=[SMEM, SMEM] + [VMEM] * (2 + 2 * GROUP),
        out_specs=VMEM,
        compiler_params=room(rel, rel, weights, *pieces, *sides, *sides),
        cost_estimate=cost(2 * own * width * PANEL),
    )(place, scale, rel, weights, *pieces, *sides)


def nothing(*refs):
    pass


def after(x, *done):
    return pl.pallas_call(
        nothing,
        out_shape=jax.ShapeDtypeStruct(x.shape, x.dtype),
        in_specs=[ANYWHERE] * (1 + len(done)),
        out_specs=ANYWHERE,
        input_output_aliases={0: 0},
        compiler_params=pltpu.CompilerParams(vmem_limit_bytes=2**20),
    )(x, *done)


def select_order(blocks, member):
    bit = 1
    while bit < len(blocks):
        swap = (member & bit) != 0
        blocks = [
            jnp.where(swap, blocks[k ^ bit], blocks[k]) for k in range(len(blocks))
        ]
        bit *= 2
    return blocks


def make(n_rows, n_snp):
    lines = n_rows // GROUP
    part = lines // n_snp
    far = lines // 2

    def rows_xor(x, bits):
        return lax.ppermute(x, "rows", [(r, r ^ bits) for r in range(n_rows)])

    def snp_xor(x, bits):
        return lax.ppermute(x, "snp", [(s, s ^ bits) for s in range(n_snp)])

    def from_first_snp(x, rank):
        got = x
        for s in range(1, n_snp):
            got = jnp.where(rank == s, lax.ppermute(x, "snp", [(0, s)]), got)
        return got

    def group_gather(x):
        core = rows_xor(x, 1)
        other = rows_xor(x, 2)
        return [x, core, other, rows_xor(other, 1)]

    def line_gather(x, hold):
        near = {k: rows_xor(x, k * GROUP) for k in range(1, far)}
        passed = hold(rows_xor(x, far * GROUP), list(near.values()))
        parts = {0: x, far: passed, **near}
        for k in range(1, far):
            parts[far + k] = rows_xor(passed, k * GROUP)
        return [parts[k] for k in range(lines)]

    def rows_sum(x):
        bit = 1
        while bit < n_rows:
            if bit * 2 < n_rows:
                parts = [x] + [rows_xor(x, bit * k) for k in (1, 2, 3)]
                x = (parts[0] + parts[1]) + (parts[2] + parts[3])
                bit *= 4
            else:
                x = x + rows_xor(x, bit)
                bit *= 2
        return x

    def snp_sum(x):
        bit = 1
        while bit < n_snp:
            x = x + snp_xor(x, bit)
            bit *= 2
        return x

    def per_device(genotypes, relationship):
        own = genotypes.shape[1]
        rank = lax.axis_index("rows")
        col = lax.axis_index("snp")
        q = rank % GROUP
        z = rank // GROUP
        place = jnp.stack([q, z - col * part]).astype(jnp.int32)

        called = genotypes >= 0
        dosage = jnp.where(called, genotypes, 0.0)
        stats = jnp.stack(
            [jnp.sum(dosage, axis=1), jnp.sum(called.astype(jnp.float32), axis=1)]
        )
        stats = rows_sum(stats)
        frequency = stats[0] / (2.0 * stats[1])
        scale_part = jnp.sum(2.0 * frequency * (1.0 - frequency))
        gt = lax.optimization_barrier(genotypes.T)
        centered = jnp.where(gt >= 0, gt - 2.0 * frequency[None, :], 0.0).astype(
            jnp.bfloat16
        )

        rel_own = from_first_snp(relationship[:, :PANEL], col)
        ids = rank * own + lax.broadcasted_iota(jnp.int32, rel_own.shape, 0)
        rel_own = rel_own + jnp.where(
            ids == lax.broadcasted_iota(jnp.int32, rel_own.shape, 1), RIDGE, 0.0
        )

        core, other = rows_xor(centered, 1), rows_xor(centered, 2)
        line = line_gather(centered, lambda x, near: after(x, rel_own, *near))
        line[-1] = after(line[-1], other)
        plane = [centered, core, other, rows_xor(other, 1)]
        first = select_order(line, z)[0]
        member = after((z ^ (col * part)).astype(jnp.int32).reshape(1), first)[0]
        ordered = select_order(line, member)
        groups = [ordered[bits * part : (bits + 1) * part] for bits in range(n_snp)]
        rel_line = line_gather(after(rel_own, line[-1]), lambda x, near: x)

        leaving = [gram_products(plane, groups[b], None, []) for b in range(1, n_snp)]

        head = [first, rows_xor(first, 1)]
        head.append(after(rows_xor(first, 2), *rel_line[1 : far + 1], *leaving))
        head.append(rows_xor(head[2], 1))
        (rows,) = head_products(place, [[first]], head, [])
        rows = jnp.concatenate(
            [rows, jnp.broadcast_to(scale_part.reshape(1, 1), (SUB, PANEL))], axis=0
        )
        total = snp_sum(rows)
        inverse = 1.0 / total[own, 0]
        total = total[:own] * inverse + select_order(rel_line, z)[0]
        sides = head_products(place, groups, head, [rows])
        total = after(total, *sides[1:])
        side_got = [snp_xor(sides[bits], bits) for bits in range(1, n_snp)]

        (lead,) = head_products(place, [[centered]], head, [total])
        diagonal = [total, rows_xor(total, 1)]
        diagonal.append(after(rows_xor(total, 2), lead))
        diagonal.append(rows_xor(diagonal[2], 1))

        gram_got = [
            snp_xor(after(leaving[b - 1], *side_got), b) for b in range(1, n_snp)
        ]
        pieces = gram_products(plane, groups[0], gram_got, [])
        moved = [pieces[0]] + [rows_xor(pieces[k], k) for k in range(1, GROUP)]

        inv, column, square = factor_step(place, diagonal, PANEL, side_got)
        inverses, below = [inv], [column]
        side = sides[0]
        for got in side_got:
            side = side + after(got, inverses[0])
        rel_side = select_order(rel_line, z ^ (col * part))[:part]
        side = jnp.concatenate(
            [
                rel_side[j] + side[j * own : (j + 1) * own] * inverse
                for j in range(part)
            ],
            axis=0,
        )
        sides = [side, rows_xor(side, 1), rows_xor(side, 2)]

        waits = [[], [side], [], [pieces[1]]]
        for k in range(1, PANEL // BLOCK):
            inv, *more = factor_step(place, [square], PANEL - k * BLOCK, waits[k])
            inverses.append(inv)
            if more:
                column, square = more
                below.append(column)

        sides[2] = after(sides[2], inverses[2])
        sides.append(rows_xor(sides[2], 1))

        own_columns = rel_own + snp_sum(lead) * inverse
        panel, weights = solve(own_columns, inverses, below)
        updated = final_update(
            place, inverse.reshape(1), relationship, weights, moved, sides
        )
        return updated, panel

    return per_device


def solution(mesh):
    return jax.shard_map(
        make(mesh.shape["rows"], mesh.shape["snp"]),
        mesh=mesh,
        in_specs=(P("snp", "rows"), P("rows", "snp")),
        out_specs=(P("rows", "snp"), P("rows", None)),
        check_vma=False,
    )
```

```python
import functools

import jax
import jax.numpy as jnp
from jax import lax
from jax.experimental import pallas as pl
from jax.experimental.pallas import tpu as pltpu
from jax.sharding import PartitionSpec as P

PANEL = 512
RIDGE = 0.25
GROUP = 4
BLOCK = 128
SUB = 8

VMEM = pl.BlockSpec(memory_space=pltpu.VMEM)
SMEM = pl.BlockSpec(memory_space=pltpu.SMEM)
ANYWHERE = pl.BlockSpec(memory_space=pl.ANY)


def precise(a, b, contract):
    return lax.dot_general(
        a,
        b,
        (((1,), (contract,)), ((), ())),
        precision=lax.Precision.HIGHEST,
        preferred_element_type=jnp.float32,
    )


def times(a, b):
    return lax.dot_general(
        a, b, (((1,), (1,)), ((), ())), preferred_element_type=jnp.float32
    )


def split(x):
    high = x.astype(jnp.bfloat16)
    return high, (x - high.astype(jnp.float32)).astype(jnp.bfloat16)


def cost(flops):
    return pl.CostEstimate(flops=flops, bytes_accessed=131072, transcendentals=0)


def room(*arrays):
    total = sum(x.size * x.dtype.itemsize for x in arrays)
    return pltpu.CompilerParams(vmem_limit_bytes=total * 3 // 2 + 3 * 2**20)


def f32(*shape):
    return jax.ShapeDtypeStruct(shape, jnp.float32)


def invert_factor(work):
    lane = lax.broadcasted_iota(jnp.int32, (SUB, BLOCK), 1)
    for g in range(BLOCK // SUB):
        at = g * SUB
        own = work[at : at + SUB, :]
        inside = (lane >= at) & (lane < at + SUB)
        rows = [jnp.broadcast_to(own[u : u + 1, :], (SUB, BLOCK)) for u in range(SUB)]
        e = [
            [
                jnp.broadcast_to(rows[t][:, at + u : at + u + 1], (SUB, BLOCK))
                for t in range(u + 1)
            ]
            for u in range(SUB)
        ]
        rows = [
            jnp.where(inside, jnp.where(lane == at + u, 1.0, 0.0), rows[u])
            for u in range(SUB)
        ]
        low = [[None] * SUB for _ in range(SUB)]
        scale = []
        for t in range(SUB):
            r = lax.rsqrt(e[t][t])
            scale.append(r)
            for u in range(t + 1, SUB):
                low[u][t] = e[u][t] * r
            for u in range(t + 1, SUB):
                for v in range(t + 1, u + 1):
                    e[u][v] = e[u][v] - low[u][t] * low[v][t]
            rows[t] = rows[t] * r
            for u in range(t + 1, SUB):
                rows[u] = rows[u] - low[u][t] * rows[t]
        for below in range(g + 1, BLOCK // SUB):
            base = below * SUB
            rest = work[base : base + SUB, :]
            c = [
                jnp.broadcast_to(rest[:, at + t : at + t + 1], (SUB, BLOCK))
                for t in range(SUB)
            ]
            rest = jnp.where(inside, 0.0, rest)
            for t in range(SUB):
                c[t] = c[t] * scale[t]
                for s in range(t + 1, SUB):
                    c[s] = c[s] - low[s][t] * c[t]
                rest = rest - c[t] * rows[t]
            work[base : base + SUB, :] = rest
        for t in range(SUB):
            work[at + t : at + t + 1, :] = rows[t][0:1, :]


def in_order(place, blocks, out):
    rows = blocks[0].shape[0]
    for k in range(GROUP):
        start = pl.multiple_of((place[0] ^ k) * rows, 16)
        out[pl.ds(start, rows), :] = blocks[k][...]


def factor_step_kernel(size, n_in, *refs):
    place, squares = refs[0], refs[1 : 1 + n_in]
    if size > BLOCK:
        inverse, column, rest, work = refs[-4:]
    else:
        inverse, work = refs[-2:]
    if n_in == 1:
        square = squares[0]
    else:
        square = rest_in = refs[-5]
        in_order(place, squares, rest_in)
    work[...] = square[:BLOCK, :BLOCK]
    invert_factor(work)
    i = lax.broadcasted_iota(jnp.int32, (BLOCK, BLOCK), 0)
    j = lax.broadcasted_iota(jnp.int32, (BLOCK, BLOCK), 1)
    value = jnp.where(j <= i, work[...], 0.0)
    inverse[...] = value
    if size > BLOCK:
        below = precise(square[BLOCK:size, :BLOCK], value, 1)
        column[...] = below
        for n in range(size // BLOCK - 1):
            cut = slice(n * BLOCK, size - BLOCK)
            across = slice(n * BLOCK, (n + 1) * BLOCK)
            rest[cut, across] = square[
                (n + 1) * BLOCK : size, (n + 1) * BLOCK : (n + 2) * BLOCK
            ] - precise(below[n * BLOCK :, :], below[across, :], 1)


def factor_step(place, squares, size, waits):
    left = size - BLOCK
    out_shape = [f32(BLOCK, BLOCK)]
    scratch = [pltpu.VMEM((BLOCK, BLOCK), jnp.float32)]
    if left:
        out_shape += [f32(left, BLOCK), f32(left, left)]
    n_in = len(squares)
    kernel = functools.partial(factor_step_kernel, size, n_in)
    if n_in > 1:

        def kernel(*refs):
            *others, work, whole = refs
            outs = 3 if left else 1
            return factor_step_kernel(
                size, n_in, *others[:-outs], whole, *others[-outs:], work
            )

        scratch.append(pltpu.VMEM((GROUP * squares[0].shape[0], size), jnp.float32))
    return pl.pallas_call(
        kernel,
        out_shape=out_shape,
        in_specs=[SMEM] + [VMEM] * n_in + [ANYWHERE] * len(waits),
        out_specs=[VMEM] * len(out_shape),
        scratch_shapes=scratch,
        compiler_params=room(*out_shape, f32(2 * size, size), *squares),
        cost_estimate=cost(6_000_000_000),
    )(place, *squares, *waits)


def solve_kernel(blocks, columns, *refs):
    inverses, below = refs[:blocks], refs[blocks : 2 * blocks - 1]
    panel, weights = refs[-2:]
    found = []
    for k in range(blocks):
        total = columns[:, k * BLOCK : (k + 1) * BLOCK]
        for j in range(k):
            start = (k - j - 1) * BLOCK
            total = total - precise(found[j], below[j][start : start + BLOCK, :], 1)
        found.append(precise(total, inverses[k][...], 1))
        panel[:, k * BLOCK : (k + 1) * BLOCK] = found[k]
    for k in reversed(range(blocks)):
        total = found[k]
        for j in range(k + 1, blocks):
            start = (j - k - 1) * BLOCK
            total = total - precise(found[j], below[k][start : start + BLOCK, :], 0)
        found[k] = precise(total, inverses[k][...], 0)
        weights[:, k * BLOCK : (k + 1) * BLOCK] = found[k]


def solve(columns, inverses, below):
    own = columns.shape[0]
    return pl.pallas_call(
        functools.partial(solve_kernel, len(inverses)),
        out_shape=[f32(own, PANEL), f32(own, PANEL)],
        in_specs=[VMEM] * (2 * len(inverses)),
        out_specs=[VMEM, VMEM],
        compiler_params=room(columns, columns, columns, *inverses, *below),
        cost_estimate=cost(4 * own * PANEL * PANEL),
    )(columns, *inverses, *below)


def head_kernel(n_left, sizes, place, *refs):
    left, head = refs[:n_left], refs[n_left : n_left + GROUP]
    outs, order = refs[-1 - len(sizes) : -1], refs[-1]
    own = head[0].shape[0]
    in_order(place, head, order)
    at = 0
    for out, count in zip(outs, sizes):
        for n in range(count):
            out[n * own : (n + 1) * own, :] = times(left[at][...], order[:PANEL, :])
            at += 1


def head_products(place, groups, head, waits):
    own = head[0].shape[0]
    left = [x for group in groups for x in group]
    sizes = [len(group) for group in groups]
    return pl.pallas_call(
        functools.partial(head_kernel, len(left), sizes),
        out_shape=[f32(n * own, PANEL) for n in sizes],
        in_specs=[SMEM] + [VMEM] * (len(left) + GROUP) + [ANYWHERE] * len(waits),
        out_specs=[VMEM] * len(sizes),
        scratch_shapes=[pltpu.VMEM((GROUP * own, head[0].shape[1]), head[0].dtype)],
        compiler_params=room(*left, *head, *head, f32(len(left) * own, PANEL)),
        cost_estimate=cost(2 * len(left) * own * PANEL * head[0].shape[1]),
    )(place, *left, *head, *waits)


def gram_kernel(n_cols, n_more, *refs):
    plane, cols = refs[:GROUP], refs[GROUP : GROUP + n_cols]
    more = refs[GROUP + n_cols : GROUP + n_cols + n_more]
    outs = refs[-GROUP:]
    own = plane[0].shape[0]
    for k in range(GROUP):
        for j in range(n_cols):
            product = times(cols[j][...], plane[k][...])
            across = slice(j * own, (j + 1) * own)
            for x in more:
                product = product + x[across, k * own : (k + 1) * own]
            outs[k][:, across] = product.T


def gram_out_kernel(n_cols, *refs):
    plane, cols, out = refs[:GROUP], refs[GROUP : GROUP + n_cols], refs[-1]
    own = plane[0].shape[0]
    for k in range(GROUP):
        for j in range(n_cols):
            out[j * own : (j + 1) * own, k * own : (k + 1) * own] = times(
                cols[j][...], plane[k][...]
            )


def gram_products(plane, cols, more, waits):
    own, depth = plane[0].shape
    width = len(cols) * own
    if more is None:
        kernel = functools.partial(gram_out_kernel, len(cols))
        out_shape, out_specs, more = f32(width, GROUP * own), VMEM, []
    else:
        kernel = functools.partial(gram_kernel, len(cols), len(more))
        out_shape, out_specs = [f32(own, width)] * GROUP, [VMEM] * GROUP
    return pl.pallas_call(
        kernel,
        out_shape=out_shape,
        in_specs=[VMEM] * (GROUP + len(cols) + len(more))
        + [ANYWHERE] * len(waits),
        out_specs=out_specs,
        compiler_params=room(*plane, *cols, *more, f32(GROUP * own, width)),
        cost_estimate=cost(2 * GROUP * own * width * depth),
    )(*plane, *cols, *more, *waits)


def update_kernel(own, part, place, scale, rel, weights, *refs):
    pieces, sides = refs[:GROUP], refs[GROUP : 2 * GROUP]
    out, all_pieces, all_sides = refs[2 * GROUP :]
    in_order(place, pieces, all_pieces)
    in_order(place, sides, all_sides)
    i = lax.broadcasted_iota(jnp.int32, (own, own), 0)
    j = lax.broadcasted_iota(jnp.int32, (own, own), 1)
    ridge = jnp.where(i == j, RIDGE, 0.0)
    high, low = split(weights[...])
    width = part * own
    for m in range(GROUP):
        side_high, side_low = split(all_sides[m * width : (m + 1) * width, :])
        product = times(high, side_low) + times(low, side_high)
        product = product + times(high, side_high)
        for n in range(part):
            at = (n * GROUP + m) * own
            cut = slice(n * own, (n + 1) * own)
            here = (place[0] == m) & (place[1] == n)
            value = rel[:, at : at + own] - product[:, cut]
            value = value + all_pieces[m * own : (m + 1) * own, cut] * scale[0]
            out[:, at : at + own] = value + ridge * jnp.where(here, 1.0, 0.0)


def final_update(place, scale, rel, weights, pieces, sides):
    own, width = rel.shape
    part = width // (GROUP * own)
    return pl.pallas_call(
        functools.partial(update_kernel, own, part),
        out_shape=f32(own, width),
        in_specs=[SMEM, SMEM] + [VMEM] * (2 + 2 * GROUP),
        out_specs=VMEM,
        scratch_shapes=[
            pltpu.VMEM((GROUP * own, part * own), jnp.float32),
            pltpu.VMEM((width, PANEL), jnp.float32),
        ],
        compiler_params=room(rel, rel, weights, *pieces, *pieces, *sides, *sides),
        cost_estimate=cost(2 * own * width * PANEL),
    )(place, scale, rel, weights, *pieces, *sides)


def nothing(*refs):
    pass


def after(x, *done):
    return pl.pallas_call(
        nothing,
        out_shape=jax.ShapeDtypeStruct(x.shape, x.dtype),
        in_specs=[ANYWHERE] * (1 + len(done)),
        out_specs=ANYWHERE,
        input_output_aliases={0: 0},
        compiler_params=pltpu.CompilerParams(vmem_limit_bytes=2**20),
    )(x, *done)


def select_order(blocks, member):
    bit = 1
    while bit < len(blocks):
        swap = (member & bit) != 0
        blocks = [
            jnp.where(swap, blocks[k ^ bit], blocks[k]) for k in range(len(blocks))
        ]
        bit *= 2
    return blocks


def make(n_rows, n_snp):
    lines = n_rows // GROUP
    part = lines // n_snp
    far = lines // 2

    def rows_xor(x, bits):
        return lax.ppermute(x, "rows", [(r, r ^ bits) for r in range(n_rows)])

    def snp_xor(x, bits):
        return lax.ppermute(x, "snp", [(s, s ^ bits) for s in range(n_snp)])

    def from_first_snp(x, rank):
        got = x
        for s in range(1, n_snp):
            got = jnp.where(rank == s, lax.ppermute(x, "snp", [(0, s)]), got)
        return got

    def group_gather(x):
        core = rows_xor(x, 1)
        other = rows_xor(x, 2)
        return [x, core, other, rows_xor(other, 1)]

    def line_gather(x, hold):
        near = {k: rows_xor(x, k * GROUP) for k in range(1, far)}
        passed = hold(rows_xor(x, far * GROUP), list(near.values()))
        parts = {0: x, far: passed, **near}
        for k in range(1, far):
            parts[far + k] = rows_xor(passed, k * GROUP)
        return [parts[k] for k in range(lines)]

    def rows_sum(x):
        bit = 1
        while bit < n_rows:
            if bit * 2 < n_rows:
                parts = [x] + [rows_xor(x, bit * k) for k in (1, 2, 3)]
                x = (parts[0] + parts[1]) + (parts[2] + parts[3])
                bit *= 4
            else:
                x = x + rows_xor(x, bit)
                bit *= 2
        return x

    def snp_sum(x):
        bit = 1
        while bit < n_snp:
            x = x + snp_xor(x, bit)
            bit *= 2
        return x

    def per_device(genotypes, relationship):
        own = genotypes.shape[1]
        rank = lax.axis_index("rows")
        col = lax.axis_index("snp")
        q = rank % GROUP
        z = rank // GROUP
        place = jnp.stack([q, z - col * part]).astype(jnp.int32)

        called = genotypes >= 0
        dosage = jnp.where(called, genotypes, 0.0)
        stats = jnp.stack(
            [jnp.sum(dosage, axis=1), jnp.sum(called.astype(jnp.float32), axis=1)]
        )
        stats = rows_sum(stats)
        frequency = stats[0] / (2.0 * stats[1])
        scale_part = jnp.sum(2.0 * frequency * (1.0 - frequency))
        gt = lax.optimization_barrier(genotypes.T)
        centered = jnp.where(gt >= 0, gt - 2.0 * frequency[None, :], 0.0).astype(
            jnp.bfloat16
        )

        rel_own = from_first_snp(relationship[:, :PANEL], col)
        ids = rank * own + lax.broadcasted_iota(jnp.int32, rel_own.shape, 0)
        rel_own = rel_own + jnp.where(
            ids == lax.broadcasted_iota(jnp.int32, rel_own.shape, 1), RIDGE, 0.0
        )

        core, other = rows_xor(centered, 1), rows_xor(centered, 2)
        line = line_gather(centered, lambda x, near: after(x, rel_own, *near))
        line[-1] = after(line[-1], other)
        plane = [centered, core, other, rows_xor(other, 1)]
        first = select_order(line, z)[0]
        member = after((z ^ (col * part)).astype(jnp.int32).reshape(1), first)[0]
        ordered = select_order(line, member)
        groups = [ordered[bits * part : (bits + 1) * part] for bits in range(n_snp)]
        rel_line = line_gather(after(rel_own, line[-1]), lambda x, near: x)

        leaving = [gram_products(plane, groups[b], None, []) for b in range(1, n_snp)]

        head = [first, rows_xor(first, 1)]
        head.append(after(rows_xor(first, 2), *rel_line[1 : far + 1], *leaving))
        head.append(rows_xor(head[2], 1))
        (rows,) = head_products(place, [[first]], head, [])
        rows = jnp.concatenate(
            [rows, jnp.broadcast_to(scale_part.reshape(1, 1), (SUB, PANEL))], axis=0
        )
        total = snp_sum(rows)
        inverse = 1.0 / total[own, 0]
        total = total[:own] * inverse + select_order(rel_line, z)[0]
        sides = head_products(place, groups, head, [rows])
        total = after(total, *sides[1:])
        side_got = [snp_xor(sides[bits], bits) for bits in range(1, n_snp)]

        (lead,) = head_products(place, [[centered]], head, [total])
        diagonal = [total, rows_xor(total, 1)]
        diagonal.append(after(rows_xor(total, 2), lead))
        diagonal.append(rows_xor(diagonal[2], 1))

        gram_got = [
            snp_xor(after(leaving[b - 1], *side_got), b) for b in range(1, n_snp)
        ]
        pieces = gram_products(plane, groups[0], gram_got, [])
        moved = [pieces[0]] + [rows_xor(pieces[k], k) for k in range(1, GROUP)]

        inv, column, square = factor_step(place, diagonal, PANEL, side_got)
        inverses, below = [inv], [column]
        side = sides[0]
        for got in side_got:
            side = side + after(got, inverses[0])
        rel_side = select_order(rel_line, z ^ (col * part))[:part]
        side = jnp.concatenate(
            [
                rel_side[j] + side[j * own : (j + 1) * own] * inverse
                for j in range(part)
            ],
            axis=0,
        )
        sides = [side, rows_xor(side, 1), rows_xor(side, 2)]

        waits = [[], [side], [pieces[1]], []]
        for k in range(1, PANEL // BLOCK):
            inv, *more = factor_step(place, [square], PANEL - k * BLOCK, waits[k])
            inverses.append(inv)
            if more:
                column, square = more
                below.append(column)

        sides[2] = after(sides[2], inverses[2])
        sides.append(rows_xor(sides[2], 1))

        own_columns = rel_own + snp_sum(after(lead, pieces[1])) * inverse
        panel, weights = solve(own_columns, inverses, below)
        updated = final_update(
            place, inverse.reshape(1), relationship, weights, moved, sides
        )
        return updated, panel

    return per_device


def solution(mesh):
    return jax.shard_map(
        make(mesh.shape["rows"], mesh.shape["snp"]),
        mesh=mesh,
        in_specs=(P("snp", "rows"), P("rows", "snp")),
        out_specs=(P("rows", "snp"), P("rows", None)),
        check_vma=False,
    )
```

```python
import functools

import jax
import jax.numpy as jnp
from jax import lax
from jax.experimental import pallas as pl
from jax.experimental.pallas import tpu as pltpu
from jax.sharding import PartitionSpec as P

PANEL = 512
RIDGE = 0.25
GROUP = 4
BLOCK = 128
SUB = 8

VMEM = pl.BlockSpec(memory_space=pltpu.VMEM)
SMEM = pl.BlockSpec(memory_space=pltpu.SMEM)
ANYWHERE = pl.BlockSpec(memory_space=pl.ANY)


def precise(a, b, contract):
    return lax.dot_general(
        a,
        b,
        (((1,), (contract,)), ((), ())),
        precision=lax.Precision.HIGHEST,
        preferred_element_type=jnp.float32,
    )


def times(a, b):
    return lax.dot_general(
        a, b, (((1,), (1,)), ((), ())), preferred_element_type=jnp.float32
    )


def split(x):
    high = x.astype(jnp.bfloat16)
    return high, (x - high.astype(jnp.float32)).astype(jnp.bfloat16)


def cost(flops):
    return pl.CostEstimate(flops=flops, bytes_accessed=131072, transcendentals=0)


def room(*arrays):
    total = sum(x.size * x.dtype.itemsize for x in arrays)
    return pltpu.CompilerParams(vmem_limit_bytes=total * 3 // 2 + 3 * 2**20)


def f32(*shape):
    return jax.ShapeDtypeStruct(shape, jnp.float32)


def invert_factor(work):
    lane = lax.broadcasted_iota(jnp.int32, (SUB, BLOCK), 1)
    for g in range(BLOCK // SUB):
        at = g * SUB
        own = work[at : at + SUB, :]
        inside = (lane >= at) & (lane < at + SUB)
        rows = [jnp.broadcast_to(own[u : u + 1, :], (SUB, BLOCK)) for u in range(SUB)]
        e = [
            [
                jnp.broadcast_to(rows[t][:, at + u : at + u + 1], (SUB, BLOCK))
                for t in range(u + 1)
            ]
            for u in range(SUB)
        ]
        rows = [
            jnp.where(inside, jnp.where(lane == at + u, 1.0, 0.0), rows[u])
            for u in range(SUB)
        ]
        low = [[None] * SUB for _ in range(SUB)]
        scale = []
        for t in range(SUB):
            r = lax.rsqrt(e[t][t])
            scale.append(r)
            for u in range(t + 1, SUB):
                low[u][t] = e[u][t] * r
            for u in range(t + 1, SUB):
                for v in range(t + 1, u + 1):
                    e[u][v] = e[u][v] - low[u][t] * low[v][t]
            rows[t] = rows[t] * r
            for u in range(t + 1, SUB):
                rows[u] = rows[u] - low[u][t] * rows[t]
        for below in range(g + 1, BLOCK // SUB):
            base = below * SUB
            rest = work[base : base + SUB, :]
            c = [
                jnp.broadcast_to(rest[:, at + t : at + t + 1], (SUB, BLOCK))
                for t in range(SUB)
            ]
            rest = jnp.where(inside, 0.0, rest)
            for t in range(SUB):
                c[t] = c[t] * scale[t]
                for s in range(t + 1, SUB):
                    c[s] = c[s] - low[s][t] * c[t]
                rest = rest - c[t] * rows[t]
            work[base : base + SUB, :] = rest
        for t in range(SUB):
            work[at + t : at + t + 1, :] = rows[t][0:1, :]


def in_order(place, blocks, out):
    rows = blocks[0].shape[0]
    for k in range(GROUP):
        start = pl.multiple_of((place[0] ^ k) * rows, 16)
        out[pl.ds(start, rows), :] = blocks[k][...]


def factor_step_kernel(size, n_in, *refs):
    place, squares = refs[0], refs[1 : 1 + n_in]
    if size > BLOCK:
        inverse, column, rest, work = refs[-4:]
    else:
        inverse, work = refs[-2:]
    if n_in == 1:
        square = squares[0]
    else:
        square = rest_in = refs[-5]
        in_order(place, squares, rest_in)
    work[...] = square[:BLOCK, :BLOCK]
    invert_factor(work)
    i = lax.broadcasted_iota(jnp.int32, (BLOCK, BLOCK), 0)
    j = lax.broadcasted_iota(jnp.int32, (BLOCK, BLOCK), 1)
    value = jnp.where(j <= i, work[...], 0.0)
    inverse[...] = value
    if size > BLOCK:
        below = precise(square[BLOCK:size, :BLOCK], value, 1)
        column[...] = below
        for n in range(size // BLOCK - 1):
            cut = slice(n * BLOCK, size - BLOCK)
            across = slice(n * BLOCK, (n + 1) * BLOCK)
            rest[cut, across] = square[
                (n + 1) * BLOCK : size, (n + 1) * BLOCK : (n + 2) * BLOCK
            ] - precise(below[n * BLOCK :, :], below[across, :], 1)


def factor_step(place, squares, size, waits):
    left = size - BLOCK
    out_shape = [f32(BLOCK, BLOCK)]
    scratch = [pltpu.VMEM((BLOCK, BLOCK), jnp.float32)]
    if left:
        out_shape += [f32(left, BLOCK), f32(left, left)]
    n_in = len(squares)
    kernel = functools.partial(factor_step_kernel, size, n_in)
    if n_in > 1:

        def kernel(*refs):
            *others, work, whole = refs
            outs = 3 if left else 1
            return factor_step_kernel(
                size, n_in, *others[:-outs], whole, *others[-outs:], work
            )

        scratch.append(pltpu.VMEM((GROUP * squares[0].shape[0], size), jnp.float32))
    return pl.pallas_call(
        kernel,
        out_shape=out_shape,
        in_specs=[SMEM] + [VMEM] * n_in + [ANYWHERE] * len(waits),
        out_specs=[VMEM] * len(out_shape),
        scratch_shapes=scratch,
        compiler_params=room(*out_shape, f32(2 * size, size), *squares),
        cost_estimate=cost(6_000_000_000),
    )(place, *squares, *waits)


def solve_kernel(blocks, n_lead, rel, scale, *refs):
    lead, refs = refs[:n_lead], refs[n_lead:]
    inverses, below = refs[:blocks], refs[blocks : 2 * blocks - 1]
    panel, weights = refs[-2:]
    found = []
    for k in range(blocks):
        across = slice(k * BLOCK, (k + 1) * BLOCK)
        total = lead[0][:, across]
        for x in lead[1:]:
            total = total + x[:, across]
        total = rel[:, across] + total * scale[0:1, :]
        for j in range(k):
            start = (k - j - 1) * BLOCK
            total = total - precise(found[j], below[j][start : start + BLOCK, :], 1)
        found.append(precise(total, inverses[k][...], 1))
        panel[:, k * BLOCK : (k + 1) * BLOCK] = found[k]
    for k in reversed(range(blocks)):
        total = found[k]
        for j in range(k + 1, blocks):
            start = (j - k - 1) * BLOCK
            total = total - precise(found[j], below[k][start : start + BLOCK, :], 0)
        found[k] = precise(total, inverses[k][...], 0)
        weights[:, k * BLOCK : (k + 1) * BLOCK] = found[k]


def solve(rel, scale, lead, inverses, below):
    own = rel.shape[0]
    return pl.pallas_call(
        functools.partial(solve_kernel, len(inverses), len(lead)),
        out_shape=[f32(own, PANEL), f32(own, PANEL)],
        in_specs=[VMEM] * (1 + len(lead) + 2 * len(inverses)),
        out_specs=[VMEM, VMEM],
        compiler_params=room(rel, rel, rel, *lead, *inverses, *below),
        cost_estimate=cost(4 * own * PANEL * PANEL),
    )(rel, scale, *lead, *inverses, *below)


def head_kernel(n_left, sizes, place, *refs):
    left, head = refs[:n_left], refs[n_left : n_left + GROUP]
    outs, order = refs[-1 - len(sizes) : -1], refs[-1]
    own = head[0].shape[0]
    in_order(place, head, order)
    at = 0
    for out, count in zip(outs, sizes):
        for n in range(count):
            out[n * own : (n + 1) * own, :] = times(left[at][...], order[:PANEL, :])
            at += 1


def message_kernel(place, scale, first, *refs):
    head, out, order = refs[:GROUP], refs[-2], refs[-1]
    own = first.shape[0]
    in_order(place, head, order)
    out[:own, :] = times(first[...], order[:PANEL, :])
    out[own:, :] = jnp.full((SUB, PANEL), scale[0], jnp.float32)


def message(place, scale, first, head):
    own, depth = first.shape
    return pl.pallas_call(
        message_kernel,
        out_shape=f32(own + SUB, PANEL),
        in_specs=[SMEM, SMEM] + [VMEM] * (1 + GROUP),
        out_specs=VMEM,
        scratch_shapes=[pltpu.VMEM((GROUP * own, depth), first.dtype)],
        compiler_params=room(first, *head, *head, f32(own, PANEL)),
        cost_estimate=cost(2 * own * PANEL * depth),
    )(place, scale, first, *head)


def total_kernel(*refs):
    parts, (rel, total, inverse) = refs[:-3], refs[-3:]
    own = total.shape[0]
    value = parts[0][...]
    for x in parts[1:]:
        value = value + x[...]
    scale = 1.0 / value[own : own + 1, :]
    total[...] = rel[...] + value[:own, :] * scale
    inverse[...] = jnp.broadcast_to(scale[:, :BLOCK], (SUB, BLOCK))


def total_rows(parts, rel):
    return pl.pallas_call(
        total_kernel,
        out_shape=[f32(*rel.shape), f32(SUB, BLOCK)],
        in_specs=[VMEM] * (len(parts) + 1),
        out_specs=[VMEM] * 2,
        compiler_params=room(*parts, rel, rel),
        cost_estimate=cost(1_000_000),
    )(*parts, rel)


def side_kernel(n_parts, n_rel, scale, *refs):
    parts, rel, out = refs[:n_parts], refs[n_parts : n_parts + n_rel], refs[-1]
    own = rel[0].shape[0]
    factor = scale[0:1, 0:1]
    for n in range(n_rel):
        cut = slice(n * own, (n + 1) * own)
        value = parts[0][cut, :]
        for x in parts[1:]:
            value = value + x[cut, :]
        out[cut, :] = rel[n][...] + value * factor


def side_rows(scale, parts, rel, waits):
    return pl.pallas_call(
        functools.partial(side_kernel, len(parts), len(rel)),
        out_shape=f32(*parts[0].shape),
        in_specs=[VMEM] * (1 + len(parts) + len(rel)) + [ANYWHERE] * len(waits),
        out_specs=VMEM,
        compiler_params=room(*parts, *rel, parts[0]),
        cost_estimate=cost(1_000_000),
    )(scale, *parts, *rel, *waits)


def head_products(place, groups, head, waits):
    own = head[0].shape[0]
    left = [x for group in groups for x in group]
    sizes = [len(group) for group in groups]
    return pl.pallas_call(
        functools.partial(head_kernel, len(left), sizes),
        out_shape=[f32(n * own, PANEL) for n in sizes],
        in_specs=[SMEM] + [VMEM] * (len(left) + GROUP) + [ANYWHERE] * len(waits),
        out_specs=[VMEM] * len(sizes),
        scratch_shapes=[pltpu.VMEM((GROUP * own, head[0].shape[1]), head[0].dtype)],
        compiler_params=room(*left, *head, *head, f32(len(left) * own, PANEL)),
        cost_estimate=cost(2 * len(left) * own * PANEL * head[0].shape[1]),
    )(place, *left, *head, *waits)


def gram_kernel(n_cols, n_more, *refs):
    plane, cols = refs[:GROUP], refs[GROUP : GROUP + n_cols]
    more = refs[GROUP + n_cols : GROUP + n_cols + n_more]
    outs = refs[-GROUP:]
    own = plane[0].shape[0]
    for k in range(GROUP):
        for j in range(n_cols):
            product = times(cols[j][...], plane[k][...])
            across = slice(j * own, (j + 1) * own)
            for x in more:
                product = product + x[across, k * own : (k + 1) * own]
            outs[k][:, across] = product.T


def gram_out_kernel(n_cols, *refs):
    plane, cols, out = refs[:GROUP], refs[GROUP : GROUP + n_cols], refs[-1]
    own = plane[0].shape[0]
    for k in range(GROUP):
        for j in range(n_cols):
            out[j * own : (j + 1) * own, k * own : (k + 1) * own] = times(
                cols[j][...], plane[k][...]
            )


def gram_products(plane, cols, more, waits):
    own, depth = plane[0].shape
    width = len(cols) * own
    if more is None:
        kernel = functools.partial(gram_out_kernel, len(cols))
        out_shape, out_specs, more = f32(width, GROUP * own), VMEM, []
    else:
        kernel = functools.partial(gram_kernel, len(cols), len(more))
        out_shape, out_specs = [f32(own, width)] * GROUP, [VMEM] * GROUP
    return pl.pallas_call(
        kernel,
        out_shape=out_shape,
        in_specs=[VMEM] * (GROUP + len(cols) + len(more))
        + [ANYWHERE] * len(waits),
        out_specs=out_specs,
        compiler_params=room(*plane, *cols, *more, f32(GROUP * own, width)),
        cost_estimate=cost(2 * GROUP * own * width * depth),
    )(*plane, *cols, *more, *waits)


def update_kernel(own, part, place, scale, rel, weights, *refs):
    pieces, sides = refs[:GROUP], refs[GROUP : 2 * GROUP]
    out, all_pieces, all_sides = refs[2 * GROUP :]
    in_order(place, pieces, all_pieces)
    in_order(place, sides, all_sides)
    i = lax.broadcasted_iota(jnp.int32, (own, own), 0)
    j = lax.broadcasted_iota(jnp.int32, (own, own), 1)
    ridge = jnp.where(i == j, RIDGE, 0.0)
    high, low = split(weights[...])
    width = part * own
    for m in range(GROUP):
        side_high, side_low = split(all_sides[m * width : (m + 1) * width, :])
        product = times(high, side_low) + times(low, side_high)
        product = product + times(high, side_high)
        for n in range(part):
            at = (n * GROUP + m) * own
            cut = slice(n * own, (n + 1) * own)
            here = (place[0] == m) & (place[1] == n)
            value = rel[:, at : at + own] - product[:, cut]
            value = value + all_pieces[m * own : (m + 1) * own, cut] * scale[0:1, 0:1]
            out[:, at : at + own] = value + ridge * jnp.where(here, 1.0, 0.0)


def final_update(place, scale, rel, weights, pieces, sides):
    own, width = rel.shape
    part = width // (GROUP * own)
    return pl.pallas_call(
        functools.partial(update_kernel, own, part),
        out_shape=f32(own, width),
        in_specs=[SMEM] + [VMEM] * (3 + 2 * GROUP),
        out_specs=VMEM,
        scratch_shapes=[
            pltpu.VMEM((GROUP * own, part * own), jnp.float32),
            pltpu.VMEM((width, PANEL), jnp.float32),
        ],
        compiler_params=room(rel, rel, weights, *pieces, *pieces, *sides, *sides),
        cost_estimate=cost(2 * own * width * PANEL),
    )(place, scale, rel, weights, *pieces, *sides)


def nothing(*refs):
    pass


def after(x, *done):
    return pl.pallas_call(
        nothing,
        out_shape=jax.ShapeDtypeStruct(x.shape, x.dtype),
        in_specs=[ANYWHERE] * (1 + len(done)),
        out_specs=ANYWHERE,
        input_output_aliases={0: 0},
        compiler_params=pltpu.CompilerParams(vmem_limit_bytes=2**20),
    )(x, *done)


def select_order(blocks, member):
    bit = 1
    while bit < len(blocks):
        swap = (member & bit) != 0
        blocks = [
            jnp.where(swap, blocks[k ^ bit], blocks[k]) for k in range(len(blocks))
        ]
        bit *= 2
    return blocks


def make(n_rows, n_snp):
    lines = n_rows // GROUP
    part = lines // n_snp
    far = lines // 2

    def rows_xor(x, bits):
        return lax.ppermute(x, "rows", [(r, r ^ bits) for r in range(n_rows)])

    def snp_xor(x, bits):
        return lax.ppermute(x, "snp", [(s, s ^ bits) for s in range(n_snp)])

    def from_first_snp(x, rank):
        got = x
        for s in range(1, n_snp):
            got = jnp.where(rank == s, lax.ppermute(x, "snp", [(0, s)]), got)
        return got

    def group_gather(x):
        core = rows_xor(x, 1)
        other = rows_xor(x, 2)
        return [x, core, other, rows_xor(other, 1)]

    def line_gather(x, hold):
        near = {k: rows_xor(x, k * GROUP) for k in range(1, far)}
        passed = hold(rows_xor(x, far * GROUP), list(near.values()))
        parts = {0: x, far: passed, **near}
        for k in range(1, far):
            parts[far + k] = rows_xor(passed, k * GROUP)
        return [parts[k] for k in range(lines)]

    def rows_sum(x):
        bit = 1
        while bit < n_rows:
            if bit * 2 < n_rows:
                parts = [x] + [rows_xor(x, bit * k) for k in (1, 2, 3)]
                x = (parts[0] + parts[1]) + (parts[2] + parts[3])
                bit *= 4
            else:
                x = x + rows_xor(x, bit)
                bit *= 2
        return x

    def snp_sum(x):
        bit = 1
        while bit < n_snp:
            x = x + snp_xor(x, bit)
            bit *= 2
        return x

    def per_device(genotypes, relationship):
        own = genotypes.shape[1]
        rank = lax.axis_index("rows")
        col = lax.axis_index("snp")
        q = rank % GROUP
        z = rank // GROUP
        place = jnp.stack([q, z - col * part]).astype(jnp.int32)

        called = genotypes >= 0
        dosage = jnp.where(called, genotypes, 0.0)
        stats = jnp.stack(
            [jnp.sum(dosage, axis=1), jnp.sum(called.astype(jnp.float32), axis=1)]
        )
        stats = rows_sum(stats)
        frequency = stats[0] / (2.0 * stats[1])
        scale_part = jnp.sum(2.0 * frequency * (1.0 - frequency))
        gt = lax.optimization_barrier(genotypes.T)
        centered = jnp.where(gt >= 0, gt - 2.0 * frequency[None, :], 0.0).astype(
            jnp.bfloat16
        )

        rel_own = from_first_snp(relationship[:, :PANEL], col)
        ids = rank * own + lax.broadcasted_iota(jnp.int32, rel_own.shape, 0)
        rel_own = rel_own + jnp.where(
            ids == lax.broadcasted_iota(jnp.int32, rel_own.shape, 1), RIDGE, 0.0
        )

        core, other = rows_xor(centered, 1), rows_xor(centered, 2)
        line = line_gather(centered, lambda x, near: after(x, rel_own, *near))
        line[-1] = after(line[-1], other)
        plane = [centered, core, other, rows_xor(other, 1)]
        first = select_order(line, z)[0]
        member = after((z ^ (col * part)).astype(jnp.int32).reshape(1), first)[0]
        ordered = select_order(line, member)
        groups = [ordered[bits * part : (bits + 1) * part] for bits in range(n_snp)]
        rel_line = line_gather(after(rel_own, line[-1]), lambda x, near: x)

        leaving = [gram_products(plane, groups[b], None, []) for b in range(1, n_snp)]

        head = [first, rows_xor(first, 1)]
        head.append(after(rows_xor(first, 2), *rel_line[1 : far + 1], *leaving))
        head.append(rows_xor(head[2], 1))
        rows = message(place, scale_part.reshape(1), first, head)
        rows_got = [snp_xor(rows, bits) for bits in range(1, n_snp)]
        sides = head_products(place, groups, head, [rows])
        total, scale = total_rows([rows] + rows_got, select_order(rel_line, z)[0])
        sides = [sides[0]] + [after(x, total) for x in sides[1:]]
        side_got = [snp_xor(sides[bits], bits) for bits in range(1, n_snp)]
        total = after(total, *sides[1:])

        (lead,) = head_products(place, [[centered]], head, [total])
        diagonal = [total, rows_xor(total, 1)]
        diagonal.append(after(rows_xor(total, 2), lead))
        diagonal.append(rows_xor(diagonal[2], 1))

        gram_got = [
            snp_xor(after(leaving[b - 1], *side_got), b) for b in range(1, n_snp)
        ]
        pieces = gram_products(plane, groups[0], gram_got, [])
        moved = [pieces[0]] + [rows_xor(pieces[k], k) for k in range(1, GROUP)]

        inv, column, square = factor_step(place, diagonal, PANEL, side_got)
        inverses, below = [inv], [column]
        rel_side = select_order(rel_line, z ^ (col * part))[:part]
        side = side_rows(scale, [sides[0]] + side_got, rel_side, [inverses[0]])
        sides = [side, rows_xor(side, 1), rows_xor(side, 2)]

        lead = after(lead, pieces[1])
        leads = [lead] + [snp_xor(lead, bits) for bits in range(1, n_snp)]
        waits = [[], [side], [pieces[1], sides[1]], leads[1:] + [moved[2]]]
        for k in range(1, PANEL // BLOCK):
            inv, *more = factor_step(place, [square], PANEL - k * BLOCK, waits[k])
            inverses.append(inv)
            if more:
                column, square = more
                below.append(column)

        sides[2] = after(sides[2], inverses[2])
        sides.append(rows_xor(sides[2], 1))

        panel, weights = solve(rel_own, scale, leads, inverses, below)
        updated = final_update(place, scale, relationship, weights, moved, sides)
        return updated, panel

    return per_device


def solution(mesh):
    return jax.shard_map(
        make(mesh.shape["rows"], mesh.shape["snp"]),
        mesh=mesh,
        in_specs=(P("snp", "rows"), P("rows", "snp")),
        out_specs=(P("rows", "snp"), P("rows", None)),
        check_vma=False,
    )
```

```python
import functools

import jax
import jax.numpy as jnp
from jax import lax
from jax.experimental import pallas as pl
from jax.experimental.pallas import tpu as pltpu
from jax.sharding import PartitionSpec as P

PANEL = 512
RIDGE = 0.25
GROUP = 4
BLOCK = 128
SUB = 8

VMEM = pl.BlockSpec(memory_space=pltpu.VMEM)
SMEM = pl.BlockSpec(memory_space=pltpu.SMEM)
ANYWHERE = pl.BlockSpec(memory_space=pl.ANY)


def precise(a, b, contract):
    return lax.dot_general(
        a,
        b,
        (((1,), (contract,)), ((), ())),
        precision=lax.Precision.HIGHEST,
        preferred_element_type=jnp.float32,
    )


def times(a, b):
    return lax.dot_general(
        a, b, (((1,), (1,)), ((), ())), preferred_element_type=jnp.float32
    )


def split(x):
    high = x.astype(jnp.bfloat16)
    return high, (x - high.astype(jnp.float32)).astype(jnp.bfloat16)


def cost(flops):
    return pl.CostEstimate(flops=flops, bytes_accessed=131072, transcendentals=0)


def room(*arrays):
    total = sum(x.size * x.dtype.itemsize for x in arrays)
    return pltpu.CompilerParams(vmem_limit_bytes=total * 3 // 2 + 3 * 2**20)


def f32(*shape):
    return jax.ShapeDtypeStruct(shape, jnp.float32)


def invert_factor(work):
    lane = lax.broadcasted_iota(jnp.int32, (SUB, BLOCK), 1)
    for g in range(BLOCK // SUB):
        at = g * SUB
        own = work[at : at + SUB, :]
        inside = (lane >= at) & (lane < at + SUB)
        rows = [jnp.broadcast_to(own[u : u + 1, :], (SUB, BLOCK)) for u in range(SUB)]
        e = [
            [
                jnp.broadcast_to(rows[t][:, at + u : at + u + 1], (SUB, BLOCK))
                for t in range(u + 1)
            ]
            for u in range(SUB)
        ]
        rows = [
            jnp.where(inside, jnp.where(lane == at + u, 1.0, 0.0), rows[u])
            for u in range(SUB)
        ]
        low = [[None] * SUB for _ in range(SUB)]
        scale = []
        for t in range(SUB):
            r = lax.rsqrt(e[t][t])
            scale.append(r)
            for u in range(t + 1, SUB):
                low[u][t] = e[u][t] * r
            for u in range(t + 1, SUB):
                for v in range(t + 1, u + 1):
                    e[u][v] = e[u][v] - low[u][t] * low[v][t]
            rows[t] = rows[t] * r
            for u in range(t + 1, SUB):
                rows[u] = rows[u] - low[u][t] * rows[t]
        for below in range(g + 1, BLOCK // SUB):
            base = below * SUB
            rest = work[base : base + SUB, :]
            c = [
                jnp.broadcast_to(rest[:, at + t : at + t + 1], (SUB, BLOCK))
                for t in range(SUB)
            ]
            rest = jnp.where(inside, 0.0, rest)
            for t in range(SUB):
                c[t] = c[t] * scale[t]
                for s in range(t + 1, SUB):
                    c[s] = c[s] - low[s][t] * c[t]
                rest = rest - c[t] * rows[t]
            work[base : base + SUB, :] = rest
        for t in range(SUB):
            work[at + t : at + t + 1, :] = rows[t][0:1, :]


def in_order(place, blocks, out):
    rows = blocks[0].shape[0]
    for k in range(GROUP):
        start = pl.multiple_of((place[0] ^ k) * rows, 16)
        out[pl.ds(start, rows), :] = blocks[k][...]


def factor_step_kernel(size, n_in, *refs):
    place, squares = refs[0], refs[1 : 1 + n_in]
    if size > BLOCK:
        inverse, column, rest, work = refs[-4:]
    else:
        inverse, work = refs[-2:]
    if n_in == 1:
        square = squares[0]
    else:
        square = rest_in = refs[-5]
        in_order(place, squares, rest_in)
    work[...] = square[:BLOCK, :BLOCK]
    invert_factor(work)
    i = lax.broadcasted_iota(jnp.int32, (BLOCK, BLOCK), 0)
    j = lax.broadcasted_iota(jnp.int32, (BLOCK, BLOCK), 1)
    value = jnp.where(j <= i, work[...], 0.0)
    inverse[...] = value
    if size > BLOCK:
        below = precise(square[BLOCK:size, :BLOCK], value, 1)
        column[...] = below
        for n in range(size // BLOCK - 1):
            cut = slice(n * BLOCK, size - BLOCK)
            across = slice(n * BLOCK, (n + 1) * BLOCK)
            rest[cut, across] = square[
                (n + 1) * BLOCK : size, (n + 1) * BLOCK : (n + 2) * BLOCK
            ] - precise(below[n * BLOCK :, :], below[across, :], 1)


def factor_step(place, squares, size, waits):
    left = size - BLOCK
    out_shape = [f32(BLOCK, BLOCK)]
    scratch = [pltpu.VMEM((BLOCK, BLOCK), jnp.float32)]
    if left:
        out_shape += [f32(left, BLOCK), f32(left, left)]
    n_in = len(squares)
    kernel = functools.partial(factor_step_kernel, size, n_in)
    if n_in > 1:

        def kernel(*refs):
            *others, work, whole = refs
            outs = 3 if left else 1
            return factor_step_kernel(
                size, n_in, *others[:-outs], whole, *others[-outs:], work
            )

        scratch.append(pltpu.VMEM((GROUP * squares[0].shape[0], size), jnp.float32))
    return pl.pallas_call(
        kernel,
        out_shape=out_shape,
        in_specs=[SMEM] + [VMEM] * n_in + [ANYWHERE] * len(waits),
        out_specs=[VMEM] * len(out_shape),
        scratch_shapes=scratch,
        compiler_params=room(*out_shape, f32(2 * size, size), *squares),
        cost_estimate=cost(3_500_000_000),
    )(place, *squares, *waits)


def solve_kernel(blocks, n_lead, rel, scale, *refs):
    lead, refs = refs[:n_lead], refs[n_lead:]
    inverses, below = refs[:blocks], refs[blocks : 2 * blocks - 1]
    panel, weights = refs[-2:]
    found = []
    for k in range(blocks):
        across = slice(k * BLOCK, (k + 1) * BLOCK)
        total = lead[0][:, across]
        for x in lead[1:]:
            total = total + x[:, across]
        total = rel[:, across] + total * scale[0:1, :]
        for j in range(k):
            start = (k - j - 1) * BLOCK
            total = total - precise(found[j], below[j][start : start + BLOCK, :], 1)
        found.append(precise(total, inverses[k][...], 1))
        panel[:, k * BLOCK : (k + 1) * BLOCK] = found[k]
    for k in reversed(range(blocks)):
        total = found[k]
        for j in range(k + 1, blocks):
            start = (j - k - 1) * BLOCK
            total = total - precise(found[j], below[k][start : start + BLOCK, :], 0)
        found[k] = precise(total, inverses[k][...], 0)
        weights[:, k * BLOCK : (k + 1) * BLOCK] = found[k]


def solve(rel, scale, lead, inverses, below):
    own = rel.shape[0]
    return pl.pallas_call(
        functools.partial(solve_kernel, len(inverses), len(lead)),
        out_shape=[f32(own, PANEL), f32(own, PANEL)],
        in_specs=[VMEM] * (1 + len(lead) + 2 * len(inverses)),
        out_specs=[VMEM, VMEM],
        compiler_params=room(rel, rel, rel, *lead, *inverses, *below),
        cost_estimate=cost(4 * own * PANEL * PANEL),
    )(rel, scale, *lead, *inverses, *below)


def head_kernel(n_left, sizes, place, *refs):
    left, head = refs[:n_left], refs[n_left : n_left + GROUP]
    outs, order = refs[-1 - len(sizes) : -1], refs[-1]
    own = head[0].shape[0]
    in_order(place, head, order)
    at = 0
    for out, count in zip(outs, sizes):
        for n in range(count):
            out[n * own : (n + 1) * own, :] = times(left[at][...], order[:PANEL, :])
            at += 1


def message_kernel(place, scale, first, *refs):
    head, out, order = refs[:GROUP], refs[-2], refs[-1]
    own = first.shape[0]
    in_order(place, head, order)
    out[:own, :] = times(first[...], order[:PANEL, :])
    out[own:, :] = jnp.full((SUB, PANEL), scale[0], jnp.float32)


def message(place, scale, first, head):
    own, depth = first.shape
    return pl.pallas_call(
        message_kernel,
        out_shape=f32(own + SUB, PANEL),
        in_specs=[SMEM, SMEM] + [VMEM] * (1 + GROUP),
        out_specs=VMEM,
        scratch_shapes=[pltpu.VMEM((GROUP * own, depth), first.dtype)],
        compiler_params=room(first, *head, *head, f32(own, PANEL)),
        cost_estimate=cost(2 * own * PANEL * depth),
    )(place, scale, first, *head)


def total_kernel(*refs):
    parts, (rel, total, inverse) = refs[:-3], refs[-3:]
    own = total.shape[0]
    value = parts[0][...]
    for x in parts[1:]:
        value = value + x[...]
    scale = 1.0 / value[own : own + 1, :]
    total[...] = rel[...] + value[:own, :] * scale
    inverse[...] = jnp.broadcast_to(scale[:, :BLOCK], (SUB, BLOCK))


def total_rows(parts, rel):
    return pl.pallas_call(
        total_kernel,
        out_shape=[f32(*rel.shape), f32(SUB, BLOCK)],
        in_specs=[VMEM] * (len(parts) + 1),
        out_specs=[VMEM] * 2,
        compiler_params=room(*parts, rel, rel),
        cost_estimate=cost(1_000_000),
    )(*parts, rel)


def side_kernel(n_got, n_rel, scale, keep, *refs):
    rel, out = refs[-1 - n_rel : -1], refs[-1]
    got = refs[: -1 - n_rel]
    own = rel[0].shape[0]
    factor = scale[0:1, 0:1]
    each = n_rel // n_got
    for n in range(n_rel):
        cut = slice(n * own, (n + 1) * own)
        inside = slice((n % each) * own, (n % each + 1) * own)
        value = keep[cut, :]
        for x in got[n // each :: n_got]:
            value = value + x[inside, :]
        out[cut, :] = rel[n][...] + value * factor


def side_rows(scale, keep, n_got, got, rel, waits):
    count = len(got)

    def kernel(scale, keep, *refs):
        side_kernel(n_got, len(rel), scale, keep, *refs[: count + len(rel)], refs[-1])

    return pl.pallas_call(
        kernel,
        out_shape=f32(*keep.shape),
        in_specs=[VMEM] * (2 + count + len(rel)) + [ANYWHERE] * len(waits),
        out_specs=VMEM,
        compiler_params=room(keep, keep, *got, *rel),
        cost_estimate=cost(1_000_000),
    )(scale, keep, *got, *rel, *waits)


def head_products(place, groups, head, waits):
    own = head[0].shape[0]
    left = [x for group in groups for x in group]
    sizes = [len(group) for group in groups]
    return pl.pallas_call(
        functools.partial(head_kernel, len(left), sizes),
        out_shape=[f32(n * own, PANEL) for n in sizes],
        in_specs=[SMEM] + [VMEM] * (len(left) + GROUP) + [ANYWHERE] * len(waits),
        out_specs=[VMEM] * len(sizes),
        scratch_shapes=[pltpu.VMEM((GROUP * own, head[0].shape[1]), head[0].dtype)],
        compiler_params=room(*left, *head, *head, f32(len(left) * own, PANEL)),
        cost_estimate=cost(2 * len(left) * own * PANEL * head[0].shape[1]),
    )(place, *left, *head, *waits)


def gram_kernel(n_cols, n_more, *refs):
    plane, cols = refs[:GROUP], refs[GROUP : GROUP + n_cols]
    more = refs[GROUP + n_cols : GROUP + n_cols + n_more]
    outs = refs[-GROUP:]
    own = plane[0].shape[0]
    for k in range(GROUP):
        for j in range(n_cols):
            product = times(cols[j][...], plane[k][...])
            across = slice(j * own, (j + 1) * own)
            for x in more:
                product = product + x[across, k * own : (k + 1) * own]
            outs[k][:, across] = product.T


def gram_out_kernel(n_cols, *refs):
    plane, cols, out = refs[:GROUP], refs[GROUP : GROUP + n_cols], refs[-1]
    own = plane[0].shape[0]
    for k in range(GROUP):
        for j in range(n_cols):
            out[j * own : (j + 1) * own, k * own : (k + 1) * own] = times(
                cols[j][...], plane[k][...]
            )


def gram_products(plane, cols, more, waits):
    own, depth = plane[0].shape
    width = len(cols) * own
    if more is None:
        kernel = functools.partial(gram_out_kernel, len(cols))
        out_shape, out_specs, more = f32(width, GROUP * own), VMEM, []
    else:
        kernel = functools.partial(gram_kernel, len(cols), len(more))
        out_shape, out_specs = [f32(own, width)] * GROUP, [VMEM] * GROUP
    return pl.pallas_call(
        kernel,
        out_shape=out_shape,
        in_specs=[VMEM] * (GROUP + len(cols) + len(more))
        + [ANYWHERE] * len(waits),
        out_specs=out_specs,
        compiler_params=room(*plane, *cols, *more, f32(GROUP * own, width)),
        cost_estimate=cost(2 * GROUP * own * width * depth),
    )(*plane, *cols, *more, *waits)


def update_kernel(own, part, place, scale, rel, weights, *refs):
    pieces, sides = refs[:GROUP], refs[GROUP : 2 * GROUP]
    out, all_pieces, all_sides = refs[2 * GROUP :]
    in_order(place, pieces, all_pieces)
    in_order(place, sides, all_sides)
    i = lax.broadcasted_iota(jnp.int32, (own, own), 0)
    j = lax.broadcasted_iota(jnp.int32, (own, own), 1)
    ridge = jnp.where(i == j, RIDGE, 0.0)
    high, low = split(weights[...])
    width = part * own
    for m in range(GROUP):
        side_high, side_low = split(all_sides[m * width : (m + 1) * width, :])
        product = times(high, side_low) + times(low, side_high)
        product = product + times(high, side_high)
        for n in range(part):
            at = (n * GROUP + m) * own
            cut = slice(n * own, (n + 1) * own)
            here = (place[0] == m) & (place[1] == n)
            value = rel[:, at : at + own] - product[:, cut]
            value = value + all_pieces[m * own : (m + 1) * own, cut] * scale[0:1, 0:1]
            out[:, at : at + own] = value + ridge * jnp.where(here, 1.0, 0.0)


def final_update(place, scale, rel, weights, pieces, sides):
    own, width = rel.shape
    part = width // (GROUP * own)
    return pl.pallas_call(
        functools.partial(update_kernel, own, part),
        out_shape=f32(own, width),
        in_specs=[SMEM] + [VMEM] * (3 + 2 * GROUP),
        out_specs=VMEM,
        scratch_shapes=[
            pltpu.VMEM((GROUP * own, part * own), jnp.float32),
            pltpu.VMEM((width, PANEL), jnp.float32),
        ],
        compiler_params=room(rel, rel, weights, *pieces, *pieces, *sides, *sides),
        cost_estimate=cost(2 * own * width * PANEL),
    )(place, scale, rel, weights, *pieces, *sides)


def nothing(*refs):
    pass


def after(x, *done):
    return pl.pallas_call(
        nothing,
        out_shape=jax.ShapeDtypeStruct(x.shape, x.dtype),
        in_specs=[ANYWHERE] * (1 + len(done)),
        out_specs=ANYWHERE,
        input_output_aliases={0: 0},
        compiler_params=pltpu.CompilerParams(vmem_limit_bytes=2**20),
    )(x, *done)


def select_order(blocks, member):
    bit = 1
    while bit < len(blocks):
        swap = (member & bit) != 0
        blocks = [
            jnp.where(swap, blocks[k ^ bit], blocks[k]) for k in range(len(blocks))
        ]
        bit *= 2
    return blocks


def make(n_rows, n_snp):
    lines = n_rows // GROUP
    part = lines // n_snp
    far = lines // 2

    def rows_xor(x, bits):
        return lax.ppermute(x, "rows", [(r, r ^ bits) for r in range(n_rows)])

    def snp_xor(x, bits):
        return lax.ppermute(x, "snp", [(s, s ^ bits) for s in range(n_snp)])

    def from_first_snp(x, rank):
        got = x
        for s in range(1, n_snp):
            got = jnp.where(rank == s, lax.ppermute(x, "snp", [(0, s)]), got)
        return got

    def group_gather(x):
        core = rows_xor(x, 1)
        other = rows_xor(x, 2)
        return [x, core, other, rows_xor(other, 1)]

    def line_gather(x, hold):
        near = {k: rows_xor(x, k * GROUP) for k in range(1, far)}
        passed = hold(rows_xor(x, far * GROUP), list(near.values()))
        parts = {0: x, far: passed, **near}
        for k in range(1, far):
            parts[far + k] = rows_xor(passed, k * GROUP)
        return [parts[k] for k in range(lines)]

    def rows_sum(x):
        bit = 1
        while bit < n_rows:
            if bit * 2 < n_rows:
                parts = [x] + [rows_xor(x, bit * k) for k in (1, 2, 3)]
                x = (parts[0] + parts[1]) + (parts[2] + parts[3])
                bit *= 4
            else:
                x = x + rows_xor(x, bit)
                bit *= 2
        return x

    def snp_sum(x):
        bit = 1
        while bit < n_snp:
            x = x + snp_xor(x, bit)
            bit *= 2
        return x

    def per_device(genotypes, relationship):
        own = genotypes.shape[1]
        rank = lax.axis_index("rows")
        col = lax.axis_index("snp")
        q = rank % GROUP
        z = rank // GROUP
        place = jnp.stack([q, z - col * part]).astype(jnp.int32)

        called = genotypes >= 0
        dosage = jnp.where(called, genotypes, 0.0)
        stats = jnp.stack(
            [jnp.sum(dosage, axis=1), jnp.sum(called.astype(jnp.float32), axis=1)]
        )
        stats = rows_sum(stats)
        frequency = stats[0] / (2.0 * stats[1])
        scale_part = jnp.sum(2.0 * frequency * (1.0 - frequency))
        gt = lax.optimization_barrier(genotypes.T)
        centered = jnp.where(gt >= 0, gt - 2.0 * frequency[None, :], 0.0).astype(
            jnp.bfloat16
        )

        rel_own = from_first_snp(relationship[:, :PANEL], col)
        ids = rank * own + lax.broadcasted_iota(jnp.int32, rel_own.shape, 0)
        rel_own = rel_own + jnp.where(
            ids == lax.broadcasted_iota(jnp.int32, rel_own.shape, 1), RIDGE, 0.0
        )

        core, other = rows_xor(centered, 1), rows_xor(centered, 2)
        line = line_gather(centered, lambda x, near: after(x, rel_own, *near))
        line[-1] = after(line[-1], other)
        plane = [centered, core, other, rows_xor(other, 1)]
        first = select_order(line, z)[0]
        member = after((z ^ (col * part)).astype(jnp.int32).reshape(1), first)[0]
        ordered = select_order(line, member)
        groups = [ordered[bits * part : (bits + 1) * part] for bits in range(n_snp)]
        rel_line = line_gather(after(rel_own, line[-1]), lambda x, near: x)

        leaving = [gram_products(plane, groups[b], None, []) for b in range(1, n_snp)]

        head = [first, rows_xor(first, 1)]
        head.append(after(rows_xor(first, 2), *rel_line[1 : far + 1], *leaving))
        head.append(rows_xor(head[2], 1))
        rows = message(place, scale_part.reshape(1), first, head)
        rows_got = [snp_xor(rows, bits) for bits in range(1, n_snp)]
        halves = 2 if part % 2 == 0 else 1
        split_groups = [
            groups[b][h * part // halves : (h + 1) * part // halves]
            for b in range(1, n_snp)
            for h in range(halves)
        ]
        keep, *out = head_products(place, groups[:1] + split_groups, head, [rows])
        rel_line[-1] = after(rel_line[-1], out[0])
        total, scale = total_rows([rows] + rows_got, select_order(rel_line, z)[0])
        out = [after(x, total) for x in out]
        side_got = [snp_xor(x, n // halves + 1) for n, x in enumerate(out)]
        early = side_got[::halves]
        total = after(total, *out)

        (lead,) = head_products(place, [[centered]], head, [total])
        diagonal = [total, rows_xor(total, 1)]
        diagonal.append(after(rows_xor(total, 2), lead, *early))
        diagonal.append(rows_xor(diagonal[2], 1))

        gram_got = [
            snp_xor(after(leaving[b - 1], *early), b) for b in range(1, n_snp)
        ]
        pieces = gram_products(plane, groups[0], gram_got, [])
        moved = [pieces[0]] + [rows_xor(pieces[k], k) for k in range(1, GROUP)]

        inv, column, square = factor_step(place, diagonal, PANEL, [])
        inverses, below = [inv], [column]
        rel_side = select_order(rel_line, z ^ (col * part))[:part]
        side = side_rows(scale, keep, halves, side_got, rel_side, [inverses[0]])
        sides = [side, rows_xor(side, 1), rows_xor(side, 2)]

        lead = after(lead, pieces[1])
        leads = [lead] + [snp_xor(lead, bits) for bits in range(1, n_snp)]
        waits = [[], [side], [pieces[1], sides[1]], leads[1:] + [moved[2]]]
        for k in range(1, PANEL // BLOCK):
            inv, *more = factor_step(place, [square], PANEL - k * BLOCK, waits[k])
            inverses.append(inv)
            if more:
                column, square = more
                below.append(column)

        sides[2] = after(sides[2], inverses[2])
        sides.append(rows_xor(sides[2], 1))

        panel, weights = solve(rel_own, scale, leads, inverses, below)
        updated = final_update(place, scale, relationship, weights, moved, sides)
        return updated, panel

    return per_device


def solution(mesh):
    return jax.shard_map(
        make(mesh.shape["rows"], mesh.shape["snp"]),
        mesh=mesh,
        in_specs=(P("snp", "rows"), P("rows", "snp")),
        out_specs=(P("rows", "snp"), P("rows", None)),
        check_vma=False,
    )
```

```python
import functools

import jax
import jax.numpy as jnp
from jax import lax
from jax.experimental import pallas as pl
from jax.experimental.pallas import tpu as pltpu
from jax.sharding import PartitionSpec as P

PANEL = 512
RIDGE = 0.25
GROUP = 4
BLOCK = 128
SUB = 8

VMEM = pl.BlockSpec(memory_space=pltpu.VMEM)
SMEM = pl.BlockSpec(memory_space=pltpu.SMEM)
ANYWHERE = pl.BlockSpec(memory_space=pl.ANY)


def precise(a, b, contract):
    return lax.dot_general(
        a,
        b,
        (((1,), (contract,)), ((), ())),
        precision=lax.Precision.HIGHEST,
        preferred_element_type=jnp.float32,
    )


def times(a, b):
    return lax.dot_general(
        a, b, (((1,), (1,)), ((), ())), preferred_element_type=jnp.float32
    )


def split(x):
    high = x.astype(jnp.bfloat16)
    return high, (x - high.astype(jnp.float32)).astype(jnp.bfloat16)


def cost(flops):
    return pl.CostEstimate(flops=flops, bytes_accessed=131072, transcendentals=0)


def room(*arrays):
    total = sum(x.size * x.dtype.itemsize for x in arrays)
    return pltpu.CompilerParams(vmem_limit_bytes=total * 3 // 2 + 3 * 2**20)


def f32(*shape):
    return jax.ShapeDtypeStruct(shape, jnp.float32)


def invert_factor(work):
    lane = lax.broadcasted_iota(jnp.int32, (SUB, BLOCK), 1)
    for g in range(BLOCK // SUB):
        at = g * SUB
        own = work[at : at + SUB, :]
        inside = (lane >= at) & (lane < at + SUB)
        rows = [jnp.broadcast_to(own[u : u + 1, :], (SUB, BLOCK)) for u in range(SUB)]
        e = [
            [
                jnp.broadcast_to(rows[t][:, at + u : at + u + 1], (SUB, BLOCK))
                for t in range(u + 1)
            ]
            for u in range(SUB)
        ]
        rows = [
            jnp.where(inside, jnp.where(lane == at + u, 1.0, 0.0), rows[u])
            for u in range(SUB)
        ]
        low = [[None] * SUB for _ in range(SUB)]
        scale = []
        for t in range(SUB):
            r = lax.rsqrt(e[t][t])
            scale.append(r)
            for u in range(t + 1, SUB):
                low[u][t] = e[u][t] * r
            for u in range(t + 1, SUB):
                for v in range(t + 1, u + 1):
                    e[u][v] = e[u][v] - low[u][t] * low[v][t]
            rows[t] = rows[t] * r
            for u in range(t + 1, SUB):
                rows[u] = rows[u] - low[u][t] * rows[t]
        for below in range(g + 1, BLOCK // SUB):
            base = below * SUB
            rest = work[base : base + SUB, :]
            c = [
                jnp.broadcast_to(rest[:, at + t : at + t + 1], (SUB, BLOCK))
                for t in range(SUB)
            ]
            rest = jnp.where(inside, 0.0, rest)
            for t in range(SUB):
                c[t] = c[t] * scale[t]
                for s in range(t + 1, SUB):
                    c[s] = c[s] - low[s][t] * c[t]
                rest = rest - c[t] * rows[t]
            work[base : base + SUB, :] = rest
        for t in range(SUB):
            work[at + t : at + t + 1, :] = rows[t][0:1, :]


def in_order(place, blocks, out):
    rows = blocks[0].shape[0]
    for k in range(GROUP):
        start = pl.multiple_of((place[0] ^ k) * rows, 16)
        out[pl.ds(start, rows), :] = blocks[k][...]


def factor_step_kernel(size, n_in, *refs):
    place, squares = refs[0], refs[1 : 1 + n_in]
    if size > BLOCK:
        inverse, column, rest, work = refs[-4:]
    else:
        inverse, work = refs[-2:]
    if n_in == 1:
        square = squares[0]
    else:
        square = rest_in = refs[-5]
        in_order(place, squares, rest_in)
    work[...] = square[:BLOCK, :BLOCK]
    invert_factor(work)
    i = lax.broadcasted_iota(jnp.int32, (BLOCK, BLOCK), 0)
    j = lax.broadcasted_iota(jnp.int32, (BLOCK, BLOCK), 1)
    value = jnp.where(j <= i, work[...], 0.0)
    inverse[...] = value
    if size > BLOCK:
        below = precise(square[BLOCK:size, :BLOCK], value, 1)
        column[...] = below
        for n in range(size // BLOCK - 1):
            cut = slice(n * BLOCK, size - BLOCK)
            across = slice(n * BLOCK, (n + 1) * BLOCK)
            rest[cut, across] = square[
                (n + 1) * BLOCK : size, (n + 1) * BLOCK : (n + 2) * BLOCK
            ] - precise(below[n * BLOCK :, :], below[across, :], 1)


def factor_step(place, squares, size, waits):
    left = size - BLOCK
    out_shape = [f32(BLOCK, BLOCK)]
    scratch = [pltpu.VMEM((BLOCK, BLOCK), jnp.float32)]
    if left:
        out_shape += [f32(left, BLOCK), f32(left, left)]
    n_in = len(squares)
    kernel = functools.partial(factor_step_kernel, size, n_in)
    if n_in > 1:

        def kernel(*refs):
            *others, work, whole = refs
            outs = 3 if left else 1
            return factor_step_kernel(
                size, n_in, *others[:-outs], whole, *others[-outs:], work
            )

        scratch.append(pltpu.VMEM((GROUP * squares[0].shape[0], size), jnp.float32))
    return pl.pallas_call(
        kernel,
        out_shape=out_shape,
        in_specs=[SMEM] + [VMEM] * n_in + [ANYWHERE] * len(waits),
        out_specs=[VMEM] * len(out_shape),
        scratch_shapes=scratch,
        compiler_params=room(*out_shape, f32(2 * size, size), *squares),
        cost_estimate=cost(3_500_000_000),
    )(place, *squares, *waits)


def solve_kernel(blocks, n_lead, rel, scale, *refs):
    lead, refs = refs[:n_lead], refs[n_lead:]
    inverses, below = refs[:blocks], refs[blocks : 2 * blocks - 1]
    panel, weights = refs[-2:]
    found = []
    for k in range(blocks):
        across = slice(k * BLOCK, (k + 1) * BLOCK)
        total = lead[0][:, across]
        for x in lead[1:]:
            total = total + x[:, across]
        total = rel[:, across] + total * scale[0:1, :]
        for j in range(k):
            start = (k - j - 1) * BLOCK
            total = total - precise(found[j], below[j][start : start + BLOCK, :], 1)
        found.append(precise(total, inverses[k][...], 1))
        panel[:, k * BLOCK : (k + 1) * BLOCK] = found[k]
    for k in reversed(range(blocks)):
        total = found[k]
        for j in range(k + 1, blocks):
            start = (j - k - 1) * BLOCK
            total = total - precise(found[j], below[k][start : start + BLOCK, :], 0)
        found[k] = precise(total, inverses[k][...], 0)
        weights[:, k * BLOCK : (k + 1) * BLOCK] = found[k]


def solve(rel, scale, lead, inverses, below):
    own = rel.shape[0]
    return pl.pallas_call(
        functools.partial(solve_kernel, len(inverses), len(lead)),
        out_shape=[f32(own, PANEL), f32(own, PANEL)],
        in_specs=[VMEM] * (1 + len(lead) + 2 * len(inverses)),
        out_specs=[VMEM, VMEM],
        compiler_params=room(rel, rel, rel, *lead, *inverses, *below),
        cost_estimate=cost(4 * own * PANEL * PANEL),
    )(rel, scale, *lead, *inverses, *below)


def head_kernel(n_left, sizes, place, *refs):
    left, head = refs[:n_left], refs[n_left : n_left + GROUP]
    outs, order = refs[-1 - len(sizes) : -1], refs[-1]
    own = head[0].shape[0]
    in_order(place, head, order)
    at = 0
    for out, count in zip(outs, sizes):
        for n in range(count):
            out[n * own : (n + 1) * own, :] = times(left[at][...], order[:PANEL, :])
            at += 1


def message_kernel(place, scale, first, *refs):
    head, out, order = refs[:GROUP], refs[-2], refs[-1]
    own = first.shape[0]
    in_order(place, head, order)
    out[:own, :] = times(first[...], order[:PANEL, :])
    out[own:, :] = jnp.full((SUB, PANEL), scale[0], jnp.float32)


def message(place, scale, first, head):
    own, depth = first.shape
    return pl.pallas_call(
        message_kernel,
        out_shape=f32(own + SUB, PANEL),
        in_specs=[SMEM, SMEM] + [VMEM] * (1 + GROUP),
        out_specs=VMEM,
        scratch_shapes=[pltpu.VMEM((GROUP * own, depth), first.dtype)],
        compiler_params=room(first, *head, *head, f32(own, PANEL)),
        cost_estimate=cost(2 * own * PANEL * depth),
    )(place, scale, first, *head)


def total_kernel(*refs):
    parts, (rel, total, inverse) = refs[:-3], refs[-3:]
    own = total.shape[0]
    value = parts[0][...]
    for x in parts[1:]:
        value = value + x[...]
    scale = 1.0 / value[own : own + 1, :]
    total[...] = rel[...] + value[:own, :] * scale
    inverse[...] = jnp.broadcast_to(scale[:, :BLOCK], (SUB, BLOCK))


def total_rows(parts, rel):
    return pl.pallas_call(
        total_kernel,
        out_shape=[f32(*rel.shape), f32(SUB, BLOCK)],
        in_specs=[VMEM] * (len(parts) + 1),
        out_specs=[VMEM] * 2,
        compiler_params=room(*parts, rel, rel),
        cost_estimate=cost(1_000_000),
    )(*parts, rel)


def side_kernel(n_got, n_rel, scale, keep, *refs):
    rel, out = refs[-1 - n_rel : -1], refs[-1]
    got = refs[: -1 - n_rel]
    own = rel[0].shape[0]
    factor = scale[0:1, 0:1]
    each = n_rel // n_got
    for n in range(n_rel):
        cut = slice(n * own, (n + 1) * own)
        inside = slice((n % each) * own, (n % each + 1) * own)
        value = keep[cut, :]
        for x in got[n // each :: n_got]:
            value = value + x[inside, :]
        out[cut, :] = rel[n][...] + value * factor


def side_rows(scale, keep, n_got, got, rel, waits):
    count = len(got)

    def kernel(scale, keep, *refs):
        side_kernel(n_got, len(rel), scale, keep, *refs[: count + len(rel)], refs[-1])

    return pl.pallas_call(
        kernel,
        out_shape=f32(*keep.shape),
        in_specs=[VMEM] * (2 + count + len(rel)) + [ANYWHERE] * len(waits),
        out_specs=VMEM,
        compiler_params=room(keep, keep, *got, *rel),
        cost_estimate=cost(1_000_000),
    )(scale, keep, *got, *rel, *waits)


def head_products(place, groups, head, waits):
    own = head[0].shape[0]
    left = [x for group in groups for x in group]
    sizes = [len(group) for group in groups]
    return pl.pallas_call(
        functools.partial(head_kernel, len(left), sizes),
        out_shape=[f32(n * own, PANEL) for n in sizes],
        in_specs=[SMEM] + [VMEM] * (len(left) + GROUP) + [ANYWHERE] * len(waits),
        out_specs=[VMEM] * len(sizes),
        scratch_shapes=[pltpu.VMEM((GROUP * own, head[0].shape[1]), head[0].dtype)],
        compiler_params=room(*left, *head, *head, f32(len(left) * own, PANEL)),
        cost_estimate=cost(2 * len(left) * own * PANEL * head[0].shape[1]),
    )(place, *left, *head, *waits)


def gram_kernel(n_cols, n_more, *refs):
    plane, cols = refs[:GROUP], refs[GROUP : GROUP + n_cols]
    more = refs[GROUP + n_cols : GROUP + n_cols + n_more]
    outs = refs[-GROUP:]
    own = plane[0].shape[0]
    for k in range(GROUP):
        for j in range(n_cols):
            product = times(cols[j][...], plane[k][...])
            across = slice(j * own, (j + 1) * own)
            for x in more:
                product = product + x[across, k * own : (k + 1) * own]
            outs[k][:, across] = product.T


def gram_out_kernel(n_cols, *refs):
    plane, cols, out = refs[:GROUP], refs[GROUP : GROUP + n_cols], refs[-1]
    own = plane[0].shape[0]
    for k in range(GROUP):
        for j in range(n_cols):
            out[j * own : (j + 1) * own, k * own : (k + 1) * own] = times(
                cols[j][...], plane[k][...]
            )


def gram_products(plane, cols, more, waits):
    own, depth = plane[0].shape
    width = len(cols) * own
    if more is None:
        kernel = functools.partial(gram_out_kernel, len(cols))
        out_shape, out_specs, more = f32(width, GROUP * own), VMEM, []
    else:
        kernel = functools.partial(gram_kernel, len(cols), len(more))
        out_shape, out_specs = [f32(own, width)] * GROUP, [VMEM] * GROUP
    return pl.pallas_call(
        kernel,
        out_shape=out_shape,
        in_specs=[VMEM] * (GROUP + len(cols) + len(more))
        + [ANYWHERE] * len(waits),
        out_specs=out_specs,
        compiler_params=room(*plane, *cols, *more, f32(GROUP * own, width)),
        cost_estimate=cost(2 * GROUP * own * width * depth),
    )(*plane, *cols, *more, *waits)


def update_kernel(own, part, place, scale, rel, weights, *refs):
    pieces, sides = refs[:GROUP], refs[GROUP : 2 * GROUP]
    out, all_pieces, all_sides = refs[2 * GROUP :]
    in_order(place, pieces, all_pieces)
    in_order(place, sides, all_sides)
    i = lax.broadcasted_iota(jnp.int32, (own, own), 0)
    j = lax.broadcasted_iota(jnp.int32, (own, own), 1)
    ridge = jnp.where(i == j, RIDGE, 0.0)
    high, low = split(weights[...])
    width = part * own
    for m in range(GROUP):
        side_high, side_low = split(all_sides[m * width : (m + 1) * width, :])
        product = times(high, side_low) + times(low, side_high)
        product = product + times(high, side_high)
        for n in range(part):
            at = (n * GROUP + m) * own
            cut = slice(n * own, (n + 1) * own)
            here = (place[0] == m) & (place[1] == n)
            value = rel[:, at : at + own] - product[:, cut]
            value = value + all_pieces[m * own : (m + 1) * own, cut] * scale[0:1, 0:1]
            out[:, at : at + own] = value + ridge * jnp.where(here, 1.0, 0.0)


def final_update(place, scale, rel, weights, pieces, sides):
    own, width = rel.shape
    part = width // (GROUP * own)
    return pl.pallas_call(
        functools.partial(update_kernel, own, part),
        out_shape=f32(own, width),
        in_specs=[SMEM] + [VMEM] * (3 + 2 * GROUP),
        out_specs=VMEM,
        scratch_shapes=[
            pltpu.VMEM((GROUP * own, part * own), jnp.float32),
            pltpu.VMEM((width, PANEL), jnp.float32),
        ],
        compiler_params=room(rel, rel, weights, *pieces, *pieces, *sides, *sides),
        cost_estimate=cost(2 * own * width * PANEL),
    )(place, scale, rel, weights, *pieces, *sides)


def nothing(*refs):
    pass


def after(x, *done):
    return pl.pallas_call(
        nothing,
        out_shape=jax.ShapeDtypeStruct(x.shape, x.dtype),
        in_specs=[ANYWHERE] * (1 + len(done)),
        out_specs=ANYWHERE,
        input_output_aliases={0: 0},
        compiler_params=pltpu.CompilerParams(vmem_limit_bytes=2**20),
    )(x, *done)


def select_order(blocks, member):
    bit = 1
    while bit < len(blocks):
        swap = (member & bit) != 0
        blocks = [
            jnp.where(swap, blocks[k ^ bit], blocks[k]) for k in range(len(blocks))
        ]
        bit *= 2
    return blocks


def make(n_rows, n_snp):
    lines = n_rows // GROUP
    part = lines // n_snp
    far = lines // 2

    def rows_xor(x, bits):
        return lax.ppermute(x, "rows", [(r, r ^ bits) for r in range(n_rows)])

    def snp_xor(x, bits):
        return lax.ppermute(x, "snp", [(s, s ^ bits) for s in range(n_snp)])

    def from_first_snp(x, rank):
        got = x
        for s in range(1, n_snp):
            got = jnp.where(rank == s, lax.ppermute(x, "snp", [(0, s)]), got)
        return got

    def group_gather(x):
        core = rows_xor(x, 1)
        other = rows_xor(x, 2)
        return [x, core, other, rows_xor(other, 1)]

    def line_gather(x, hold):
        near = {k: rows_xor(x, k * GROUP) for k in range(1, far)}
        passed = hold(rows_xor(x, far * GROUP), list(near.values()))
        parts = {0: x, far: passed, **near}
        for k in range(1, far):
            parts[far + k] = rows_xor(passed, k * GROUP)
        return [parts[k] for k in range(lines)]

    def rows_sum(x):
        bit = 1
        while bit < n_rows:
            if bit * 2 < n_rows:
                parts = [x] + [rows_xor(x, bit * k) for k in (1, 2, 3)]
                x = (parts[0] + parts[1]) + (parts[2] + parts[3])
                bit *= 4
            else:
                x = x + rows_xor(x, bit)
                bit *= 2
        return x

    def snp_sum(x):
        bit = 1
        while bit < n_snp:
            x = x + snp_xor(x, bit)
            bit *= 2
        return x

    def per_device(genotypes, relationship):
        own = genotypes.shape[1]
        rank = lax.axis_index("rows")
        col = lax.axis_index("snp")
        q = rank % GROUP
        z = rank // GROUP
        place = jnp.stack([q, z - col * part]).astype(jnp.int32)

        called = genotypes >= 0
        dosage = jnp.where(called, genotypes, 0.0)
        stats = jnp.stack(
            [jnp.sum(dosage, axis=1), jnp.sum(called.astype(jnp.float32), axis=1)]
        )
        stats = rows_sum(stats)
        frequency = stats[0] / (2.0 * stats[1])
        scale_part = jnp.sum(2.0 * frequency * (1.0 - frequency))
        gt = lax.optimization_barrier(genotypes.T)
        centered = jnp.where(gt >= 0, gt - 2.0 * frequency[None, :], 0.0).astype(
            jnp.bfloat16
        )

        rel_own = from_first_snp(relationship[:, :PANEL], col)
        ids = rank * own + lax.broadcasted_iota(jnp.int32, rel_own.shape, 0)
        rel_own = rel_own + jnp.where(
            ids == lax.broadcasted_iota(jnp.int32, rel_own.shape, 1), RIDGE, 0.0
        )

        core, other = rows_xor(centered, 1), rows_xor(centered, 2)
        line = line_gather(centered, lambda x, near: after(x, rel_own, *near))
        line[-1] = after(line[-1], other)
        plane = [centered, core, other, rows_xor(other, 1)]
        first = select_order(line, z)[0]
        member = after((z ^ (col * part)).astype(jnp.int32).reshape(1), first)[0]
        ordered = select_order(line, member)
        groups = [ordered[bits * part : (bits + 1) * part] for bits in range(n_snp)]
        rel_line = line_gather(after(rel_own, line[-1]), lambda x, near: x)

        leaving = [gram_products(plane, groups[b], None, []) for b in range(1, n_snp)]

        head = [first, rows_xor(first, 1)]
        head.append(after(rows_xor(first, 2), *rel_line[1 : far + 1], *leaving))
        head.append(rows_xor(head[2], 1))
        rows = message(place, scale_part.reshape(1), first, head)
        rows_got = [snp_xor(rows, bits) for bits in range(1, n_snp)]
        halves = 2 if part % 2 == 0 else 1
        split_groups = [
            groups[b][h * part // halves : (h + 1) * part // halves]
            for b in range(1, n_snp)
            for h in range(halves)
        ]
        keep, *out = head_products(place, groups[:1] + split_groups, head, [rows])
        rel_line[-1] = after(rel_line[-1], out[0])
        total, scale = total_rows([rows] + rows_got, select_order(rel_line, z)[0])
        out = [after(x, total) for x in out]
        side_got = [snp_xor(x, n // halves + 1) for n, x in enumerate(out)]
        early = side_got[::halves]
        total = after(total, *out)

        (lead,) = head_products(place, [[centered]], head, [total])
        diagonal = [total, rows_xor(total, 1)]
        diagonal.append(after(rows_xor(total, 2), lead, *early))
        diagonal.append(rows_xor(diagonal[2], 1))

        gram_got = [
            snp_xor(after(leaving[b - 1], *early), b) for b in range(1, n_snp)
        ]
        pieces = gram_products(plane, groups[0], gram_got, [])
        moved = [pieces[0]] + [rows_xor(pieces[k], k) for k in range(1, GROUP)]

        inv, column, square = factor_step(place, diagonal, PANEL, [])
        inverses, below = [inv], [column]
        rel_side = select_order(rel_line, z ^ (col * part))[:part]
        side = side_rows(scale, keep, halves, side_got, rel_side, [inverses[0]])
        sides = [side, rows_xor(side, 1), rows_xor(side, 2)]

        lead = after(lead, pieces[1])
        leads = [lead] + [snp_xor(lead, bits) for bits in range(1, n_snp)]
        waits = [[], [side], [sides[1]], []]
        for k in range(1, PANEL // BLOCK):
            inv, *more = factor_step(place, [square], PANEL - k * BLOCK, waits[k])
            inverses.append(inv)
            if more:
                column, square = more
                below.append(column)

        sides[2] = after(sides[2], inverses[2])
        sides.append(rows_xor(sides[2], 1))

        panel, weights = solve(rel_own, scale, leads, inverses, below)
        updated = final_update(place, scale, relationship, weights, moved, sides)
        return updated, panel

    return per_device


def solution(mesh):
    return jax.shard_map(
        make(mesh.shape["rows"], mesh.shape["snp"]),
        mesh=mesh,
        in_specs=(P("snp", "rows"), P("rows", "snp")),
        out_specs=(P("rows", "snp"), P("rows", None)),
        check_vma=False,
    )
```
